512 devices in a mesh: dp: 32 (over y_lo, z), expert: 16 (over x, y_hi, core).
Axes of the slice: x: 4, y: 4 (y_hi: 2, y_lo: 2; y = y_hi * 2 + y_lo), z: 16, core: 2. Of those that a mesh axis runs over, the one named last changes fastest.
Arguments:
- tokens: bfloat16 [128, 256, 1280], P('dp', 'expert'), may hold values from -300 to 300
- cotangent: bfloat16 [128, 256, 1280], P('dp', 'expert'), may hold values from -6 to 6
- slot_params: bfloat16 [1280, 32], P(None, 'expert'), may hold values from -1 to 1
- w_in: bfloat16 [32, 1280, 5120], P('expert', None, 'dp'), may hold values from -0.15625 to 0.15625
- w_out: bfloat16 [32, 5120, 1280], P('expert', 'dp'), may hold values from -0.078125 to 0.078125
Outputs:
- token_grad: bfloat16 [128, 256, 1280], P('dp', 'expert')
- slot_grad: float32 [1280, 32], P(None, 'expert')
- w_in_grad: bfloat16 [32, 1280, 5120], P('expert', None, 'dp')
- w_out_grad: bfloat16 [32, 5120, 1280], P('expert', 'dp')
The draws below stay inside these ranges and needn't reach their ends.
All inputs are finite; a program needn't handle non-finite values.
Results may differ from the reference program's by a relative error of at most 0.035.
Values may be sent and summed in bfloat16 or wider, within the bound.
No kernel may reach another device: no remote copies, remote signals or barrier semaphores. Data moves between devices by JAX's collectives and lax.ppermute only.
A program may use at most 64 MiB of HBM per device.

```python
import jax
import jax.numpy as jnp
from jax import lax

D = 1280
FF = 5120
M = 256
IMG_DEV = 4
EXP_DEV = 2
IMAGES = 128
EXPERTS = 32
N_DP = 32
N_EXPERT = 16


def draw_slot_params(key, part):
    key = jax.random.fold_in(key, 1)
    slots = EXP_DEV * N_EXPERT
    values = jax.random.normal(key, (D, slots), jnp.float32) * (2.0 / D ** 0.5)
    return values.astype(jnp.bfloat16)


def draw_tokens(key, part):
    key = jax.random.fold_in(key, 2)
    images = IMG_DEV * N_DP
    values = jax.random.normal(key, (images, M, D), jnp.float32)
    return values.astype(jnp.bfloat16)


def level_of(stream_key, shape, pieces, smallest, largest):
    def one(dim, shards_of):
        heights = jax.random.uniform(jax.random.fold_in(jax.random.fold_in(stream_key, 6), dim), (shards_of,), jnp.float32, smallest / len(pieces), largest / len(pieces))
        return jnp.repeat(jnp.exp(heights), shape[dim] // shards_of).reshape((-1,) + (1,) * (len(shape) - dim - 1))

    loudness = one(*pieces[0])
    for cut in pieces[1:]:
        loudness = loudness * one(*cut)
    return loudness


def centred(stream_key, extent, spread, most, pieces=(), dtype=jnp.bfloat16):
    gain = level_of(stream_key, extent, pieces, -0.22, 0.18) if pieces else 1.0
    values = jax.random.normal(stream_key, extent, jnp.float32) * spread * gain
    return jnp.minimum(jnp.maximum(values, -most), most).astype(dtype)


def setup_inputs(seed: int = 0) -> dict:
    splits = jax.random.split(jax.random.key(seed), 6)
    return {
        "tokens": draw_tokens(jax.random.fold_in(splits[5], 71), 0),
        "cotangent": centred(splits[1], (IMAGES, M, D), 1.0, 6.0, ((0, 32), (1, 16))),
        "slot_params": draw_slot_params(jax.random.fold_in(splits[5], 71), 0),
        "w_in": centred(splits[3], (EXPERTS, D, FF), D ** -0.5, 0.15625, ((0, 16), (2, 32))),
        "w_out": centred(splits[4], (EXPERTS, FF, D), FF ** -0.5, 0.078125, ((0, 16), (1, 32))),
    }


def rounded(value):
    return lax.optimization_barrier(value.astype(jnp.bfloat16)).astype(jnp.float32)

def gelu_exact(value):
    return jax.nn.gelu(value, approximate=False)

def reference(tokens, cotangent, slot_params, w_in, w_out):
    hidden_block = FF // N_DP
    tok_wide = tokens.astype(jnp.float32)
    cot_wide = cotangent.astype(jnp.float32)
    param_wide = slot_params.astype(jnp.float32)
    w_in_wide = w_in.astype(jnp.float32)
    w_out_wide = w_out.astype(jnp.float32)
    logits = jnp.einsum('bmd,ds->bsm', tok_wide, param_wide)
    dispatch = jax.nn.softmax(logits, axis=2)
    combine = jax.nn.softmax(logits, axis=1)
    dispatch_b = dispatch.astype(jnp.bfloat16).astype(jnp.float32)
    combine_b = combine.astype(jnp.bfloat16).astype(jnp.float32)
    slot_in = jnp.einsum('bsm,bmd->bsd', dispatch_b, tok_wide).astype(jnp.bfloat16).astype(jnp.float32)
    preact = jnp.einsum('bsd,sdh->bsh', slot_in, w_in_wide)
    activated = gelu_exact(preact).astype(jnp.bfloat16).astype(jnp.float32)
    slot_total = jnp.zeros((IMAGES, EXPERTS, D), jnp.float32)
    for block_id in range(N_DP):
        lower = block_id * hidden_block
        upper = lower + hidden_block
        slot_total = slot_total + rounded(jnp.einsum('bsh,shd->bsd', activated[:, :, lower:upper], w_out_wide[:, lower:upper, :]))
    slot_out = slot_total.astype(jnp.bfloat16).astype(jnp.float32)
    combine_grad = jnp.einsum('bmd,bsd->bsm', cot_wide, slot_out)
    slot_out_grad = jnp.einsum('bsm,bmd->bsd', combine_b, cot_wide).astype(jnp.bfloat16).astype(jnp.float32)
    w_out_grad = jnp.einsum('bsh,bsd->shd', activated, slot_out_grad).astype(jnp.bfloat16)
    act_grad = jnp.einsum('bsd,shd->bsh', slot_out_grad, w_out_wide)
    _, pullback = jax.vjp(gelu_exact, preact)
    preact_grad = pullback(act_grad)[0].astype(jnp.bfloat16).astype(jnp.float32)
    w_in_grad = jnp.einsum('bsd,bsh->sdh', slot_in, preact_grad).astype(jnp.bfloat16)
    grad_total = jnp.zeros((IMAGES, EXPERTS, D), jnp.float32)
    for block_id in range(N_DP):
        lower = block_id * hidden_block
        upper = lower + hidden_block
        grad_total = grad_total + rounded(jnp.einsum('bsh,sdh->bsd', preact_grad[:, :, lower:upper], w_in_wide[:, :, lower:upper]))
    slot_in_grad = grad_total.astype(jnp.bfloat16).astype(jnp.float32)
    dispatch_grad = jnp.einsum('bsd,bmd->bsm', slot_in_grad, tok_wide)
    row_sums = lax.optimization_barrier(jnp.sum(combine * combine_grad, axis=1, keepdims=True))
    col_sums = lax.optimization_barrier(jnp.sum(dispatch * dispatch_grad, axis=2, keepdims=True))
    logit_grad = (dispatch * (dispatch_grad - col_sums) + combine * (combine_grad - row_sums)).astype(jnp.bfloat16).astype(jnp.float32)
    slot_grad = jnp.einsum('bsm,bmd->ds', logit_grad, tok_wide)
    token_total = jnp.zeros((IMAGES, M, D), jnp.float32)
    for block_id in range(N_EXPERT):
        lower = block_id * EXP_DEV
        upper = lower + EXP_DEV
        term = jnp.einsum('bsm,bsd->bmd', dispatch_b[:, lower:upper], slot_in_grad[:, lower:upper])
        term = term + jnp.einsum('bsm,ds->bmd', logit_grad[:, lower:upper], param_wide[:, lower:upper])
        token_total = token_total + rounded(term)
    token_grad = token_total.astype(jnp.bfloat16)
    return (token_grad, slot_grad, w_in_grad, w_out_grad)
```

```python
import jax
import jax.numpy as jnp
from jax import lax
from jax.sharding import PartitionSpec as P

F32 = jnp.float32
BF16 = jnp.bfloat16


def gelu_exact(value):
    return jax.nn.gelu(value, approximate=False)


def split3(value):
    high = lax.reduce_precision(value, 8, 7)
    middle = lax.reduce_precision(value - high, 8, 7)
    low = value - high - middle
    return [high.astype(BF16), middle.astype(BF16), low.astype(BF16)]


def join3(terms):
    wide = terms.astype(F32)
    return wide[..., 0:1] + wide[..., 1:2] + wide[..., 2:3]


def along_z(value, step):
    depth = lax.axis_size("dp") // 2
    pairs = [
        (y * depth + z, y * depth + (z + step) % depth) for y in range(2) for z in range(depth)
    ]
    return lax.ppermute(value, "dp", pairs)


def across_y(value):
    depth = lax.axis_size("dp") // 2
    pairs = [(y * depth + z, (1 - y) * depth + z) for y in range(2) for z in range(depth)]
    return lax.ppermute(value, "dp", pairs)


def add_narrow(left, right):
    return (left.astype(F32) + right.astype(F32)).astype(BF16)


def gather_dp(own):
    half = lax.axis_size("dp") // 4
    both = jnp.concatenate([own, across_y(own)], axis=2)
    up, down = [both], [both]
    for _ in range(1, half):
        up.append(along_z(up[-1], 1))
        down.append(along_z(down[-1], -1))
    far = jnp.concatenate([along_z(up[-1][:1], 1), along_z(down[-1][1:], -1)], axis=0)
    return up, down, far


def reduce_dp(up, down, far):
    half = lax.axis_size("dp") // 4
    imgs = far.shape[2] // 2
    to_low = along_z(far[:1], -1)
    to_high = along_z(far[1:], 1)
    for r in range(half - 1, 0, -1):
        if r == half - 1:
            low = jnp.concatenate([add_narrow(up[r][:1], to_low), up[r][1:]], axis=0)
            high = jnp.concatenate([down[r][:1], add_narrow(down[r][1:], to_high)], axis=0)
        else:
            low = add_narrow(up[r], to_low)
            high = add_narrow(down[r], to_high)
        to_low = along_z(low, -1)
        to_high = along_z(high, 1)
    total = up[0].astype(F32) + to_low.astype(F32) + to_high.astype(F32)
    other = across_y(total[:, :, imgs:].astype(BF16))
    return total[:, :, :imgs] + other.astype(F32)


def exchange(value, axis):
    return lax.all_to_all(value, axis, split_axis=0, concat_axis=0, tiled=True)


def everywhere(value, axis):
    return exchange(jnp.broadcast_to(value[None], (lax.axis_size(axis),) + value.shape), axis)


def expert_part(gathered, w_in, w_out):
    all_in, all_out_grad = gathered[0], gathered[1]
    preact = jnp.einsum("sbd,sdh->sbh", all_in, w_in, preferred_element_type=F32)
    activated_wide, pullback = jax.vjp(gelu_exact, preact)
    activated = activated_wide.astype(BF16)
    slot_out = jnp.einsum("sbh,shd->sbd", activated, w_out, preferred_element_type=F32)
    act_grad = jnp.einsum("sbd,shd->sbh", all_out_grad, w_out, preferred_element_type=F32)
    preact_grad = pullback(act_grad)[0].astype(BF16)
    slot_in_grad = jnp.einsum("sbh,sdh->sbd", preact_grad, w_in, preferred_element_type=F32)
    w_out_grad = jnp.einsum(
        "sbh,sbd->shd", activated, all_out_grad, preferred_element_type=F32
    ).astype(BF16)
    w_in_grad = jnp.einsum(
        "sbd,sbh->sdh", all_in, preact_grad, preferred_element_type=F32
    ).astype(BF16)
    partial = jnp.stack([slot_out.astype(BF16), slot_in_grad.astype(BF16)])
    return partial, w_in_grad, w_out_grad


def on_device(tokens, cotangent, slot_params, w_in, w_out):
    imgs, share, d = tokens.shape
    peers = lax.axis_size("expert")
    own_slots = slot_params.shape[1]
    slots = peers * own_slots
    rows = own_slots * imgs

    params = everywhere(slot_params.T, "expert").reshape(slots, d)
    logits = jnp.einsum("sd,bmd->sbm", params, tokens, preferred_element_type=F32)
    combine = jax.nn.softmax(logits, axis=0)
    combine_b = combine.astype(BF16)
    peak = jnp.max(logits, axis=2, keepdims=True)
    weight = jnp.exp(logits - peak)
    mass = jnp.sum(weight, axis=2, keepdims=True)
    part_in = jnp.einsum("sbm,bmd->sbd", weight.astype(BF16), tokens, preferred_element_type=F32)
    part_grad = jnp.einsum("sbm,bmd->sbd", combine_b, cotangent, preferred_element_type=F32)
    stats = jnp.concatenate(
        split3(peak) + split3(mass) + [jnp.zeros((slots, imgs, 122), BF16)], axis=2
    )
    sent = jnp.concatenate([part_in.astype(BF16), stats, part_grad.astype(BF16)], axis=2)
    taken = exchange(sent.reshape(peers, rows, 2 * d + 128), "expert")

    peaks = join3(taken[:, :, d : d + 3])
    masses = join3(taken[:, :, d + 3 : d + 6])
    top = jnp.max(peaks, axis=0)
    scale = jnp.exp(peaks - top[None])
    total = jnp.sum(masses * scale, axis=0)
    slot_in_wide = jnp.sum(taken[:, :, :d].astype(F32) * scale, axis=0) / total
    slot_out_grad = jnp.sum(taken[:, :, d + 128 :].astype(F32), axis=0)
    own = jnp.stack([slot_in_wide.astype(BF16), slot_out_grad.astype(BF16)])

    up, down, far = gather_dp(own.reshape(2, own_slots, imgs, d))
    chunks = up + down[1:] + [far]
    partial, w_in_grad, w_out_grad = expert_part(jnp.concatenate(chunks, axis=2), w_in, w_out)
    pieces = jnp.split(partial, len(chunks), axis=2)
    half = len(up)
    owned = reduce_dp(pieces[:half], [None] + pieces[half : 2 * half - 1], pieces[-1])
    owned_b = owned.astype(BF16).reshape(2, rows, d)

    col = jnp.sum(owned_b[1].astype(F32) * slot_in_wide, axis=1, keepdims=True)
    stats = jnp.concatenate(
        split3(top) + split3(total) + split3(col) + [jnp.zeros((rows, 119), BF16)], axis=1
    )
    back = everywhere(jnp.concatenate([owned_b[0], owned_b[1], stats], axis=1), "expert")
    back = back.reshape(slots, imgs, 2 * d + 128)
    slot_out, slot_in_grad = back[:, :, :d], back[:, :, d : 2 * d]
    top = join3(back[:, :, 2 * d : 2 * d + 3])
    total = join3(back[:, :, 2 * d + 3 : 2 * d + 6])
    col = join3(back[:, :, 2 * d + 6 : 2 * d + 9])

    dispatch = jnp.exp(logits - top) / total
    dispatch_b = dispatch.astype(BF16)
    combine_grad = jnp.einsum("bmd,sbd->sbm", cotangent, slot_out, preferred_element_type=F32)
    dispatch_grad = jnp.einsum("sbd,bmd->sbm", slot_in_grad, tokens, preferred_element_type=F32)
    row_sums = jnp.sum(combine * combine_grad, axis=0, keepdims=True)
    logit_grad = (
        dispatch * (dispatch_grad - col) + combine * (combine_grad - row_sums)
    ).astype(BF16)
    token_grad = jnp.einsum("sbm,sbd->bmd", dispatch_b, slot_in_grad, preferred_element_type=F32)
    token_grad = token_grad + jnp.einsum(
        "sbm,sd->bmd", logit_grad, params, preferred_element_type=F32
    )
    token_grad = token_grad.astype(BF16)

    share_grad = jnp.einsum("sbm,bmd->sd", logit_grad, tokens, preferred_element_type=F32)
    share_grad = jnp.sum(exchange(share_grad.reshape(peers, own_slots, d), "expert"), axis=0)
    n_dp = lax.axis_size("dp")
    share_grad = exchange(share_grad.reshape(n_dp, 1, own_slots * d // n_dp), "dp")
    share_grad = everywhere(jnp.sum(share_grad, axis=0), "dp")
    slot_grad = share_grad.reshape(own_slots, d).T
    return (token_grad, slot_grad, w_in_grad, w_out_grad)


def solution(mesh):
    placed = (
        P("dp", "expert", None),
        P("dp", "expert", None),
        P(None, "expert"),
        P("expert", None, "dp"),
        P("expert", "dp", None),
    )
    return jax.shard_map(
        on_device,
        mesh=mesh,
        in_specs=placed,
        out_specs=(
            P("dp", "expert", None),
            P(None, "expert"),
            P("expert", None, "dp"),
            P("expert", "dp", None),
        ),
        check_vma=False,
    )
```

```python
import jax
import jax.numpy as jnp
import numpy as np
from jax import lax
from jax.sharding import PartitionSpec as P

F32 = jnp.float32
BF16 = jnp.bfloat16


def gelu_exact(value):
    return jax.nn.gelu(value, approximate=False)


def split3(value):
    high = lax.reduce_precision(value, 8, 7)
    middle = lax.reduce_precision(value - high, 8, 7)
    low = value - high - middle
    return [high.astype(BF16), middle.astype(BF16), low.astype(BF16)]


def join3(terms):
    wide = terms.astype(F32)
    return wide[..., 0:1] + wide[..., 1:2] + wide[..., 2:3]


def groups_of(axis, sizes, inner):
    shape = [lax.axis_size(axis) // sizes[0] // sizes[1], sizes[0], sizes[1]]
    ids = np.arange(lax.axis_size(axis)).reshape(shape)
    outer = [part for part in range(3) if part not in inner]
    width = int(np.prod([shape[part] for part in inner]))
    return ids.transpose(outer + list(inner)).reshape(-1, width).tolist()


def exchange(value, axis, groups=None):
    return lax.all_to_all(
        value, axis, split_axis=0, concat_axis=0, axis_index_groups=groups, tiled=True
    )


def everywhere(value, axis, groups=None):
    peers = lax.axis_size(axis) if groups is None else len(groups[0])
    return exchange(jnp.broadcast_to(value[None], (peers,) + value.shape), axis, groups)


def dp_groups(*inner):
    depth = lax.axis_size("dp") // 2
    near = 4 if depth >= 16 else 2
    return groups_of("dp", (depth // near, near), inner)


def expert_groups(*inner):
    return groups_of("expert", (2, 2), inner)


def gather_dp(own):
    rows, d = own.shape[1:]
    far = everywhere(own, "dp", dp_groups(1))
    near = everywhere(far, "dp", dp_groups(2))
    near = jnp.transpose(near, (2, 0, 1, 3, 4)).reshape(2, -1, d)
    return everywhere(near, "dp", dp_groups(0))


def reduce_dp(partial, rows):
    d = partial.shape[-1]
    near, far = len(dp_groups(2)[0]), len(dp_groups(1)[0])
    total = jnp.sum(exchange(partial, "dp", dp_groups(0)).astype(F32), axis=0).astype(BF16)
    total = jnp.transpose(total.reshape(2, near, far * rows, d), (1, 0, 2, 3))
    total = jnp.sum(exchange(total, "dp", dp_groups(2)).astype(F32), axis=0).astype(BF16)
    total = jnp.transpose(total.reshape(2, far, rows, d), (1, 0, 2, 3))
    return jnp.sum(exchange(total, "dp", dp_groups(1)).astype(F32), axis=0)


def expert_part(gathered, w_in, w_out, imgs):
    slots, d, width = w_in.shape
    all_in = gathered[:, 0].reshape(-1, d)
    all_out_grad = gathered[:, 1].reshape(-1, d)
    row = lax.broadcasted_iota(jnp.int32, (slots, all_in.shape[0], 1), 1)
    slot = lax.broadcasted_iota(jnp.int32, (slots, all_in.shape[0], 1), 0)
    mine = (row // imgs) % slots == slot
    preact = jnp.einsum("rd,sdh->srh", all_in, w_in, preferred_element_type=F32)
    activated_wide, pullback = jax.vjp(gelu_exact, preact)
    activated = jnp.where(mine, activated_wide, 0.0).astype(BF16)
    slot_out = jnp.einsum("srh,shd->rd", activated, w_out, preferred_element_type=F32)
    act_grad = jnp.einsum("rd,shd->srh", all_out_grad, w_out, preferred_element_type=F32)
    preact_grad = jnp.where(mine, pullback(act_grad)[0], 0.0).astype(BF16)
    slot_in_grad = jnp.einsum("srh,sdh->rd", preact_grad, w_in, preferred_element_type=F32)
    w_out_grad = jnp.einsum(
        "srh,rd->shd", activated, all_out_grad, preferred_element_type=F32
    ).astype(BF16)
    w_in_grad = jnp.einsum(
        "rd,srh->sdh", all_in, preact_grad, preferred_element_type=F32
    ).astype(BF16)
    shape = (gathered.shape[0], 1) + gathered.shape[2:]
    partial = jnp.concatenate(
        [slot_out.astype(BF16).reshape(shape), slot_in_grad.astype(BF16).reshape(shape)], axis=1
    )
    return partial, w_in_grad, w_out_grad


def on_device(tokens, cotangent, slot_params, w_in, w_out):
    imgs, share, d = tokens.shape
    peers = lax.axis_size("expert")
    own_slots = slot_params.shape[1]
    slots = peers * own_slots
    rows = own_slots * imgs

    params = everywhere(slot_params.T, "expert", expert_groups(1, 2))
    params = everywhere(params, "expert", expert_groups(0)).reshape(slots, d)
    logits = jnp.einsum("sd,bmd->sbm", params, tokens, preferred_element_type=F32)
    combine = jax.nn.softmax(logits, axis=0)
    combine_b = combine.astype(BF16)
    peak = jnp.max(logits, axis=2, keepdims=True)
    weight = jnp.exp(logits - peak)
    mass = jnp.sum(weight, axis=2, keepdims=True)
    part_in = jnp.einsum("sbm,bmd->sbd", weight.astype(BF16), tokens, preferred_element_type=F32)
    part_grad = jnp.einsum("sbm,bmd->sbd", combine_b, cotangent, preferred_element_type=F32)
    stats = jnp.concatenate(
        split3(peak) + split3(mass) + [jnp.zeros((slots, imgs, 122), BF16)], axis=2
    )
    sent = jnp.concatenate([part_in.astype(BF16), stats, part_grad.astype(BF16)], axis=2)
    taken = exchange(sent.reshape(peers, rows, 2 * d + 128), "expert")

    peaks = join3(taken[:, :, d : d + 3])
    masses = join3(taken[:, :, d + 3 : d + 6])
    top = jnp.max(peaks, axis=0)
    scale = jnp.exp(peaks - top[None])
    total = jnp.sum(masses * scale, axis=0)
    slot_in_wide = jnp.sum(taken[:, :, :d].astype(F32) * scale, axis=0) / total
    slot_out_grad = jnp.sum(taken[:, :, d + 128 :].astype(F32), axis=0)
    own = jnp.stack([slot_in_wide.astype(BF16), slot_out_grad.astype(BF16)])

    gathered = gather_dp(own)
    partial, w_in_grad, w_out_grad = expert_part(gathered, w_in, w_out, imgs)
    owned_b = reduce_dp(partial, rows).astype(BF16)

    col = jnp.sum(owned_b[1].astype(F32) * slot_in_wide, axis=1, keepdims=True)
    stats = jnp.concatenate(
        split3(top) + split3(total) + split3(col) + [jnp.zeros((rows, 119), BF16)], axis=1
    )
    back = everywhere(jnp.concatenate([owned_b[0], owned_b[1], stats], axis=1), "expert")
    back = back.reshape(slots, imgs, 2 * d + 128)
    slot_out, slot_in_grad = back[:, :, :d], back[:, :, d : 2 * d]
    top = join3(back[:, :, 2 * d : 2 * d + 3])
    total = join3(back[:, :, 2 * d + 3 : 2 * d + 6])
    col = join3(back[:, :, 2 * d + 6 : 2 * d + 9])

    dispatch = jnp.exp(logits - top) / total
    dispatch_b = dispatch.astype(BF16)
    combine_grad = jnp.einsum("bmd,sbd->sbm", cotangent, slot_out, preferred_element_type=F32)
    dispatch_grad = jnp.einsum("sbd,bmd->sbm", slot_in_grad, tokens, preferred_element_type=F32)
    row_sums = jnp.sum(combine * combine_grad, axis=0, keepdims=True)
    logit_grad = (
        dispatch * (dispatch_grad - col) + combine * (combine_grad - row_sums)
    ).astype(BF16)
    token_grad = jnp.einsum("sbm,sbd->bmd", dispatch_b, slot_in_grad, preferred_element_type=F32)
    token_grad = token_grad + jnp.einsum(
        "sbm,sd->bmd", logit_grad, params, preferred_element_type=F32
    )
    token_grad = token_grad.astype(BF16)

    share_grad = jnp.einsum("sbm,bmd->sd", logit_grad, tokens, preferred_element_type=F32)
    share_grad = share_grad.reshape(peers // 4, 4 * own_slots, d)
    share_grad = jnp.sum(exchange(share_grad, "expert", expert_groups(0)), axis=0)
    share_grad = share_grad.reshape(4, own_slots, d)
    share_grad = jnp.sum(exchange(share_grad, "expert", expert_groups(1, 2)), axis=0)
    share_grad = jnp.sum(everywhere(share_grad, "dp", dp_groups(1)), axis=0)
    share_grad = jnp.sum(everywhere(share_grad, "dp", dp_groups(0, 2)), axis=0)
    slot_grad = share_grad.T
    return (token_grad, slot_grad, w_in_grad, w_out_grad)


def solution(mesh):
    placed = (
        P("dp", "expert", None),
        P("dp", "expert", None),
        P(None, "expert"),
        P("expert", None, "dp"),
        P("expert", "dp", None),
    )
    return jax.shard_map(
        on_device,
        mesh=mesh,
        in_specs=placed,
        out_specs=(
            P("dp", "expert", None),
            P(None, "expert"),
            P("expert", None, "dp"),
            P("expert", "dp", None),
        ),
        check_vma=False,
    )
```

```python
import jax
import jax.numpy as jnp
import numpy as np
from jax import lax
from jax.sharding import PartitionSpec as P

F32 = jnp.float32
BF16 = jnp.bfloat16


def gelu_exact(value):
    return jax.nn.gelu(value, approximate=False)


def split3(value):
    high = lax.reduce_precision(value, 8, 7)
    middle = lax.reduce_precision(value - high, 8, 7)
    low = value - high - middle
    return [high.astype(BF16), middle.astype(BF16), low.astype(BF16)]


def join3(terms):
    wide = terms.astype(F32)
    return wide[..., 0:1] + wide[..., 1:2] + wide[..., 2:3]


def groups_of(axis, sizes, inner):
    shape = [lax.axis_size(axis) // sizes[0] // sizes[1], sizes[0], sizes[1]]
    ids = np.arange(lax.axis_size(axis)).reshape(shape)
    outer = [part for part in range(3) if part not in inner]
    width = int(np.prod([shape[part] for part in inner]))
    return ids.transpose(outer + list(inner)).reshape(-1, width).tolist()


def exchange(value, axis, groups=None):
    return lax.all_to_all(
        value, axis, split_axis=0, concat_axis=0, axis_index_groups=groups, tiled=True
    )


def everywhere(value, axis, groups=None):
    peers = lax.axis_size(axis) if groups is None else len(groups[0])
    return exchange(jnp.broadcast_to(value[None], (peers,) + value.shape), axis, groups)


def dp_groups(*inner):
    return groups_of("dp", (lax.axis_size("dp") // 4, 2), inner)


def gather_dp(own):
    rows, d = own.shape[1:]
    far = everywhere(own, "dp", dp_groups(1))
    far = jnp.transpose(far, (1, 0, 2, 3)).reshape(2, -1, d)
    return everywhere(far, "dp", dp_groups(0, 2))


def reduce_dp(partial, rows):
    d = partial.shape[-1]
    total = jnp.sum(exchange(partial, "dp", dp_groups(0, 2)).astype(F32), axis=0).astype(BF16)
    total = jnp.transpose(total.reshape(2, -1, rows, d), (1, 0, 2, 3))
    return jnp.sum(exchange(total, "dp", dp_groups(1)).astype(F32), axis=0)


def expert_part(gathered, w_in, w_out, imgs):
    slots, d, width = w_in.shape
    all_in = gathered[:, 0].reshape(-1, d)
    all_out_grad = gathered[:, 1].reshape(-1, d)
    row = lax.broadcasted_iota(jnp.int32, (slots, all_in.shape[0], 1), 1)
    slot = lax.broadcasted_iota(jnp.int32, (slots, all_in.shape[0], 1), 0)
    mine = (row // imgs) % slots == slot
    preact = jnp.einsum("rd,sdh->srh", all_in, w_in, preferred_element_type=F32)
    activated_wide, pullback = jax.vjp(gelu_exact, preact)
    activated = jnp.where(mine, activated_wide, 0.0).astype(BF16)
    slot_out = jnp.einsum("srh,shd->rd", activated, w_out, preferred_element_type=F32)
    act_grad = jnp.einsum("rd,shd->srh", all_out_grad, w_out, preferred_element_type=F32)
    preact_grad = jnp.where(mine, pullback(act_grad)[0], 0.0).astype(BF16)
    slot_in_grad = jnp.einsum("srh,sdh->rd", preact_grad, w_in, preferred_element_type=F32)
    w_out_grad = jnp.einsum(
        "srh,rd->shd", activated, all_out_grad, preferred_element_type=F32
    ).astype(BF16)
    w_in_grad = jnp.einsum(
        "rd,srh->sdh", all_in, preact_grad, preferred_element_type=F32
    ).astype(BF16)
    shape = (gathered.shape[0], 1) + gathered.shape[2:]
    partial = jnp.concatenate(
        [slot_out.astype(BF16).reshape(shape), slot_in_grad.astype(BF16).reshape(shape)], axis=1
    )
    return partial, w_in_grad, w_out_grad


def on_device(tokens, cotangent, slot_params, w_in, w_out):
    imgs, share, d = tokens.shape
    peers = lax.axis_size("expert")
    own_slots = slot_params.shape[1]
    slots = peers * own_slots
    rows = own_slots * imgs

    params = everywhere(slot_params.T, "expert").reshape(slots, d)
    logits = jnp.einsum("sd,bmd->sbm", params, tokens, preferred_element_type=F32)
    combine = jax.nn.softmax(logits, axis=0)
    combine_b = combine.astype(BF16)
    peak = jnp.max(logits, axis=2, keepdims=True)
    weight = jnp.exp(logits - peak)
    mass = jnp.sum(weight, axis=2, keepdims=True)
    part_in = jnp.einsum("sbm,bmd->sbd", weight.astype(BF16), tokens, preferred_element_type=F32)
    part_grad = jnp.einsum("sbm,bmd->sbd", combine_b, cotangent, preferred_element_type=F32)
    stats = jnp.concatenate(
        split3(peak) + split3(mass) + [jnp.zeros((slots, imgs, 122), BF16)], axis=2
    )
    sent = jnp.concatenate([part_in.astype(BF16), stats, part_grad.astype(BF16)], axis=2)
    taken = exchange(sent.reshape(peers, rows, 2 * d + 128), "expert")

    peaks = join3(taken[:, :, d : d + 3])
    masses = join3(taken[:, :, d + 3 : d + 6])
    top = jnp.max(peaks, axis=0)
    scale = jnp.exp(peaks - top[None])
    total = jnp.sum(masses * scale, axis=0)
    slot_in_wide = jnp.sum(taken[:, :, :d].astype(F32) * scale, axis=0) / total
    slot_out_grad = jnp.sum(taken[:, :, d + 128 :].astype(F32), axis=0)
    own = jnp.stack([slot_in_wide.astype(BF16), slot_out_grad.astype(BF16)])

    gathered = gather_dp(own)
    partial, w_in_grad, w_out_grad = expert_part(gathered, w_in, w_out, imgs)
    owned_b = reduce_dp(partial, rows).astype(BF16)

    col = jnp.sum(owned_b[1].astype(F32) * slot_in_wide, axis=1, keepdims=True)
    stats = jnp.concatenate(
        split3(top) + split3(total) + split3(col) + [jnp.zeros((rows, 119), BF16)], axis=1
    )
    back = everywhere(jnp.concatenate([owned_b[0], owned_b[1], stats], axis=1), "expert")
    back = back.reshape(slots, imgs, 2 * d + 128)
    slot_out, slot_in_grad = back[:, :, :d], back[:, :, d : 2 * d]
    top = join3(back[:, :, 2 * d : 2 * d + 3])
    total = join3(back[:, :, 2 * d + 3 : 2 * d + 6])
    col = join3(back[:, :, 2 * d + 6 : 2 * d + 9])

    dispatch = jnp.exp(logits - top) / total
    dispatch_b = dispatch.astype(BF16)
    combine_grad = jnp.einsum("bmd,sbd->sbm", cotangent, slot_out, preferred_element_type=F32)
    dispatch_grad = jnp.einsum("sbd,bmd->sbm", slot_in_grad, tokens, preferred_element_type=F32)
    row_sums = jnp.sum(combine * combine_grad, axis=0, keepdims=True)
    logit_grad = (
        dispatch * (dispatch_grad - col) + combine * (combine_grad - row_sums)
    ).astype(BF16)
    token_grad = jnp.einsum("sbm,sbd->bmd", dispatch_b, slot_in_grad, preferred_element_type=F32)
    token_grad = token_grad + jnp.einsum(
        "sbm,sd->bmd", logit_grad, params, preferred_element_type=F32
    )
    token_grad = token_grad.astype(BF16)

    share_grad = jnp.einsum("sbm,bmd->sd", logit_grad, tokens, preferred_element_type=F32)
    share_grad = jnp.sum(exchange(share_grad.reshape(peers, own_slots, d), "expert"), axis=0)
    share_grad = jnp.sum(everywhere(share_grad, "dp", dp_groups(1)), axis=0)
    share_grad = jnp.sum(everywhere(share_grad, "dp", dp_groups(0, 2)), axis=0)
    slot_grad = share_grad.T
    return (token_grad, slot_grad, w_in_grad, w_out_grad)


def solution(mesh):
    placed = (
        P("dp", "expert", None),
        P("dp", "expert", None),
        P(None, "expert"),
        P("expert", None, "dp"),
        P("expert", "dp", None),
    )
    return jax.shard_map(
        on_device,
        mesh=mesh,
        in_specs=placed,
        out_specs=(
            P("dp", "expert", None),
            P(None, "expert"),
            P("expert", None, "dp"),
            P("expert", "dp", None),
        ),
        check_vma=False,
    )
```

```python
import jax
import jax.numpy as jnp
import numpy as np
from jax import lax
from jax.sharding import PartitionSpec as P

F32 = jnp.float32
BF16 = jnp.bfloat16


def gelu_exact(value):
    return jax.nn.gelu(value, approximate=False)


def split3(value):
    high = lax.reduce_precision(value, 8, 7)
    middle = lax.reduce_precision(value - high, 8, 7)
    low = value - high - middle
    return [high.astype(BF16), middle.astype(BF16), low.astype(BF16)]


def join3(terms):
    wide = terms.astype(F32)
    return wide[..., 0:1] + wide[..., 1:2] + wide[..., 2:3]


def groups_of(axis, sizes, inner):
    shape = [lax.axis_size(axis) // sizes[0] // sizes[1], sizes[0], sizes[1]]
    ids = np.arange(lax.axis_size(axis)).reshape(shape)
    outer = [part for part in range(3) if part not in inner]
    width = int(np.prod([shape[part] for part in inner]))
    return ids.transpose(outer + list(inner)).reshape(-1, width).tolist()


def exchange(value, axis, groups=None):
    return lax.all_to_all(
        value, axis, split_axis=0, concat_axis=0, axis_index_groups=groups, tiled=True
    )


def everywhere(value, axis, groups=None):
    peers = lax.axis_size(axis) if groups is None else len(groups[0])
    return exchange(jnp.broadcast_to(value[None], (peers,) + value.shape), axis, groups)


def dp_groups(*inner):
    return groups_of("dp", (lax.axis_size("dp") // 4, 2), inner)


def gather_dp(own):
    return everywhere(everywhere(own, "dp", dp_groups(1)), "dp", dp_groups(0, 2))


def reduce_dp(partial, rows):
    d = partial.shape[-1]
    total = jnp.sum(exchange(partial, "dp", dp_groups(0, 2)).astype(F32), axis=0).astype(BF16)
    return jnp.sum(exchange(total.reshape(-1, rows, d), "dp", dp_groups(1)).astype(F32), axis=0)


def slot_mask(rows, slots, imgs):
    row = lax.broadcasted_iota(jnp.int32, (slots, rows, 1), 1)
    slot = lax.broadcasted_iota(jnp.int32, (slots, rows, 1), 0)
    return (row // imgs) % slots == slot


def expert_forward(all_in, w_in, w_out, mine):
    preact = jnp.einsum("rd,sdh->srh", all_in, w_in, preferred_element_type=F32)
    activated = jnp.where(mine, gelu_exact(preact), 0.0).astype(BF16)
    slot_out = jnp.einsum("srh,shd->rd", activated, w_out, preferred_element_type=F32)
    return preact, activated, slot_out.astype(BF16)


def expert_backward(all_in, all_out_grad, preact, activated, w_in, w_out, mine):
    _, pullback = jax.vjp(gelu_exact, preact)
    act_grad = jnp.einsum("rd,shd->srh", all_out_grad, w_out, preferred_element_type=F32)
    preact_grad = jnp.where(mine, pullback(act_grad)[0], 0.0).astype(BF16)
    slot_in_grad = jnp.einsum("srh,sdh->rd", preact_grad, w_in, preferred_element_type=F32)
    w_out_grad = jnp.einsum(
        "srh,rd->shd", activated, all_out_grad, preferred_element_type=F32
    ).astype(BF16)
    w_in_grad = jnp.einsum(
        "rd,srh->sdh", all_in, preact_grad, preferred_element_type=F32
    ).astype(BF16)
    return slot_in_grad.astype(BF16), w_in_grad, w_out_grad


def on_device(tokens, cotangent, slot_params, w_in, w_out):
    imgs, share, d = tokens.shape
    peers = lax.axis_size("expert")
    own_slots = slot_params.shape[1]
    slots = peers * own_slots
    rows = own_slots * imgs

    params = everywhere(slot_params.T, "expert").reshape(slots, d)
    logits = jnp.einsum("sd,bmd->sbm", params, tokens, preferred_element_type=F32)
    combine = jax.nn.softmax(logits, axis=0)
    combine_b = combine.astype(BF16)
    peak = jnp.max(logits, axis=2, keepdims=True)
    weight = jnp.exp(logits - peak)
    mass = jnp.sum(weight, axis=2, keepdims=True)
    part_in = jnp.einsum("sbm,bmd->sbd", weight.astype(BF16), tokens, preferred_element_type=F32)
    part_grad = jnp.einsum("sbm,bmd->sbd", combine_b, cotangent, preferred_element_type=F32)
    stats = jnp.concatenate(
        split3(peak) + split3(mass) + [jnp.zeros((slots, imgs, 122), BF16)], axis=2
    )
    sent = jnp.concatenate([part_in.astype(BF16), stats, part_grad.astype(BF16)], axis=2)
    taken = exchange(sent.reshape(peers, rows, 2 * d + 128), "expert")

    peaks = join3(taken[:, :, d : d + 3])
    masses = join3(taken[:, :, d + 3 : d + 6])
    top = jnp.max(peaks, axis=0)
    scale = jnp.exp(peaks - top[None])
    total = jnp.sum(masses * scale, axis=0)
    slot_in_wide = jnp.sum(taken[:, :, :d].astype(F32) * scale, axis=0) / total
    slot_out_grad = jnp.sum(taken[:, :, d + 128 :].astype(F32), axis=0)
    squared = len(dp_groups(0, 2)[0])
    all_in = gather_dp(slot_in_wide.astype(BF16)).reshape(-1, d)
    all_out_grad = gather_dp(slot_out_grad.astype(BF16)).reshape(-1, d)
    mine = slot_mask(all_in.shape[0], own_slots, imgs)
    preact, activated, out_partial = expert_forward(all_in, w_in, w_out, mine)
    owned_out = reduce_dp(out_partial.reshape(squared, -1, d), rows).astype(BF16)
    in_partial, w_in_grad, w_out_grad = expert_backward(
        all_in, all_out_grad, preact, activated, w_in, w_out, mine
    )
    owned_in = reduce_dp(in_partial.reshape(squared, -1, d), rows).astype(BF16)

    col = jnp.sum(owned_in.astype(F32) * slot_in_wide, axis=1, keepdims=True)
    stats = jnp.concatenate(
        split3(top) + split3(total) + split3(col) + [jnp.zeros((rows, 119), BF16)], axis=1
    )
    back = everywhere(jnp.concatenate([owned_out, owned_in, stats], axis=1), "expert")
    back = back.reshape(slots, imgs, 2 * d + 128)
    slot_out, slot_in_grad = back[:, :, :d], back[:, :, d : 2 * d]
    top = join3(back[:, :, 2 * d : 2 * d + 3])
    total = join3(back[:, :, 2 * d + 3 : 2 * d + 6])
    col = join3(back[:, :, 2 * d + 6 : 2 * d + 9])

    dispatch = jnp.exp(logits - top) / total
    dispatch_b = dispatch.astype(BF16)
    combine_grad = jnp.einsum("bmd,sbd->sbm", cotangent, slot_out, preferred_element_type=F32)
    dispatch_grad = jnp.einsum("sbd,bmd->sbm", slot_in_grad, tokens, preferred_element_type=F32)
    row_sums = jnp.sum(combine * combine_grad, axis=0, keepdims=True)
    logit_grad = (
        dispatch * (dispatch_grad - col) + combine * (combine_grad - row_sums)
    ).astype(BF16)
    token_grad = jnp.einsum("sbm,sbd->bmd", dispatch_b, slot_in_grad, preferred_element_type=F32)
    token_grad = token_grad + jnp.einsum(
        "sbm,sd->bmd", logit_grad, params, preferred_element_type=F32
    )
    token_grad = token_grad.astype(BF16)

    share_grad = jnp.einsum("sbm,bmd->sd", logit_grad, tokens, preferred_element_type=F32)
    share_grad = jnp.sum(exchange(share_grad.reshape(peers, own_slots, d), "expert"), axis=0)
    share_grad = jnp.sum(everywhere(share_grad, "dp", dp_groups(1)), axis=0)
    share_grad = jnp.sum(everywhere(share_grad, "dp", dp_groups(0, 2)), axis=0)
    slot_grad = share_grad.T
    return (token_grad, slot_grad, w_in_grad, w_out_grad)


def solution(mesh):
    placed = (
        P("dp", "expert", None),
        P("dp", "expert", None),
        P(None, "expert"),
        P("expert", None, "dp"),
        P("expert", "dp", None),
    )
    return jax.shard_map(
        on_device,
        mesh=mesh,
        in_specs=placed,
        out_specs=(
            P("dp", "expert", None),
            P(None, "expert"),
            P("expert", None, "dp"),
            P("expert", "dp", None),
        ),
        check_vma=False,
    )
```

```python
import functools

import jax
import jax.numpy as jnp
import numpy as np
from jax import lax
from jax.experimental import pallas as pl
from jax.experimental.pallas import tpu as pltpu
from jax.sharding import PartitionSpec as P

F32 = jnp.float32
BF16 = jnp.bfloat16


def gelu_exact(value):
    return jax.nn.gelu(value, approximate=False)


def split3(value):
    high = lax.reduce_precision(value, 8, 7)
    middle = lax.reduce_precision(value - high, 8, 7)
    low = value - high - middle
    return [high.astype(BF16), middle.astype(BF16), low.astype(BF16)]


def join3(terms):
    wide = terms.astype(F32)
    return wide[..., 0:1] + wide[..., 1:2] + wide[..., 2:3]


def groups_of(axis, sizes, inner):
    shape = [lax.axis_size(axis) // sizes[0] // sizes[1], sizes[0], sizes[1]]
    ids = np.arange(lax.axis_size(axis)).reshape(shape)
    outer = [part for part in range(3) if part not in inner]
    width = int(np.prod([shape[part] for part in inner]))
    return ids.transpose(outer + list(inner)).reshape(-1, width).tolist()


def exchange(value, axis, groups=None):
    return lax.all_to_all(
        value, axis, split_axis=0, concat_axis=0, axis_index_groups=groups, tiled=True
    )


def everywhere(value, axis, groups=None):
    peers = lax.axis_size(axis) if groups is None else len(groups[0])
    return exchange(jnp.broadcast_to(value[None], (peers,) + value.shape), axis, groups)


def dp_groups(*inner):
    return groups_of("dp", (lax.axis_size("dp") // 4, 2), inner)


def plane_groups():
    peers, depth = lax.axis_size("expert"), lax.axis_size("dp") // 2
    ids = np.arange(2 * depth * peers).reshape(2, depth, peers)
    return ids.transpose(1, 0, 2).reshape(depth, 2 * peers).tolist()


def gather_dp(own):
    far = everywhere(own, "dp", dp_groups(1))
    return everywhere(far.reshape(-1, own.shape[1]), "dp", dp_groups(0, 2))


def reduce_dp(partial, rows):
    d = partial.shape[-1]
    total = jnp.sum(exchange(partial, "dp", dp_groups(0, 2)).astype(F32), axis=0).astype(BF16)
    return jnp.sum(exchange(total.reshape(-1, rows, d), "dp", dp_groups(1)).astype(F32), axis=0)


def dot(left, right, left_dim=1, right_dim=0):
    return lax.dot_general(
        left, right, (((left_dim,), (right_dim,)), ((), ())), preferred_element_type=F32
    )


def own_image(rows, columns, imgs, own_slots, share):
    row = lax.broadcasted_iota(jnp.int32, (rows, columns), 0)
    column = lax.broadcasted_iota(jnp.int32, (rows, columns), 1)
    return (row // own_slots) % imgs == column // share


def slot_rows(rows, slots, imgs, own_slots):
    row = lax.broadcasted_iota(jnp.int32, (rows, slots), 0)
    column = lax.broadcasted_iota(jnp.int32, (rows, slots), 1)
    slot = (row // (imgs * own_slots)) * own_slots + row % own_slots
    return jnp.where(slot == column, 1.0, 0.0).astype(BF16)


def lanes_of(columns, rows):
    lane = lax.broadcasted_iota(jnp.int32, (rows, 128), 1)
    block = jnp.zeros((rows, 128), F32)
    at = 0
    for value in columns:
        high = value.astype(BF16).astype(F32)
        middle = (value - high).astype(BF16).astype(F32)
        for term in (high, middle, value - high - middle):
            block = jnp.where(lane == at, term, block)
            at += 1
    return block.astype(BF16)


def column_of(block, at):
    lane = lax.broadcasted_iota(jnp.int32, block.shape, 1)
    inside = (lane >= 3 * at) & (lane < 3 * at + 3)
    return jnp.sum(jnp.where(inside, block, 0.0), axis=1, keepdims=True)


def route(imgs, own_slots, params_ref, tok_ref, cot_ref, sent_ref, logits_ref, combine_ref):
    tokens, cotangent = tok_ref[...], cot_ref[...]
    slots, d = params_ref.shape
    rows, columns = logits_ref.shape
    spread = dot(slot_rows(rows, slots, imgs, own_slots), params_ref[...]).astype(BF16)
    logits = dot(spread, tokens, 1, 1)
    mine = own_image(rows, columns, imgs, own_slots, columns // imgs)
    logits = jnp.where(mine, logits, jnp.finfo(F32).min)
    logits_ref[...] = logits
    raised = jnp.exp(logits - jnp.max(logits, axis=0, keepdims=True))
    combine = raised / jnp.sum(raised, axis=0, keepdims=True)
    combine_ref[...] = combine
    peak = jnp.max(logits, axis=1, keepdims=True)
    weight = jnp.exp(logits - peak)
    mass = jnp.sum(weight, axis=1, keepdims=True)
    sent_ref[:, :d] = dot(weight.astype(BF16), tokens).astype(BF16)
    sent_ref[:, d : d + 128] = lanes_of([peak, mass], rows)
    sent_ref[:, d + 128 :] = dot(combine.astype(BF16), cotangent).astype(BF16)


def finish(
    imgs, own_slots, back_ref, logits_ref, combine_ref, params_ref, tok_ref, cot_ref,
    token_grad_ref, share_ref,
):
    tokens, cotangent = tok_ref[...], cot_ref[...]
    slots, d = params_ref.shape
    rows = logits_ref.shape[0]
    slot_out, slot_in_grad = back_ref[:, :d], back_ref[:, d : 2 * d]
    stats = back_ref[:, 2 * d :].astype(F32)
    top, total, col = [column_of(stats, at) for at in range(3)]
    combine = combine_ref[...]
    dispatch = jnp.exp(logits_ref[...] - top) / total
    combine_grad = dot(slot_out, cotangent, 1, 1)
    dispatch_grad = dot(slot_in_grad, tokens, 1, 1)
    row_sums = jnp.sum(combine * combine_grad, axis=0, keepdims=True)
    logit_grad = dispatch * (dispatch_grad - col) + combine * (combine_grad - row_sums)
    members = slot_rows(rows, slots, imgs, own_slots)
    by_slot = dot(members, logit_grad.astype(BF16), 0, 0).astype(BF16)
    share_ref[...] = dot(by_slot, tokens).astype(BF16)
    token_grad = dot(dispatch.astype(BF16), slot_in_grad, 0, 0)
    token_grad = token_grad + dot(by_slot, params_ref[...], 0, 0)
    token_grad_ref[...] = token_grad.astype(BF16)


def call(kernel, out_shape, *operands):
    shapes = [jax.ShapeDtypeStruct(shape, dtype) for shape, dtype in out_shape]
    return pl.pallas_call(
        kernel,
        out_shape=shapes,
        compiler_params=pltpu.CompilerParams(vmem_limit_bytes=32 * 1024 * 1024),
        cost_estimate=pl.CostEstimate(flops=120_000_000, bytes_accessed=2_000_000, transcendentals=16384),
    )(*operands)


def expert_part(gathered, w_in, w_out, imgs):
    slots, d, _ = w_in.shape
    rows = slots * imgs
    blocks = (gathered.shape[0], gathered.shape[1] // (2 * rows), rows, d)
    halves = gathered.reshape(blocks[:2] + (2 * rows, d))
    all_in = halves[:, :, :rows].reshape(-1, d)
    all_out_grad = halves[:, :, rows:].reshape(-1, d)
    row = lax.broadcasted_iota(jnp.int32, (slots, all_in.shape[0], 1), 1)
    slot = lax.broadcasted_iota(jnp.int32, (slots, all_in.shape[0], 1), 0)
    mine = row % slots == slot
    preact = jnp.einsum("rd,sdh->srh", all_in, w_in, preferred_element_type=F32)
    activated_wide, pullback = jax.vjp(gelu_exact, preact)
    activated = jnp.where(mine, activated_wide, 0.0).astype(BF16)
    slot_out = jnp.einsum("srh,shd->rd", activated, w_out, preferred_element_type=F32)
    act_grad = jnp.einsum("rd,shd->srh", all_out_grad, w_out, preferred_element_type=F32)
    preact_grad = jnp.where(mine, pullback(act_grad)[0], 0.0).astype(BF16)
    slot_in_grad = jnp.einsum("srh,sdh->rd", preact_grad, w_in, preferred_element_type=F32)
    w_out_grad = jnp.einsum(
        "srh,rd->shd", activated, all_out_grad, preferred_element_type=F32
    ).astype(BF16)
    w_in_grad = jnp.einsum(
        "rd,srh->sdh", all_in, preact_grad, preferred_element_type=F32
    ).astype(BF16)
    pair = [value.astype(BF16).reshape(blocks) for value in (slot_out, slot_in_grad)]
    partial = jnp.concatenate(pair, axis=2).reshape(gathered.shape)
    return partial, w_in_grad, w_out_grad


def on_device(tokens, cotangent, slot_params, w_in, w_out):
    imgs, share, d = tokens.shape
    peers = lax.axis_size("expert")
    own_slots = slot_params.shape[1]
    slots = peers * own_slots
    rows = own_slots * imgs

    params = everywhere(slot_params.T, "expert").reshape(slots, d)
    flat_tok, flat_cot = tokens.reshape(-1, d), cotangent.reshape(-1, d)
    pairs = (peers * rows, imgs * share)
    sent, logits, combine = call(
        functools.partial(route, imgs, own_slots),
        [((peers * rows, 2 * d + 128), BF16), (pairs, F32), (pairs, F32)],
        params, flat_tok, flat_cot,
    )
    taken = exchange(sent.reshape(peers, rows, 2 * d + 128), "expert")

    peaks = join3(taken[:, :, d : d + 3])
    masses = join3(taken[:, :, d + 3 : d + 6])
    top = jnp.max(peaks, axis=0)
    scale = jnp.exp(peaks - top[None])
    total = jnp.sum(masses * scale, axis=0)
    slot_in_wide = jnp.sum(taken[:, :, :d].astype(F32) * scale, axis=0) / total
    slot_out_grad = jnp.sum(taken[:, :, d + 128 :].astype(F32), axis=0)
    own = jnp.concatenate([slot_in_wide.astype(BF16), slot_out_grad.astype(BF16)], axis=0)

    gathered = gather_dp(own)
    partial, w_in_grad, w_out_grad = expert_part(gathered, w_in, w_out, imgs)
    owned_b = reduce_dp(partial, 2 * rows).astype(BF16).reshape(2, rows, d)

    col = jnp.sum(owned_b[1].astype(F32) * slot_in_wide, axis=1, keepdims=True)
    stats = jnp.concatenate(
        split3(top) + split3(total) + split3(col) + [jnp.zeros((rows, 119), BF16)], axis=1
    )
    back = everywhere(jnp.concatenate([owned_b[0], owned_b[1], stats], axis=1), "expert")
    token_grad, share_grad = call(
        functools.partial(finish, imgs, own_slots),
        [(flat_tok.shape, BF16), ((slots, d), BF16)],
        back.reshape(peers * rows, 2 * d + 128), logits, combine, params, flat_tok, flat_cot,
    )
    token_grad = token_grad.reshape(tokens.shape)

    share_grad = jnp.broadcast_to(share_grad.reshape(1, peers, own_slots, d), (2, peers, own_slots, d))
    share_grad = exchange(
        share_grad.reshape(2 * peers, own_slots, d), ("dp", "expert"), plane_groups()
    )
    share_grad = jnp.sum(share_grad.astype(F32), axis=0).astype(BF16)
    share_grad = everywhere(share_grad, "dp", dp_groups(1, 2))
    share_grad = jnp.sum(share_grad.astype(F32), axis=0)
    slot_grad = share_grad.T
    return (token_grad, slot_grad, w_in_grad, w_out_grad)


def solution(mesh):
    placed = (
        P("dp", "expert", None),
        P("dp", "expert", None),
        P(None, "expert"),
        P("expert", None, "dp"),
        P("expert", "dp", None),
    )
    return jax.shard_map(
        on_device,
        mesh=mesh,
        in_specs=placed,
        out_specs=(
            P("dp", "expert", None),
            P(None, "expert"),
            P("expert", None, "dp"),
            P("expert", "dp", None),
        ),
        check_vma=False,
    )
```

```python
import functools

import jax
import jax.numpy as jnp
import numpy as np
from jax import lax
from jax.experimental import pallas as pl
from jax.sharding import PartitionSpec as P

F32 = jnp.float32
BF16 = jnp.bfloat16


def gelu_exact(value):
    return jax.nn.gelu(value, approximate=False)


def split3(value):
    high = lax.reduce_precision(value, 8, 7)
    middle = lax.reduce_precision(value - high, 8, 7)
    low = value - high - middle
    return [high.astype(BF16), middle.astype(BF16), low.astype(BF16)]


def join3(terms):
    wide = terms.astype(F32)
    return wide[..., 0:1] + wide[..., 1:2] + wide[..., 2:3]


def groups_of(axis, sizes, inner):
    shape = [lax.axis_size(axis) // sizes[0] // sizes[1], sizes[0], sizes[1]]
    ids = np.arange(lax.axis_size(axis)).reshape(shape)
    outer = [part for part in range(3) if part not in inner]
    width = int(np.prod([shape[part] for part in inner]))
    return ids.transpose(outer + list(inner)).reshape(-1, width).tolist()


def exchange(value, axis, groups=None):
    return lax.all_to_all(
        value, axis, split_axis=0, concat_axis=0, axis_index_groups=groups, tiled=True
    )


def everywhere(value, axis, groups=None):
    peers = lax.axis_size(axis) if groups is None else len(groups[0])
    return exchange(jnp.broadcast_to(value[None], (peers,) + value.shape), axis, groups)


def dp_groups(*inner):
    return groups_of("dp", (lax.axis_size("dp") // 4, 2), inner)


def plane_groups():
    peers, depth = lax.axis_size("expert"), lax.axis_size("dp") // 2
    ids = np.arange(2 * depth * peers).reshape(2, depth, peers)
    return ids.transpose(1, 0, 2).reshape(depth, 2 * peers).tolist()


def across_y(value):
    depth = lax.axis_size("dp") // 2
    pairs = [(y * depth + z, (1 - y) * depth + z) for y in range(2) for z in range(depth)]
    return lax.ppermute(value, "dp", pairs)


def gather_z(own, beside):
    far = everywhere(own, "dp", dp_groups(1)).reshape(-1, own.shape[1])
    far, beside = lax.optimization_barrier((far, beside))
    return everywhere(far, "dp", dp_groups(2)), beside


def reduce_z(partial, rows):
    d = partial.shape[-1]
    total = jnp.sum(exchange(partial, "dp", dp_groups(2)).astype(F32), axis=0).astype(BF16)
    return jnp.sum(exchange(total.reshape(-1, rows, d), "dp", dp_groups(1)).astype(F32), axis=0)


def dot(left, right, left_dim=1, right_dim=0):
    return lax.dot_general(
        left, right, (((left_dim,), (right_dim,)), ((), ())), preferred_element_type=F32
    )


def own_image(rows, columns, imgs, own_slots, share):
    row = lax.broadcasted_iota(jnp.int32, (rows, columns), 0)
    column = lax.broadcasted_iota(jnp.int32, (rows, columns), 1)
    return (row // own_slots) % imgs == column // share


def slot_rows(rows, slots, imgs, own_slots):
    row = lax.broadcasted_iota(jnp.int32, (rows, slots), 0)
    column = lax.broadcasted_iota(jnp.int32, (rows, slots), 1)
    slot = (row // (imgs * own_slots)) * own_slots + row % own_slots
    return jnp.where(slot == column, 1.0, 0.0).astype(BF16)


def lanes_of(columns, rows):
    lane = lax.broadcasted_iota(jnp.int32, (rows, 128), 1)
    block = jnp.zeros((rows, 128), F32)
    at = 0
    for value in columns:
        high = value.astype(BF16).astype(F32)
        middle = (value - high).astype(BF16).astype(F32)
        for term in (high, middle, value - high - middle):
            block = jnp.where(lane == at, term, block)
            at += 1
    return block.astype(BF16)


def column_of(block, at):
    lane = lax.broadcasted_iota(jnp.int32, block.shape, 1)
    inside = (lane >= 3 * at) & (lane < 3 * at + 3)
    return jnp.sum(jnp.where(inside, block, 0.0), axis=1, keepdims=True)


def route(imgs, own_slots, params_ref, tok_ref, cot_ref, sent_ref, logits_ref, combine_ref):
    tokens, cotangent = tok_ref[...], cot_ref[...]
    slots, d = params_ref.shape
    rows, columns = logits_ref.shape
    spread = dot(slot_rows(rows, slots, imgs, own_slots), params_ref[...]).astype(BF16)
    logits = dot(spread, tokens, 1, 1)
    mine = own_image(rows, columns, imgs, own_slots, columns // imgs)
    logits = jnp.where(mine, logits, jnp.finfo(F32).min)
    logits_ref[...] = logits
    raised = jnp.exp(logits - jnp.max(logits, axis=0, keepdims=True))
    combine = raised / jnp.sum(raised, axis=0, keepdims=True)
    combine_ref[...] = combine
    peak = jnp.max(logits, axis=1, keepdims=True)
    weight = jnp.exp(logits - peak)
    mass = jnp.sum(weight, axis=1, keepdims=True)
    sent_ref[:, :d] = dot(weight.astype(BF16), tokens).astype(BF16)
    sent_ref[:, d : d + 128] = lanes_of([peak, mass], rows)
    sent_ref[:, d + 128 :] = dot(combine.astype(BF16), cotangent).astype(BF16)


def finish(
    imgs, own_slots, back_ref, logits_ref, combine_ref, params_ref, tok_ref, cot_ref,
    token_grad_ref, share_ref,
):
    tokens, cotangent = tok_ref[...], cot_ref[...]
    slots, d = params_ref.shape
    rows = logits_ref.shape[0]
    slot_out, slot_in_grad = back_ref[:, :d], back_ref[:, d : 2 * d]
    stats = back_ref[:, 2 * d :].astype(F32)
    top, total, col = [column_of(stats, at) for at in range(3)]
    combine = combine_ref[...]
    dispatch = jnp.exp(logits_ref[...] - top) / total
    combine_grad = dot(slot_out, cotangent, 1, 1)
    dispatch_grad = dot(slot_in_grad, tokens, 1, 1)
    row_sums = jnp.sum(combine * combine_grad, axis=0, keepdims=True)
    logit_grad = dispatch * (dispatch_grad - col) + combine * (combine_grad - row_sums)
    members = slot_rows(rows, slots, imgs, own_slots)
    by_slot = dot(members, logit_grad.astype(BF16), 0, 0).astype(BF16)
    share_ref[...] = dot(by_slot, tokens).astype(BF16)
    token_grad = dot(dispatch.astype(BF16), slot_in_grad, 0, 0)
    token_grad = token_grad + dot(by_slot, params_ref[...], 0, 0)
    token_grad_ref[...] = token_grad.astype(BF16)


def call(kernel, out_shape, *operands):
    shapes = [jax.ShapeDtypeStruct(shape, dtype) for shape, dtype in out_shape]
    return pl.pallas_call(
        kernel,
        out_shape=shapes,
        cost_estimate=pl.CostEstimate(flops=120_000_000, bytes_accessed=2_000_000, transcendentals=16384),
    )(*operands)


def halves_of(gathered, rows):
    d = gathered.shape[-1]
    blocks = gathered.reshape(-1, 2 * rows, d)
    return blocks[:, :rows].reshape(-1, d), blocks[:, rows:].reshape(-1, d)


def own_slot(rows, slots):
    row = lax.broadcasted_iota(jnp.int32, (slots, rows, 1), 1)
    slot = lax.broadcasted_iota(jnp.int32, (slots, rows, 1), 0)
    return row % slots == slot


def hidden_forward(all_in, w_in, mine):
    preact = jnp.einsum("rd,shd->srh", all_in, w_in, preferred_element_type=F32)
    return preact, jnp.where(mine, gelu_exact(preact), 0.0).astype(BF16)


def hidden_backward(all_out_grad, preact, w_out, mine):
    _, pullback = jax.vjp(gelu_exact, preact)
    act_grad = jnp.einsum("rd,shd->srh", all_out_grad, w_out, preferred_element_type=F32)
    return jnp.where(mine, pullback(act_grad)[0], 0.0).astype(BF16)


def expert_part(gathered, weights, rows):
    all_in, all_out_grad = halves_of(gathered, rows)
    mine = own_slot(all_in.shape[0], weights[0].shape[1])
    slot_out, slot_in_grad = 0.0, 0.0
    for w_in, w_out in weights:
        preact, activated = hidden_forward(all_in, w_in, mine)
        preact_grad = hidden_backward(all_out_grad, preact, w_out, mine)
        slot_out += jnp.einsum("srh,shd->rd", activated, w_out, preferred_element_type=F32)
        slot_in_grad += jnp.einsum("srh,shd->rd", preact_grad, w_in, preferred_element_type=F32)
    blocks = (gathered.shape[0], -1, rows, gathered.shape[2])
    pair = [value.astype(BF16).reshape(blocks) for value in (slot_out, slot_in_grad)]
    return jnp.concatenate(pair, axis=2).reshape(gathered.shape)


def weight_grads(gathered, w_in, w_out, rows):
    all_in, all_out_grad = halves_of(gathered, rows)
    mine = own_slot(all_in.shape[0], w_in.shape[0])
    preact, activated = hidden_forward(all_in, w_in, mine)
    preact_grad = hidden_backward(all_out_grad, preact, w_out, mine)
    w_out_grad = jnp.einsum("srh,rd->shd", activated, all_out_grad, preferred_element_type=F32)
    w_in_grad = jnp.einsum("rd,srh->sdh", all_in, preact_grad, preferred_element_type=F32)
    return w_in_grad.astype(BF16), w_out_grad.astype(BF16)


def on_device(tokens, cotangent, slot_params, w_in, w_out):
    imgs, share, d = tokens.shape
    peers = lax.axis_size("expert")
    own_slots = slot_params.shape[1]
    slots = peers * own_slots
    rows = own_slots * imgs

    params = everywhere(slot_params.T, "expert").reshape(slots, d)
    flat_tok, flat_cot = tokens.reshape(-1, d), cotangent.reshape(-1, d)
    pairs = (peers * rows, imgs * share)
    sent, logits, combine = call(
        functools.partial(route, imgs, own_slots),
        [((peers * rows, 2 * d + 128), BF16), (pairs, F32), (pairs, F32)],
        params, flat_tok, flat_cot,
    )
    taken = exchange(sent.reshape(peers, rows, 2 * d + 128), "expert")
    weights = jnp.stack([jnp.swapaxes(w_in, 1, 2), w_out])
    weights, taken = lax.optimization_barrier((weights, taken))
    weights_y = across_y(weights)

    peaks = join3(taken[:, :, d : d + 3])
    masses = join3(taken[:, :, d + 3 : d + 6])
    top = jnp.max(peaks, axis=0)
    scale = jnp.exp(peaks - top[None])
    total = jnp.sum(masses * scale, axis=0)
    slot_in_wide = jnp.sum(taken[:, :, :d].astype(F32) * scale, axis=0) / total
    slot_out_grad = jnp.sum(taken[:, :, d + 128 :].astype(F32), axis=0)
    own = jnp.concatenate([slot_in_wide.astype(BF16), slot_out_grad.astype(BF16)], axis=0)

    gathered, weights_y = gather_z(own, weights_y)
    partial = expert_part(gathered, (weights, weights_y), rows)
    gathered, partial = lax.optimization_barrier((gathered, partial))
    gathered_y = across_y(gathered)
    owned_b = reduce_z(partial, 2 * rows).astype(BF16)
    owned_b, gathered_y = lax.optimization_barrier((owned_b, gathered_y))
    owned_b = owned_b.reshape(2, rows, d)

    col = jnp.sum(owned_b[1].astype(F32) * slot_in_wide, axis=1, keepdims=True)
    stats = jnp.concatenate(
        split3(top) + split3(total) + split3(col) + [jnp.zeros((rows, 119), BF16)], axis=1
    )
    back = everywhere(jnp.concatenate([owned_b[0], owned_b[1], stats], axis=1), "expert")
    token_grad, share_grad = call(
        functools.partial(finish, imgs, own_slots),
        [(flat_tok.shape, BF16), ((slots, d), BF16)],
        back.reshape(peers * rows, 2 * d + 128), logits, combine, params, flat_tok, flat_cot,
    )
    token_grad = token_grad.reshape(tokens.shape)

    share_grad, gathered, gathered_y = lax.optimization_barrier((share_grad, gathered, gathered_y))
    both = jnp.concatenate([gathered, gathered_y], axis=0)
    w_in_grad, w_out_grad = weight_grads(both, weights[0], weights[1], rows)
    share_grad = jnp.broadcast_to(share_grad.reshape(1, peers, own_slots, d), (2, peers, own_slots, d))
    share_grad = exchange(
        share_grad.reshape(2 * peers, own_slots, d), ("dp", "expert"), plane_groups()
    )
    share_grad = jnp.sum(share_grad.astype(F32), axis=0).astype(BF16)
    share_grad = everywhere(share_grad, "dp", dp_groups(1, 2))
    share_grad = jnp.sum(share_grad.astype(F32), axis=0)
    slot_grad = share_grad.T
    return (token_grad, slot_grad, w_in_grad, w_out_grad)


def solution(mesh):
    placed = (
        P("dp", "expert", None),
        P("dp", "expert", None),
        P(None, "expert"),
        P("expert", None, "dp"),
        P("expert", "dp", None),
    )
    return jax.shard_map(
        on_device,
        mesh=mesh,
        in_specs=placed,
        out_specs=(
            P("dp", "expert", None),
            P(None, "expert"),
            P("expert", None, "dp"),
            P("expert", "dp", None),
        ),
        check_vma=False,
    )
```

```python
import functools

import jax
import jax.numpy as jnp
import numpy as np
from jax import lax
from jax.experimental import pallas as pl
from jax.experimental.pallas import tpu as pltpu
from jax.sharding import PartitionSpec as P

F32 = jnp.float32
BF16 = jnp.bfloat16


def gelu_and_slope(value):
    below = 0.5 * (1.0 + lax.erf(value * 0.5**0.5))
    density = jnp.exp(-0.5 * value * value) * (1.0 / (2.0 * np.pi) ** 0.5)
    return value * below, below + value * density


def split3(value):
    high = lax.reduce_precision(value, 8, 7)
    middle = lax.reduce_precision(value - high, 8, 7)
    low = value - high - middle
    return [high.astype(BF16), middle.astype(BF16), low.astype(BF16)]


def join3(terms):
    wide = terms.astype(F32)
    return wide[..., 0:1] + wide[..., 1:2] + wide[..., 2:3]


def groups_of(axis, sizes, inner):
    shape = [lax.axis_size(axis) // sizes[0] // sizes[1], sizes[0], sizes[1]]
    ids = np.arange(lax.axis_size(axis)).reshape(shape)
    outer = [part for part in range(3) if part not in inner]
    width = int(np.prod([shape[part] for part in inner]))
    return ids.transpose(outer + list(inner)).reshape(-1, width).tolist()


def exchange(value, axis, groups=None):
    return lax.all_to_all(
        value, axis, split_axis=0, concat_axis=0, axis_index_groups=groups, tiled=True
    )


def everywhere(value, axis, groups=None):
    peers = lax.axis_size(axis) if groups is None else len(groups[0])
    return exchange(jnp.broadcast_to(value[None], (peers,) + value.shape), axis, groups)


def dp_groups(*inner):
    return groups_of("dp", (lax.axis_size("dp") // 4, 2), inner)


def plane_groups():
    peers, depth = lax.axis_size("expert"), lax.axis_size("dp") // 2
    ids = np.arange(2 * depth * peers).reshape(2, depth, peers)
    return ids.transpose(1, 0, 2).reshape(depth, 2 * peers).tolist()


def across_y(value):
    depth = lax.axis_size("dp") // 2
    pairs = [(y * depth + z, (1 - y) * depth + z) for y in range(2) for z in range(depth)]
    return lax.ppermute(value, "dp", pairs)


def gather_z(own, beside):
    far = everywhere(own, "dp", dp_groups(1)).reshape(-1, own.shape[1])
    far, beside = lax.optimization_barrier((far, beside))
    return everywhere(far, "dp", dp_groups(2)), beside


def reduce_z(partial, rows, beside):
    d = partial.shape[-1]
    total = jnp.sum(exchange(partial, "dp", dp_groups(2)).astype(F32), axis=0).astype(BF16)
    total, beside = lax.optimization_barrier((total, beside))
    total = jnp.sum(exchange(total.reshape(-1, rows, d), "dp", dp_groups(1)).astype(F32), axis=0)
    return total, beside


def dot(left, right, left_dim=1, right_dim=0):
    return lax.dot_general(
        left, right, (((left_dim,), (right_dim,)), ((), ())), preferred_element_type=F32
    )


def own_image(rows, columns, imgs, own_slots, share):
    row = lax.broadcasted_iota(jnp.int32, (rows, columns), 0)
    column = lax.broadcasted_iota(jnp.int32, (rows, columns), 1)
    return (row // own_slots) % imgs == column // share


def slot_rows(rows, slots, imgs, own_slots):
    row = lax.broadcasted_iota(jnp.int32, (rows, slots), 0)
    column = lax.broadcasted_iota(jnp.int32, (rows, slots), 1)
    slot = (row // (imgs * own_slots)) * own_slots + row % own_slots
    return jnp.where(slot == column, 1.0, 0.0).astype(BF16)


def lanes_of(columns, rows):
    lane = lax.broadcasted_iota(jnp.int32, (rows, 128), 1)
    block = jnp.zeros((rows, 128), F32)
    at = 0
    for value in columns:
        high = value.astype(BF16).astype(F32)
        middle = (value - high).astype(BF16).astype(F32)
        for term in (high, middle, value - high - middle):
            block = jnp.where(lane == at, term, block)
            at += 1
    return block.astype(BF16)


def column_of(block, at):
    lane = lax.broadcasted_iota(jnp.int32, block.shape, 1)
    inside = (lane >= 3 * at) & (lane < 3 * at + 3)
    return jnp.sum(jnp.where(inside, block, 0.0), axis=1, keepdims=True)


def route(imgs, own_slots, params_ref, tok_ref, cot_ref, sent_ref, logits_ref, combine_ref):
    tokens, cotangent = tok_ref[...], cot_ref[...]
    slots, d = params_ref.shape
    rows, columns = logits_ref.shape
    spread = dot(slot_rows(rows, slots, imgs, own_slots), params_ref[...]).astype(BF16)
    logits = dot(spread, tokens, 1, 1)
    mine = own_image(rows, columns, imgs, own_slots, columns // imgs)
    logits = jnp.where(mine, logits, jnp.finfo(F32).min)
    logits_ref[...] = logits
    raised = jnp.exp(logits - jnp.max(logits, axis=0, keepdims=True))
    combine = raised / jnp.sum(raised, axis=0, keepdims=True)
    combine_ref[...] = combine
    peak = jnp.max(logits, axis=1, keepdims=True)
    weight = jnp.exp(logits - peak)
    mass = jnp.sum(weight, axis=1, keepdims=True)
    sent_ref[:, :d] = dot(weight.astype(BF16), tokens).astype(BF16)
    sent_ref[:, d : d + 128] = lanes_of([peak, mass], rows)
    sent_ref[:, d + 128 :] = dot(combine.astype(BF16), cotangent).astype(BF16)


def finish(
    imgs, own_slots, back_ref, logits_ref, combine_ref, params_ref, tok_ref, cot_ref,
    token_grad_ref, share_ref,
):
    tokens, cotangent = tok_ref[...], cot_ref[...]
    slots, d = params_ref.shape
    rows = logits_ref.shape[0]
    slot_out, slot_in_grad = back_ref[:, :d], back_ref[:, d : 2 * d]
    stats = back_ref[:, 2 * d :].astype(F32)
    top, total, col = [column_of(stats, at) for at in range(3)]
    combine = combine_ref[...]
    dispatch = jnp.exp(logits_ref[...] - top) / total
    combine_grad = dot(slot_out, cotangent, 1, 1)
    dispatch_grad = dot(slot_in_grad, tokens, 1, 1)
    row_sums = jnp.sum(combine * combine_grad, axis=0, keepdims=True)
    logit_grad = dispatch * (dispatch_grad - col) + combine * (combine_grad - row_sums)
    members = slot_rows(rows, slots, imgs, own_slots)
    by_slot = dot(members, logit_grad.astype(BF16), 0, 0).astype(BF16)
    share_ref[...] = dot(by_slot, tokens).astype(BF16)
    token_grad = dot(dispatch.astype(BF16), slot_in_grad, 0, 0)
    token_grad = token_grad + dot(by_slot, params_ref[...], 0, 0)
    token_grad_ref[...] = token_grad.astype(BF16)


def call(kernel, out_shape, flops, *operands):
    shapes = [jax.ShapeDtypeStruct(shape, dtype) for shape, dtype in out_shape]
    size = sum(value.size * value.dtype.itemsize for value in list(operands) + shapes)
    return pl.pallas_call(
        kernel,
        out_shape=shapes,
        compiler_params=pltpu.CompilerParams(vmem_limit_bytes=32 * 1024 * 1024),
        cost_estimate=pl.CostEstimate(flops=flops, bytes_accessed=size, transcendentals=16384),
    )(*operands)


def picked(gathered, half, block):
    total = gathered.shape[0]
    row = lax.broadcasted_iota(jnp.int32, (total // 2, total), 0)
    column = lax.broadcasted_iota(jnp.int32, (total // 2, total), 1)
    here = (row // block) * (2 * block) + half * block + row % block == column
    select = jnp.where(here, 1.0, 0.0).astype(BF16)
    return dot(select, gathered).astype(BF16), select


def hidden(all_in, all_out_grad, w_in, w_out, own_slots):
    shape = (all_in.shape[0], w_in.shape[0])
    row = lax.broadcasted_iota(jnp.int32, shape, 0)
    column = lax.broadcasted_iota(jnp.int32, shape, 1)
    mine = row % own_slots == column // (shape[1] // own_slots)
    activated, slope = gelu_and_slope(dot(all_in, w_in, 1, 1))
    preact_grad = dot(all_out_grad, w_out, 1, 1) * slope
    return (
        jnp.where(mine, activated, 0.0).astype(BF16),
        jnp.where(mine, preact_grad, 0.0).astype(BF16),
    )


def experts(block, own_slots, gathered_ref, own_ref, other_ref, partial_ref):
    gathered = gathered_ref[...]
    all_in, first = picked(gathered, 0, block)
    all_out_grad, second = picked(gathered, 1, block)
    slot_out = jnp.zeros(all_in.shape, F32)
    slot_in_grad = jnp.zeros(all_in.shape, F32)
    for weights_ref in (own_ref, other_ref):
        w_in, w_out = weights_ref[0], weights_ref[1]
        activated, preact_grad = hidden(all_in, all_out_grad, w_in, w_out, own_slots)
        slot_out += dot(activated, w_out)
        slot_in_grad += dot(preact_grad, w_in)
    partial = dot(first, slot_out.astype(BF16), 0, 0) + dot(second, slot_in_grad.astype(BF16), 0, 0)
    partial_ref[...] = partial.astype(BF16)


def weight_grads(
    block, own_slots, gathered_ref, other_ref, weights_ref, w_in_grad_ref, w_out_grad_ref
):
    w_in, w_out = weights_ref[0], weights_ref[1]
    w_in_grad = jnp.zeros(w_in.shape, F32)
    w_out_grad = jnp.zeros(w_out.shape, F32)
    for rows_ref in (gathered_ref, other_ref):
        rows = rows_ref[...]
        all_in, all_out_grad = picked(rows, 0, block)[0], picked(rows, 1, block)[0]
        activated, preact_grad = hidden(all_in, all_out_grad, w_in, w_out, own_slots)
        w_in_grad += dot(preact_grad, all_in, 0, 0)
        w_out_grad += dot(activated, all_out_grad, 0, 0)
    w_in_grad_ref[...] = w_in_grad.astype(BF16)
    w_out_grad_ref[...] = w_out_grad.astype(BF16)


def on_device(tokens, cotangent, slot_params, w_in, w_out):
    imgs, share, d = tokens.shape
    peers = lax.axis_size("expert")
    own_slots = slot_params.shape[1]
    slots = peers * own_slots
    rows = own_slots * imgs

    params = everywhere(slot_params.T, "expert").reshape(slots, d)
    flat_tok, flat_cot = tokens.reshape(-1, d), cotangent.reshape(-1, d)
    pairs = (peers * rows, imgs * share)
    sent, logits, combine = call(
        functools.partial(route, imgs, own_slots),
        [((peers * rows, 2 * d + 128), BF16), (pairs, F32), (pairs, F32)],
        100_000_000, params, flat_tok, flat_cot,
    )
    taken = exchange(sent.reshape(peers, rows, 2 * d + 128), "expert")
    weights = jnp.stack([jnp.swapaxes(w_in, 1, 2).reshape(-1, d), w_out.reshape(-1, d)])
    weights, head = lax.optimization_barrier((weights, taken[:, :, d : d + 128]))
    weights_y = across_y(weights)

    peaks = join3(head[:, :, :3])
    masses = join3(head[:, :, 3:6])
    top = jnp.max(peaks, axis=0)
    scale = jnp.exp(peaks - top[None])
    total = jnp.sum(masses * scale, axis=0)
    slot_in_wide = jnp.sum(taken[:, :, :d].astype(F32) * scale, axis=0) / total
    slot_out_grad = jnp.sum(taken[:, :, d + 128 :].astype(F32), axis=0)
    own = jnp.concatenate([slot_in_wide.astype(BF16), slot_out_grad.astype(BF16)], axis=0)

    gathered, weights_y = gather_z(own, weights_y)
    gathered_y = across_y(gathered)
    flat = gathered.reshape(-1, d)
    (partial,) = call(
        functools.partial(experts, rows, own_slots), [(flat.shape, BF16)], 1_400_000_000,
        flat, weights, weights_y,
    )
    owned_b, gathered_y = reduce_z(partial.reshape(gathered.shape), 2 * rows, gathered_y)
    owned_b = owned_b.astype(BF16).reshape(2, rows, d)
    w_in_grad, w_out_grad = call(
        functools.partial(weight_grads, rows, own_slots), [(weights.shape[1:], BF16)] * 2,
        1_400_000_000, flat, gathered_y.reshape(-1, d), weights,
    )
    w_in_grad = jnp.swapaxes(w_in_grad.reshape(own_slots, -1, d), 1, 2)
    w_out_grad = w_out_grad.reshape(w_out.shape)

    col = jnp.sum(owned_b[1].astype(F32) * slot_in_wide, axis=1, keepdims=True)
    stats = jnp.concatenate(
        split3(top) + split3(total) + split3(col) + [jnp.zeros((rows, 119), BF16)], axis=1
    )
    back = everywhere(jnp.concatenate([owned_b[0], owned_b[1], stats], axis=1), "expert")
    token_grad, share_grad = call(
        functools.partial(finish, imgs, own_slots),
        [(flat_tok.shape, BF16), ((slots, d), BF16)],
        100_000_000, back.reshape(peers * rows, 2 * d + 128), logits, combine, params, flat_tok, flat_cot,
    )
    token_grad = token_grad.reshape(tokens.shape)

    share_grad = jnp.broadcast_to(share_grad.reshape(1, peers, own_slots, d), (2, peers, own_slots, d))
    share_grad = exchange(
        share_grad.reshape(2 * peers, own_slots, d), ("dp", "expert"), plane_groups()
    )
    share_grad = jnp.sum(share_grad.astype(F32), axis=0).astype(BF16)
    share_grad = everywhere(share_grad, "dp", dp_groups(1, 2))
    share_grad = jnp.sum(share_grad.astype(F32), axis=0)
    slot_grad = share_grad.T
    return (token_grad, slot_grad, w_in_grad, w_out_grad)


def solution(mesh):
    placed = (
        P("dp", "expert", None),
        P("dp", "expert", None),
        P(None, "expert"),
        P("expert", None, "dp"),
        P("expert", "dp", None),
    )
    return jax.shard_map(
        on_device,
        mesh=mesh,
        in_specs=placed,
        out_specs=(
            P("dp", "expert", None),
            P(None, "expert"),
            P("expert", None, "dp"),
            P("expert", "dp", None),
        ),
        check_vma=False,
    )
```

```python
import functools

import jax
import jax.numpy as jnp
import numpy as np
from jax import lax
from jax.experimental import pallas as pl
from jax.experimental.pallas import tpu as pltpu
from jax.sharding import PartitionSpec as P

F32 = jnp.float32
BF16 = jnp.bfloat16


def gelu_and_slope(value):
    below = 0.5 * (1.0 + lax.erf(value * 0.5**0.5))
    density = jnp.exp(-0.5 * value * value) * (1.0 / (2.0 * np.pi) ** 0.5)
    return value * below, below + value * density


def split3(value):
    high = lax.reduce_precision(value, 8, 7)
    middle = lax.reduce_precision(value - high, 8, 7)
    low = value - high - middle
    return [high.astype(BF16), middle.astype(BF16), low.astype(BF16)]


def join3(terms):
    wide = terms.astype(F32)
    return wide[..., 0:1] + wide[..., 1:2] + wide[..., 2:3]


def groups_of(axis, sizes, inner):
    shape = [lax.axis_size(axis) // sizes[0] // sizes[1], sizes[0], sizes[1]]
    ids = np.arange(lax.axis_size(axis)).reshape(shape)
    outer = [part for part in range(3) if part not in inner]
    width = int(np.prod([shape[part] for part in inner]))
    return ids.transpose(outer + list(inner)).reshape(-1, width).tolist()


def exchange(value, axis, groups=None):
    return lax.all_to_all(
        value, axis, split_axis=0, concat_axis=0, axis_index_groups=groups, tiled=True
    )


def everywhere(value, axis, groups=None):
    peers = lax.axis_size(axis) if groups is None else len(groups[0])
    return exchange(jnp.broadcast_to(value[None], (peers,) + value.shape), axis, groups)


def dp_groups(*inner):
    return groups_of("dp", (lax.axis_size("dp") // 4, 2), inner)


def plane_groups():
    peers, depth = lax.axis_size("expert"), lax.axis_size("dp") // 2
    ids = np.arange(2 * depth * peers).reshape(2, depth, peers)
    return ids.transpose(1, 0, 2).reshape(depth, 2 * peers).tolist()


def across_y(value):
    depth = lax.axis_size("dp") // 2
    pairs = [(y * depth + z, (1 - y) * depth + z) for y in range(2) for z in range(depth)]
    return lax.ppermute(value, "dp", pairs)


def gather_z(own, beside):
    far = everywhere(own, "dp", dp_groups(1)).reshape(-1, own.shape[1])
    far, beside = lax.optimization_barrier((far, beside))
    return everywhere(far, "dp", dp_groups(2)), beside


def reduce_z(partial, rows, beside):
    d = partial.shape[-1]
    total = jnp.sum(exchange(partial, "dp", dp_groups(2)).astype(F32), axis=0).astype(BF16)
    total, beside = lax.optimization_barrier((total, beside))
    beside = across_y(beside)
    total = jnp.sum(exchange(total.reshape(-1, rows, d), "dp", dp_groups(1)).astype(F32), axis=0)
    return lax.optimization_barrier((total, beside))


def dot(left, right, left_dim=1, right_dim=0):
    return lax.dot_general(
        left, right, (((left_dim,), (right_dim,)), ((), ())), preferred_element_type=F32
    )


def own_image(rows, columns, imgs, own_slots, share):
    row = lax.broadcasted_iota(jnp.int32, (rows, columns), 0)
    column = lax.broadcasted_iota(jnp.int32, (rows, columns), 1)
    return (row // own_slots) % imgs == column // share


def slot_rows(rows, slots, imgs, own_slots):
    row = lax.broadcasted_iota(jnp.int32, (rows, slots), 0)
    column = lax.broadcasted_iota(jnp.int32, (rows, slots), 1)
    slot = (row // (imgs * own_slots)) * own_slots + row % own_slots
    return jnp.where(slot == column, 1.0, 0.0).astype(BF16)


def lanes_of(columns, rows):
    lane = lax.broadcasted_iota(jnp.int32, (rows, 128), 1)
    block = jnp.zeros((rows, 128), F32)
    at = 0
    for value in columns:
        high = value.astype(BF16).astype(F32)
        middle = (value - high).astype(BF16).astype(F32)
        for term in (high, middle, value - high - middle):
            block = jnp.where(lane == at, term, block)
            at += 1
    return block.astype(BF16)


def column_of(block, at):
    lane = lax.broadcasted_iota(jnp.int32, block.shape, 1)
    inside = (lane >= 3 * at) & (lane < 3 * at + 3)
    return jnp.sum(jnp.where(inside, block, 0.0), axis=1, keepdims=True)


def route(imgs, own_slots, params_ref, both_ref, sent_ref, logits_ref, combine_ref):
    tokens, cotangent = both_ref[0], both_ref[1]
    slots, d = params_ref.shape
    rows, columns = logits_ref.shape
    spread = dot(slot_rows(rows, slots, imgs, own_slots), params_ref[...]).astype(BF16)
    logits = dot(spread, tokens, 1, 1)
    mine = own_image(rows, columns, imgs, own_slots, columns // imgs)
    logits = jnp.where(mine, logits, jnp.finfo(F32).min)
    logits_ref[...] = logits
    raised = jnp.exp(logits - jnp.max(logits, axis=0, keepdims=True))
    combine = raised / jnp.sum(raised, axis=0, keepdims=True)
    combine_ref[...] = combine
    peak = jnp.max(logits, axis=1, keepdims=True)
    weight = jnp.exp(logits - peak)
    mass = jnp.sum(weight, axis=1, keepdims=True)
    sent_ref[:, :d] = dot(weight.astype(BF16), tokens).astype(BF16)
    sent_ref[:, d : d + 128] = lanes_of([peak, mass], rows)
    sent_ref[:, d + 128 :] = dot(combine.astype(BF16), cotangent).astype(BF16)


def finish(
    imgs, own_slots, back_ref, logits_ref, combine_ref, params_ref, both_ref,
    token_grad_ref, share_ref,
):
    tokens, cotangent = both_ref[0], both_ref[1]
    slots, d = params_ref.shape
    rows = logits_ref.shape[0]
    slot_out, slot_in_grad = back_ref[:, :d], back_ref[:, d : 2 * d]
    stats = back_ref[:, 2 * d :].astype(F32)
    top, total, col = [column_of(stats, at) for at in range(3)]
    combine = combine_ref[...]
    dispatch = jnp.exp(logits_ref[...] - top) / total
    combine_grad = dot(slot_out, cotangent, 1, 1)
    dispatch_grad = dot(slot_in_grad, tokens, 1, 1)
    row_sums = jnp.sum(combine * combine_grad, axis=0, keepdims=True)
    logit_grad = dispatch * (dispatch_grad - col) + combine * (combine_grad - row_sums)
    members = slot_rows(rows, slots, imgs, own_slots)
    by_slot = dot(members, logit_grad.astype(BF16), 0, 0).astype(BF16)
    share_ref[...] = dot(by_slot, tokens).astype(BF16)
    token_grad = dot(dispatch.astype(BF16), slot_in_grad, 0, 0)
    token_grad = token_grad + dot(by_slot, params_ref[...], 0, 0)
    token_grad_ref[...] = token_grad.astype(BF16)


def call(kernel, out_shape, flops, *operands):
    shapes = [jax.ShapeDtypeStruct(shape, dtype) for shape, dtype in out_shape]
    size = sum(value.size * value.dtype.itemsize for value in list(operands) + shapes)
    return pl.pallas_call(
        kernel,
        out_shape=shapes,
        compiler_params=pltpu.CompilerParams(vmem_limit_bytes=32 * 1024 * 1024),
        cost_estimate=pl.CostEstimate(flops=flops, bytes_accessed=size, transcendentals=16384),
    )(*operands)


def picked(gathered, half, block):
    total = gathered.shape[0]
    row = lax.broadcasted_iota(jnp.int32, (total // 2, total), 0)
    column = lax.broadcasted_iota(jnp.int32, (total // 2, total), 1)
    here = (row // block) * (2 * block) + half * block + row % block == column
    select = jnp.where(here, 1.0, 0.0).astype(BF16)
    return dot(select, gathered).astype(BF16), select


def hidden(all_in, all_out_grad, w_in, w_out, own_slots):
    shape = (all_in.shape[0], w_in.shape[0])
    row = lax.broadcasted_iota(jnp.int32, shape, 0)
    column = lax.broadcasted_iota(jnp.int32, shape, 1)
    mine = row % own_slots == column // (shape[1] // own_slots)
    activated, slope = gelu_and_slope(dot(all_in, w_in, 1, 1))
    preact_grad = dot(all_out_grad, w_out, 1, 1) * slope
    return (
        jnp.where(mine, activated, 0.0).astype(BF16),
        jnp.where(mine, preact_grad, 0.0).astype(BF16),
    )


def experts(
    block, own_slots, gathered_ref, w_in_ref, w_out_ref, early_ref, late_ref, partial_ref
):
    gathered = gathered_ref[...]
    all_in, first = picked(gathered, 0, block)
    all_out_grad, second = picked(gathered, 1, block)
    slot_out = jnp.zeros(all_in.shape, F32)
    slot_in_grad = jnp.zeros(all_in.shape, F32)
    rest = w_in_ref.shape[0] - early_ref.shape[0]
    other_in = jnp.concatenate([early_ref[...], late_ref[:rest]], axis=0)
    for w_in, w_out in ((w_in_ref[...], w_out_ref[...]), (other_in, late_ref[rest:])):
        activated, preact_grad = hidden(all_in, all_out_grad, w_in, w_out, own_slots)
        slot_out += dot(activated, w_out)
        slot_in_grad += dot(preact_grad, w_in)
    partial = dot(first, slot_out.astype(BF16), 0, 0) + dot(second, slot_in_grad.astype(BF16), 0, 0)
    partial_ref[...] = partial.astype(BF16)


def weight_grads(
    block, own_slots, gathered_ref, other_ref, w_in_ref, w_out_ref, w_in_grad_ref, w_out_grad_ref
):
    w_in, w_out = w_in_ref[...], w_out_ref[...]
    w_in_grad = jnp.zeros(w_in.shape, F32)
    w_out_grad = jnp.zeros(w_out.shape, F32)
    for rows_ref in (gathered_ref, other_ref):
        rows = rows_ref[...]
        all_in, all_out_grad = picked(rows, 0, block)[0], picked(rows, 1, block)[0]
        activated, preact_grad = hidden(all_in, all_out_grad, w_in, w_out, own_slots)
        w_in_grad += dot(preact_grad, all_in, 0, 0)
        w_out_grad += dot(activated, all_out_grad, 0, 0)
    w_in_grad_ref[...] = w_in_grad.astype(BF16)
    w_out_grad_ref[...] = w_out_grad.astype(BF16)


def on_device(tokens, cotangent, slot_params, w_in, w_out):
    imgs, share, d = tokens.shape
    peers = lax.axis_size("expert")
    own_slots = slot_params.shape[1]
    slots = peers * own_slots
    rows = own_slots * imgs

    flat_in, flat_out = jnp.swapaxes(w_in, 1, 2).reshape(-1, d), w_out.reshape(-1, d)
    early = flat_in.shape[0] * 3 // 5 // 16 * 16
    early_y = across_y(flat_in[:early])

    params = everywhere(slot_params.T, "expert").reshape(slots, d)
    both = jnp.stack([tokens.reshape(-1, d), cotangent.reshape(-1, d)])
    pairs = (peers * rows, imgs * share)
    sent, logits, combine = call(
        functools.partial(route, imgs, own_slots),
        [((peers * rows, 2 * d + 128), BF16), (pairs, F32), (pairs, F32)],
        100_000_000, params, both,
    )
    sent, early_y = lax.optimization_barrier((sent, early_y))
    taken = exchange(sent.reshape(peers, rows, 2 * d + 128), "expert")
    late = jnp.concatenate([flat_in[early:], flat_out], axis=0)
    late, head = lax.optimization_barrier((late, taken[:, :, d : d + 128]))
    late_y = across_y(late)

    peaks = join3(head[:, :, :3])
    masses = join3(head[:, :, 3:6])
    top = jnp.max(peaks, axis=0)
    scale = jnp.exp(peaks - top[None])
    total = jnp.sum(masses * scale, axis=0)
    slot_in_wide = jnp.sum(taken[:, :, :d].astype(F32) * scale, axis=0) / total
    slot_out_grad = jnp.sum(taken[:, :, d + 128 :].astype(F32), axis=0)
    own = jnp.concatenate([slot_in_wide.astype(BF16), slot_out_grad.astype(BF16)], axis=0)

    gathered, late_y = gather_z(own, late_y)
    flat = gathered.reshape(-1, d)
    (partial,) = call(
        functools.partial(experts, rows, own_slots), [(flat.shape, BF16)], 1_400_000_000,
        flat, flat_in, flat_out, early_y, late_y,
    )
    owned_b, gathered_y = reduce_z(partial.reshape(gathered.shape), 2 * rows, gathered)
    owned_b = owned_b.astype(BF16).reshape(2, rows, d)
    w_in_grad, w_out_grad = call(
        functools.partial(weight_grads, rows, own_slots), [(flat_in.shape, BF16)] * 2,
        1_400_000_000, flat, gathered_y.reshape(-1, d), flat_in, flat_out,
    )
    w_in_grad = jnp.swapaxes(w_in_grad.reshape(own_slots, -1, d), 1, 2)
    w_out_grad = w_out_grad.reshape(w_out.shape)

    col = jnp.sum(owned_b[1].astype(F32) * slot_in_wide, axis=1, keepdims=True)
    stats = jnp.concatenate(
        split3(top) + split3(total) + split3(col) + [jnp.zeros((rows, 119), BF16)], axis=1
    )
    back = everywhere(jnp.concatenate([owned_b[0], owned_b[1], stats], axis=1), "expert")
    token_grad, share_grad = call(
        functools.partial(finish, imgs, own_slots),
        [(both.shape[1:], BF16), ((slots, d), BF16)],
        100_000_000, back.reshape(peers * rows, 2 * d + 128), logits, combine, params, both,
    )
    token_grad = token_grad.reshape(tokens.shape)

    share_grad = jnp.broadcast_to(share_grad.reshape(1, peers, own_slots, d), (2, peers, own_slots, d))
    share_grad = exchange(
        share_grad.reshape(2 * peers, own_slots, d), ("dp", "expert"), plane_groups()
    )
    share_grad = jnp.sum(share_grad.astype(F32), axis=0).astype(BF16)
    share_grad = everywhere(share_grad, "dp", dp_groups(1, 2))
    share_grad = jnp.sum(share_grad.astype(F32), axis=0)
    slot_grad = share_grad.T
    return (token_grad, slot_grad, w_in_grad, w_out_grad)


def solution(mesh):
    placed = (
        P("dp", "expert", None),
        P("dp", "expert", None),
        P(None, "expert"),
        P("expert", None, "dp"),
        P("expert", "dp", None),
    )
    return jax.shard_map(
        on_device,
        mesh=mesh,
        in_specs=placed,
        out_specs=(
            P("dp", "expert", None),
            P(None, "expert"),
            P("expert", None, "dp"),
            P("expert", "dp", None),
        ),
        check_vma=False,
    )
```

```python
import functools

import jax
import jax.numpy as jnp
import numpy as np
from jax import lax
from jax.experimental import pallas as pl
from jax.experimental.pallas import tpu as pltpu
from jax.sharding import PartitionSpec as P

F32 = jnp.float32
BF16 = jnp.bfloat16


def gelu_exact(value):
    return jax.nn.gelu(value, approximate=False)


def split3(value):
    high = lax.reduce_precision(value, 8, 7)
    middle = lax.reduce_precision(value - high, 8, 7)
    low = value - high - middle
    return [high.astype(BF16), middle.astype(BF16), low.astype(BF16)]


def join3(terms):
    wide = terms.astype(F32)
    return wide[..., 0:1] + wide[..., 1:2] + wide[..., 2:3]


def groups_of(axis, sizes, inner):
    shape = [lax.axis_size(axis) // sizes[0] // sizes[1], sizes[0], sizes[1]]
    ids = np.arange(lax.axis_size(axis)).reshape(shape)
    outer = [part for part in range(3) if part not in inner]
    width = int(np.prod([shape[part] for part in inner]))
    return ids.transpose(outer + list(inner)).reshape(-1, width).tolist()


def exchange(value, axis, groups=None):
    return lax.all_to_all(
        value, axis, split_axis=0, concat_axis=0, axis_index_groups=groups, tiled=True
    )


def everywhere(value, axis, groups=None):
    peers = lax.axis_size(axis) if groups is None else len(groups[0])
    return exchange(jnp.broadcast_to(value[None], (peers,) + value.shape), axis, groups)


def dp_groups(*inner):
    return groups_of("dp", (lax.axis_size("dp") // 4, 2), inner)


def plane_groups():
    peers, depth = lax.axis_size("expert"), lax.axis_size("dp") // 2
    ids = np.arange(2 * depth * peers).reshape(2, depth, peers)
    return ids.transpose(1, 0, 2).reshape(depth, 2 * peers).tolist()


def gather_dp(own):
    whole = lax.all_gather(own, "dp", axis=0, tiled=True)
    return whole.reshape(2, -1, 2 * own.shape[0], own.shape[1])


def reduce_dp(partial, rows):
    d = partial.shape[-1]
    partial = jnp.transpose(partial.reshape(2, -1, 2, rows, d), (0, 2, 1, 3, 4)).reshape(4, -1, d)
    total = jnp.sum(exchange(partial, "dp", dp_groups(0, 2)).astype(F32), axis=0).astype(BF16)
    return jnp.sum(exchange(total.reshape(-1, rows, d), "dp", dp_groups(1)).astype(F32), axis=0)


def dot(left, right, left_dim=1, right_dim=0):
    return lax.dot_general(
        left, right, (((left_dim,), (right_dim,)), ((), ())), preferred_element_type=F32
    )


def own_image(rows, columns, imgs, own_slots, share):
    row = lax.broadcasted_iota(jnp.int32, (rows, columns), 0)
    column = lax.broadcasted_iota(jnp.int32, (rows, columns), 1)
    return (row // own_slots) % imgs == column // share


def slot_rows(rows, slots, imgs, own_slots):
    row = lax.broadcasted_iota(jnp.int32, (rows, slots), 0)
    column = lax.broadcasted_iota(jnp.int32, (rows, slots), 1)
    slot = (row // (imgs * own_slots)) * own_slots + row % own_slots
    return jnp.where(slot == column, 1.0, 0.0).astype(BF16)


def lanes_of(columns, rows):
    lane = lax.broadcasted_iota(jnp.int32, (rows, 128), 1)
    block = jnp.zeros((rows, 128), F32)
    at = 0
    for value in columns:
        high = value.astype(BF16).astype(F32)
        middle = (value - high).astype(BF16).astype(F32)
        for term in (high, middle, value - high - middle):
            block = jnp.where(lane == at, term, block)
            at += 1
    return block.astype(BF16)


def column_of(block, at):
    lane = lax.broadcasted_iota(jnp.int32, block.shape, 1)
    inside = (lane >= 3 * at) & (lane < 3 * at + 3)
    return jnp.sum(jnp.where(inside, block, 0.0), axis=1, keepdims=True)


def route(imgs, own_slots, params_ref, both_ref, sent_ref, logits_ref, combine_ref):
    tokens, cotangent = both_ref[0], both_ref[1]
    slots, d = params_ref.shape
    rows, columns = logits_ref.shape
    spread = dot(slot_rows(rows, slots, imgs, own_slots), params_ref[...]).astype(BF16)
    logits = dot(spread, tokens, 1, 1)
    mine = own_image(rows, columns, imgs, own_slots, columns // imgs)
    logits = jnp.where(mine, logits, jnp.finfo(F32).min)
    logits_ref[...] = logits
    raised = jnp.exp(logits - jnp.max(logits, axis=0, keepdims=True))
    combine = raised / jnp.sum(raised, axis=0, keepdims=True)
    combine_ref[...] = combine
    peak = jnp.max(logits, axis=1, keepdims=True)
    weight = jnp.exp(logits - peak)
    mass = jnp.sum(weight, axis=1, keepdims=True)
    sent_ref[:, :d] = dot(weight.astype(BF16), tokens).astype(BF16)
    sent_ref[:, d : d + 128] = lanes_of([peak, mass], rows)
    sent_ref[:, d + 128 :] = dot(combine.astype(BF16), cotangent).astype(BF16)


def finish(
    imgs, own_slots, back_ref, logits_ref, combine_ref, params_ref, both_ref,
    token_grad_ref, share_ref,
):
    tokens, cotangent = both_ref[0], both_ref[1]
    slots, d = params_ref.shape
    rows = logits_ref.shape[0]
    slot_out, slot_in_grad = back_ref[:, :d], back_ref[:, d : 2 * d]
    stats = back_ref[:, 2 * d :].astype(F32)
    top, total, col = [column_of(stats, at) for at in range(3)]
    combine = combine_ref[...]
    dispatch = jnp.exp(logits_ref[...] - top) / total
    combine_grad = dot(slot_out, cotangent, 1, 1)
    dispatch_grad = dot(slot_in_grad, tokens, 1, 1)
    row_sums = jnp.sum(combine * combine_grad, axis=0, keepdims=True)
    logit_grad = dispatch * (dispatch_grad - col) + combine * (combine_grad - row_sums)
    members = slot_rows(rows, slots, imgs, own_slots)
    by_slot = dot(members, logit_grad.astype(BF16), 0, 0).astype(BF16)
    share_ref[...] = dot(by_slot, tokens).astype(BF16)
    token_grad = dot(dispatch.astype(BF16), slot_in_grad, 0, 0)
    token_grad = token_grad + dot(by_slot, params_ref[...], 0, 0)
    token_grad_ref[...] = token_grad.astype(BF16)


def call(kernel, out_shape, *operands):
    shapes = [jax.ShapeDtypeStruct(shape, dtype) for shape, dtype in out_shape]
    return pl.pallas_call(
        kernel,
        out_shape=shapes,
        compiler_params=pltpu.CompilerParams(vmem_limit_bytes=32 * 1024 * 1024),
        cost_estimate=pl.CostEstimate(flops=120_000_000, bytes_accessed=2_000_000, transcendentals=16384),
    )(*operands)


def expert_part(gathered, w_in, w_out, imgs):
    slots, d, _ = w_in.shape
    rows = slots * imgs
    blocks = (gathered.shape[0], 2 * gathered.shape[1], rows, d)
    halves = gathered.reshape(blocks[:2] + (2 * rows, d))
    all_in = halves[:, :, :rows].reshape(-1, d)
    all_out_grad = halves[:, :, rows:].reshape(-1, d)
    row = lax.broadcasted_iota(jnp.int32, (slots, all_in.shape[0], 1), 1)
    slot = lax.broadcasted_iota(jnp.int32, (slots, all_in.shape[0], 1), 0)
    mine = row % slots == slot
    preact = jnp.einsum("rd,sdh->srh", all_in, w_in, preferred_element_type=F32)
    activated_wide, pullback = jax.vjp(gelu_exact, preact)
    activated = jnp.where(mine, activated_wide, 0.0).astype(BF16)
    slot_out = jnp.einsum("srh,shd->rd", activated, w_out, preferred_element_type=F32)
    act_grad = jnp.einsum("rd,shd->srh", all_out_grad, w_out, preferred_element_type=F32)
    preact_grad = jnp.where(mine, pullback(act_grad)[0], 0.0).astype(BF16)
    slot_in_grad = jnp.einsum("srh,sdh->rd", preact_grad, w_in, preferred_element_type=F32)
    w_out_grad = jnp.einsum(
        "srh,rd->shd", activated, all_out_grad, preferred_element_type=F32
    ).astype(BF16)
    w_in_grad = jnp.einsum(
        "rd,srh->sdh", all_in, preact_grad, preferred_element_type=F32
    ).astype(BF16)
    pair = [value.astype(BF16).reshape(blocks) for value in (slot_out, slot_in_grad)]
    partial = jnp.concatenate(pair, axis=2).reshape(gathered.shape)
    return partial, w_in_grad, w_out_grad


def on_device(tokens, cotangent, slot_params, w_in, w_out):
    imgs, share, d = tokens.shape
    peers = lax.axis_size("expert")
    own_slots = slot_params.shape[1]
    slots = peers * own_slots
    rows = own_slots * imgs

    params = everywhere(slot_params.T, "expert").reshape(slots, d)
    both = jnp.stack([tokens.reshape(-1, d), cotangent.reshape(-1, d)])
    pairs = (peers * rows, imgs * share)
    sent, logits, combine = call(
        functools.partial(route, imgs, own_slots),
        [((peers * rows, 2 * d + 128), BF16), (pairs, F32), (pairs, F32)],
        params, both,
    )
    taken = exchange(sent.reshape(peers, rows, 2 * d + 128), "expert")

    peaks = join3(taken[:, :, d : d + 3])
    masses = join3(taken[:, :, d + 3 : d + 6])
    top = jnp.max(peaks, axis=0)
    scale = jnp.exp(peaks - top[None])
    total = jnp.sum(masses * scale, axis=0)
    slot_in_wide = jnp.sum(taken[:, :, :d].astype(F32) * scale, axis=0) / total
    slot_out_grad = jnp.sum(taken[:, :, d + 128 :].astype(F32), axis=0)
    own = jnp.concatenate([slot_in_wide.astype(BF16), slot_out_grad.astype(BF16)], axis=0)

    gathered = gather_dp(own)
    partial, w_in_grad, w_out_grad = expert_part(gathered, w_in, w_out, imgs)
    owned_b = reduce_dp(partial, 2 * rows).astype(BF16).reshape(2, rows, d)

    col = jnp.sum(owned_b[1].astype(F32) * slot_in_wide, axis=1, keepdims=True)
    stats = jnp.concatenate(
        split3(top) + split3(total) + split3(col) + [jnp.zeros((rows, 119), BF16)], axis=1
    )
    back = everywhere(jnp.concatenate([owned_b[0], owned_b[1], stats], axis=1), "expert")
    token_grad, share_grad = call(
        functools.partial(finish, imgs, own_slots),
        [(both.shape[1:], BF16), ((slots, d), BF16)],
        back.reshape(peers * rows, 2 * d + 128), logits, combine, params, both,
    )
    token_grad = token_grad.reshape(tokens.shape)

    share_grad = jnp.broadcast_to(share_grad.reshape(1, peers, own_slots, d), (2, peers, own_slots, d))
    share_grad = exchange(
        share_grad.reshape(2 * peers, own_slots, d), ("dp", "expert"), plane_groups()
    )
    share_grad = jnp.sum(share_grad.astype(F32), axis=0).astype(BF16)
    share_grad = everywhere(share_grad, "dp", dp_groups(1, 2))
    share_grad = jnp.sum(share_grad.astype(F32), axis=0)
    slot_grad = share_grad.T
    return (token_grad, slot_grad, w_in_grad, w_out_grad)


def solution(mesh):
    placed = (
        P("dp", "expert", None),
        P("dp", "expert", None),
        P(None, "expert"),
        P("expert", None, "dp"),
        P("expert", "dp", None),
    )
    return jax.shard_map(
        on_device,
        mesh=mesh,
        in_specs=placed,
        out_specs=(
            P("dp", "expert", None),
            P(None, "expert"),
            P("expert", None, "dp"),
            P("expert", "dp", None),
        ),
        check_vma=False,
    )
```

```python
import functools

import jax
import jax.numpy as jnp
import numpy as np
from jax import lax
from jax.experimental import pallas as pl
from jax.experimental.pallas import tpu as pltpu
from jax.sharding import PartitionSpec as P

F32 = jnp.float32
BF16 = jnp.bfloat16


def gelu_and_slope(value):
    below = 0.5 * (1.0 + lax.erf(value * 0.5**0.5))
    density = jnp.exp(-0.5 * value * value) * (1.0 / (2.0 * np.pi) ** 0.5)
    return value * below, below + value * density


def split3(value):
    high = lax.reduce_precision(value, 8, 7)
    middle = lax.reduce_precision(value - high, 8, 7)
    low = value - high - middle
    return [high.astype(BF16), middle.astype(BF16), low.astype(BF16)]


def join3(terms):
    wide = terms.astype(F32)
    return wide[..., 0:1] + wide[..., 1:2] + wide[..., 2:3]


def groups_of(axis, sizes, inner):
    shape = [lax.axis_size(axis) // sizes[0] // sizes[1], sizes[0], sizes[1]]
    ids = np.arange(lax.axis_size(axis)).reshape(shape)
    outer = [part for part in range(3) if part not in inner]
    width = int(np.prod([shape[part] for part in inner]))
    return ids.transpose(outer + list(inner)).reshape(-1, width).tolist()


def exchange(value, axis, groups=None):
    return lax.all_to_all(
        value, axis, split_axis=0, concat_axis=0, axis_index_groups=groups, tiled=True
    )


def everywhere(value, axis, groups=None):
    peers = lax.axis_size(axis) if groups is None else len(groups[0])
    return exchange(jnp.broadcast_to(value[None], (peers,) + value.shape), axis, groups)


def dp_groups(*inner):
    return groups_of("dp", (lax.axis_size("dp") // 4, 2), inner)


def plane_groups():
    peers, depth = lax.axis_size("expert"), lax.axis_size("dp") // 2
    ids = np.arange(2 * depth * peers).reshape(2, depth, peers)
    return ids.transpose(1, 0, 2).reshape(depth, 2 * peers).tolist()


def gather_dp(own):
    rows, d = own.shape[1:]
    far = everywhere(own.reshape(2 * rows, d), "dp", dp_groups(1)).reshape(-1, 2, rows, d)
    far = jnp.transpose(far, (1, 0, 2, 3)).reshape(2, -1, d)
    return everywhere(far, "dp", dp_groups(0, 2))


def reduce_dp(partial, rows):
    d = partial.shape[-1]
    taken = exchange(partial, "dp", dp_groups(0, 2))
    (total,) = call(
        functools.partial(add_square, rows), [((2 * partial.shape[2], d), BF16)], 2_000_000, taken
    )
    total = exchange(total.reshape(-1, 2 * rows, d), "dp", dp_groups(1))
    return jnp.sum(total.astype(F32), axis=0)


def dot(left, right, left_dim=1, right_dim=0):
    return lax.dot_general(
        left, right, (((left_dim,), (right_dim,)), ((), ())), preferred_element_type=F32
    )


def own_image(rows, columns, imgs, own_slots, share):
    row = lax.broadcasted_iota(jnp.int32, (rows, columns), 0)
    column = lax.broadcasted_iota(jnp.int32, (rows, columns), 1)
    return (row // own_slots) % imgs == column // share


def slot_rows(rows, slots, imgs, own_slots):
    row = lax.broadcasted_iota(jnp.int32, (rows, slots), 0)
    column = lax.broadcasted_iota(jnp.int32, (rows, slots), 1)
    slot = (row // (imgs * own_slots)) * own_slots + row % own_slots
    return jnp.where(slot == column, 1.0, 0.0).astype(BF16)


def lanes_of(columns, rows):
    lane = lax.broadcasted_iota(jnp.int32, (rows, 128), 1)
    block = jnp.zeros((rows, 128), F32)
    at = 0
    for value in columns:
        high = value.astype(BF16).astype(F32)
        middle = (value - high).astype(BF16).astype(F32)
        for term in (high, middle, value - high - middle):
            block = jnp.where(lane == at, term, block)
            at += 1
    return block.astype(BF16)


def column_of(block, at):
    lane = lax.broadcasted_iota(jnp.int32, block.shape, 1)
    inside = (lane >= 3 * at) & (lane < 3 * at + 3)
    return jnp.sum(jnp.where(inside, block, 0.0), axis=1, keepdims=True)


def route(imgs, own_slots, params_ref, both_ref, sent_ref, logits_ref, combine_ref):
    tokens, cotangent = both_ref[0], both_ref[1]
    slots, d = params_ref.shape
    rows, columns = logits_ref.shape
    spread = dot(slot_rows(rows, slots, imgs, own_slots), params_ref[...]).astype(BF16)
    logits = dot(spread, tokens, 1, 1)
    mine = own_image(rows, columns, imgs, own_slots, columns // imgs)
    logits = jnp.where(mine, logits, jnp.finfo(F32).min)
    logits_ref[...] = logits
    raised = jnp.exp(logits - jnp.max(logits, axis=0, keepdims=True))
    combine = raised / jnp.sum(raised, axis=0, keepdims=True)
    combine_ref[...] = combine
    peak = jnp.max(logits, axis=1, keepdims=True)
    weight = jnp.exp(logits - peak)
    mass = jnp.sum(weight, axis=1, keepdims=True)
    sent_ref[:, :d] = dot(weight.astype(BF16), tokens).astype(BF16)
    sent_ref[:, d : d + 128] = lanes_of([peak, mass], rows)
    sent_ref[:, d + 128 :] = dot(combine.astype(BF16), cotangent).astype(BF16)


def finish(
    imgs, own_slots, back_ref, logits_ref, combine_ref, params_ref, both_ref,
    token_grad_ref, share_ref,
):
    tokens, cotangent = both_ref[0], both_ref[1]
    slots, d = params_ref.shape
    rows = logits_ref.shape[0]
    slot_out, slot_in_grad = back_ref[:, :d], back_ref[:, d : 2 * d]
    stats = back_ref[:, 2 * d :].astype(F32)
    top, total, col = [column_of(stats, at) for at in range(3)]
    combine = combine_ref[...]
    dispatch = jnp.exp(logits_ref[...] - top) / total
    combine_grad = dot(slot_out, cotangent, 1, 1)
    dispatch_grad = dot(slot_in_grad, tokens, 1, 1)
    row_sums = jnp.sum(combine * combine_grad, axis=0, keepdims=True)
    logit_grad = dispatch * (dispatch_grad - col) + combine * (combine_grad - row_sums)
    members = slot_rows(rows, slots, imgs, own_slots)
    by_slot = dot(members, logit_grad.astype(BF16), 0, 0).astype(BF16)
    share_ref[...] = dot(by_slot, tokens).astype(BF16)
    token_grad = dot(dispatch.astype(BF16), slot_in_grad, 0, 0)
    token_grad = token_grad + dot(by_slot, params_ref[...], 0, 0)
    token_grad_ref[...] = token_grad.astype(BF16)


def call(kernel, out_shape, flops, *operands):
    shapes = [jax.ShapeDtypeStruct(shape, dtype) for shape, dtype in out_shape]
    size = sum(value.size * value.dtype.itemsize for value in list(operands) + shapes)
    return pl.pallas_call(
        kernel,
        out_shape=shapes,
        compiler_params=pltpu.CompilerParams(vmem_limit_bytes=32 * 1024 * 1024),
        cost_estimate=pl.CostEstimate(flops=flops, bytes_accessed=size, transcendentals=16384),
    )(*operands)


def hidden(all_in, all_out_grad, w_in, w_out, own_slots):
    shape = (all_in.shape[0], w_in.shape[0])
    row = lax.broadcasted_iota(jnp.int32, shape, 0)
    column = lax.broadcasted_iota(jnp.int32, shape, 1)
    mine = row % own_slots == column // (shape[1] // own_slots)
    activated, slope = gelu_and_slope(dot(all_in, w_in, 1, 1))
    preact_grad = dot(all_out_grad, w_out, 1, 1) * slope
    return (
        jnp.where(mine, activated, 0.0).astype(BF16),
        jnp.where(mine, preact_grad, 0.0).astype(BF16),
    )


def rows_of(gathered_ref, which):
    return jnp.concatenate([gathered_ref[q, which] for q in range(gathered_ref.shape[0])], axis=0)


def experts(
    own_slots, gathered_ref, w_in_ref, w_out_ref, partial_ref, activated_ref, preact_grad_ref
):
    w_in, w_out = w_in_ref[...], w_out_ref[...]
    activated, preact_grad = hidden(
        rows_of(gathered_ref, 0), rows_of(gathered_ref, 1), w_in, w_out, own_slots
    )
    activated_ref[...] = activated
    preact_grad_ref[...] = preact_grad
    slot_out = dot(activated, w_out).astype(BF16)
    slot_in_grad = dot(preact_grad, w_in).astype(BF16)
    size = partial_ref.shape[2]
    for q in range(partial_ref.shape[0]):
        partial_ref[q, 0] = slot_out[q * size : (q + 1) * size]
        partial_ref[q, 1] = slot_in_grad[q * size : (q + 1) * size]


def weight_grads(gathered_ref, activated_ref, preact_grad_ref, w_in_grad_ref, w_out_grad_ref):
    all_in, all_out_grad = rows_of(gathered_ref, 0), rows_of(gathered_ref, 1)
    w_in_grad_ref[...] = dot(preact_grad_ref[...], all_in, 0, 0).astype(BF16)
    w_out_grad_ref[...] = dot(activated_ref[...], all_out_grad, 0, 0).astype(BF16)


def add_square(rows, taken_ref, total_ref):
    total = taken_ref[0].astype(F32)
    for q in range(1, taken_ref.shape[0]):
        total += taken_ref[q].astype(F32)
    pieces = [
        total[which, at : at + rows] for at in range(0, total.shape[1], rows) for which in range(2)
    ]
    total_ref[...] = jnp.concatenate(pieces, axis=0).astype(BF16)


def on_device(tokens, cotangent, slot_params, w_in, w_out):
    imgs, share, d = tokens.shape
    peers = lax.axis_size("expert")
    own_slots = slot_params.shape[1]
    slots = peers * own_slots
    rows = own_slots * imgs

    params = everywhere(slot_params.T, "expert").reshape(slots, d)
    both = jnp.stack([tokens.reshape(-1, d), cotangent.reshape(-1, d)])
    pairs = (peers * rows, imgs * share)
    sent, logits, combine = call(
        functools.partial(route, imgs, own_slots),
        [((peers * rows, 2 * d + 128), BF16), (pairs, F32), (pairs, F32)],
        100_000_000, params, both,
    )
    taken = exchange(sent.reshape(peers, rows, 2 * d + 128), "expert")

    peaks = join3(taken[:, :, d : d + 3])
    masses = join3(taken[:, :, d + 3 : d + 6])
    top = jnp.max(peaks, axis=0)
    scale = jnp.exp(peaks - top[None])
    total = jnp.sum(masses * scale, axis=0)
    slot_in_wide = jnp.sum(taken[:, :, :d].astype(F32) * scale, axis=0) / total
    slot_out_grad = jnp.sum(taken[:, :, d + 128 :].astype(F32), axis=0)
    own = jnp.stack([slot_in_wide.astype(BF16), slot_out_grad.astype(BF16)])

    gathered = gather_dp(own)
    flat_in, flat_out = jnp.swapaxes(w_in, 1, 2).reshape(-1, d), w_out.reshape(-1, d)
    units = (gathered.shape[0] * gathered.shape[2], flat_in.shape[0])
    partial, activated, preact_grad = call(
        functools.partial(experts, own_slots),
        [(gathered.shape, BF16), (units, BF16), (units, BF16)],
        1_000_000_000, gathered, flat_in, flat_out,
    )
    w_in_grad, w_out_grad = call(
        weight_grads, [(flat_in.shape, BF16)] * 2, 600_000_000, gathered, activated, preact_grad
    )
    w_in_grad = jnp.swapaxes(w_in_grad.reshape(own_slots, -1, d), 1, 2)
    w_out_grad = w_out_grad.reshape(w_out.shape)
    owned_b = reduce_dp(partial, rows).astype(BF16).reshape(2, rows, d)

    col = jnp.sum(owned_b[1].astype(F32) * slot_in_wide, axis=1, keepdims=True)
    stats = jnp.concatenate(
        split3(top) + split3(total) + split3(col) + [jnp.zeros((rows, 119), BF16)], axis=1
    )
    back = everywhere(jnp.concatenate([owned_b[0], owned_b[1], stats], axis=1), "expert")
    token_grad, share_grad = call(
        functools.partial(finish, imgs, own_slots),
        [(both.shape[1:], BF16), ((slots, d), BF16)],
        100_000_000, back.reshape(peers * rows, 2 * d + 128), logits, combine, params, both,
    )
    token_grad = token_grad.reshape(tokens.shape)

    share_grad = jnp.broadcast_to(share_grad.reshape(1, peers, own_slots, d), (2, peers, own_slots, d))
    share_grad = exchange(
        share_grad.reshape(2 * peers, own_slots, d), ("dp", "expert"), plane_groups()
    )
    share_grad = jnp.sum(share_grad.astype(F32), axis=0).astype(BF16)
    share_grad = everywhere(share_grad, "dp", dp_groups(1, 2))
    share_grad = jnp.sum(share_grad.astype(F32), axis=0)
    slot_grad = share_grad.T
    return (token_grad, slot_grad, w_in_grad, w_out_grad)


def solution(mesh):
    placed = (
        P("dp", "expert", None),
        P("dp", "expert", None),
        P(None, "expert"),
        P("expert", None, "dp"),
        P("expert", "dp", None),
    )
    return jax.shard_map(
        on_device,
        mesh=mesh,
        in_specs=placed,
        out_specs=(
            P("dp", "expert", None),
            P(None, "expert"),
            P("expert", None, "dp"),
            P("expert", "dp", None),
        ),
        check_vma=False,
    )
```

```python
import functools

import jax
import jax.numpy as jnp
import numpy as np
from jax import lax
from jax.experimental import pallas as pl
from jax.experimental.pallas import tpu as pltpu
from jax.sharding import PartitionSpec as P

F32 = jnp.float32
BF16 = jnp.bfloat16


def gelu_and_slope(value):
    below = 0.5 * (1.0 + lax.erf(value * 0.5**0.5))
    density = jnp.exp(-0.5 * value * value) * (1.0 / (2.0 * np.pi) ** 0.5)
    return value * below, below + value * density


def groups_of(axis, sizes, inner):
    shape = [lax.axis_size(axis) // sizes[0] // sizes[1], sizes[0], sizes[1]]
    ids = np.arange(lax.axis_size(axis)).reshape(shape)
    outer = [part for part in range(3) if part not in inner]
    width = int(np.prod([shape[part] for part in inner]))
    return ids.transpose(outer + list(inner)).reshape(-1, width).tolist()


def exchange(value, axis, groups=None):
    return lax.all_to_all(
        value, axis, split_axis=0, concat_axis=0, axis_index_groups=groups, tiled=True
    )


def everywhere(value, axis, groups=None):
    peers = lax.axis_size(axis) if groups is None else len(groups[0])
    return exchange(jnp.broadcast_to(value[None], (peers,) + value.shape), axis, groups)


def dp_groups(*inner):
    return groups_of("dp", (lax.axis_size("dp") // 4, 2), inner)


def plane_groups():
    peers, depth = lax.axis_size("expert"), lax.axis_size("dp") // 2
    ids = np.arange(2 * depth * peers).reshape(2, depth, peers)
    return ids.transpose(1, 0, 2).reshape(depth, 2 * peers).tolist()


def gather_dp(own):
    rows, d = own.shape[0] // 2, own.shape[1]
    far = everywhere(own, "dp", dp_groups(1)).reshape(-1, 2, rows, d)
    far = jnp.transpose(far, (1, 0, 2, 3)).reshape(2, -1, d)
    return everywhere(far, "dp", dp_groups(0, 2))


def reduce_dp(partial, rows):
    d = partial.shape[-1]
    taken = exchange(partial, "dp", dp_groups(0, 2))
    (total,) = call(
        functools.partial(add_square, rows), [((2 * partial.shape[2], d), BF16)], 2_000_000, taken
    )
    return exchange(total.reshape(-1, 2 * rows, d), "dp", dp_groups(1))


def dot(left, right, left_dim=1, right_dim=0):
    return lax.dot_general(
        left, right, (((left_dim,), (right_dim,)), ((), ())), preferred_element_type=F32
    )


def own_image(rows, columns, imgs, own_slots, share):
    row = lax.broadcasted_iota(jnp.int32, (rows, columns), 0)
    column = lax.broadcasted_iota(jnp.int32, (rows, columns), 1)
    return (row // own_slots) % imgs == column // share


def slot_rows(rows, slots, imgs, own_slots):
    row = lax.broadcasted_iota(jnp.int32, (rows, slots), 0)
    column = lax.broadcasted_iota(jnp.int32, (rows, slots), 1)
    slot = (row // (imgs * own_slots)) * own_slots + row % own_slots
    return jnp.where(slot == column, 1.0, 0.0).astype(BF16)


def lanes_of(columns, rows):
    lane = lax.broadcasted_iota(jnp.int32, (rows, 128), 1)
    block = jnp.zeros((rows, 128), F32)
    at = 0
    for value in columns:
        high = value.astype(BF16).astype(F32)
        middle = (value - high).astype(BF16).astype(F32)
        for term in (high, middle, value - high - middle):
            block = jnp.where(lane == at, term, block)
            at += 1
    return block


def column_of(block, at):
    lane = lax.broadcasted_iota(jnp.int32, block.shape, 1)
    inside = (lane >= 3 * at) & (lane < 3 * at + 3)
    return jnp.sum(jnp.where(inside, block, 0.0), axis=1, keepdims=True)


def route(
    imgs, own_slots, params_ref, tok_ref, cot_ref, sent_ref, logits_ref, combine_ref, both_ref, sem
):
    copies = [
        pltpu.make_async_copy(source, both_ref.at[at], sem.at[at])
        for at, source in enumerate((tok_ref, cot_ref))
    ]
    for copy in copies:
        copy.start()
    slots, d = params_ref.shape
    rows, columns = logits_ref.shape
    spread = dot(slot_rows(rows, slots, imgs, own_slots), params_ref[...]).astype(BF16)
    for copy in copies:
        copy.wait()
    tokens, cotangent = both_ref[0], both_ref[1]
    logits = dot(spread, tokens, 1, 1)
    mine = own_image(rows, columns, imgs, own_slots, columns // imgs)
    logits = jnp.where(mine, logits, jnp.finfo(F32).min)
    logits_ref[...] = logits
    raised = jnp.exp(logits - jnp.max(logits, axis=0, keepdims=True))
    combine = raised / jnp.sum(raised, axis=0, keepdims=True)
    combine_ref[...] = combine
    peak = jnp.max(logits, axis=1, keepdims=True)
    weight = jnp.exp(logits - peak)
    mass = jnp.sum(weight, axis=1, keepdims=True)
    sent_ref[:, :d] = dot(weight.astype(BF16), tokens).astype(BF16)
    sent_ref[:, d : d + 128] = lanes_of([peak, mass], rows).astype(BF16)
    sent_ref[:, d + 128 :] = dot(combine.astype(BF16), cotangent).astype(BF16)


def collect(peers, taken_ref, own_ref, wide_ref, scalars_ref):
    rows, d = wide_ref.shape
    stats = taken_ref[:, d : d + 128].astype(F32)
    peaks = column_of(stats, 0).reshape(peers, rows, 1)
    masses = column_of(stats, 1).reshape(peers, rows, 1)
    top = jnp.max(peaks, axis=0)
    scale = jnp.exp(peaks - top[None])
    total = jnp.sum(masses * scale, axis=0)
    part_in = taken_ref[:, :d].astype(F32).reshape(peers, rows, d)
    slot_in = jnp.sum(part_in * scale, axis=0) / total
    slot_out_grad = jnp.sum(taken_ref[:, d + 128 :].astype(F32).reshape(peers, rows, d), axis=0)
    own_ref[...] = jnp.concatenate([slot_in, slot_out_grad], axis=0).astype(BF16)
    wide_ref[...] = slot_in
    lane = lax.broadcasted_iota(jnp.int32, scalars_ref.shape, 1)
    scalars_ref[...] = jnp.where(lane == 0, top, total)


def deliver(far, peers, taken_ref, wide_ref, scalars_ref, back_ref):
    rows, d = wide_ref.shape
    owned = jnp.sum(taken_ref[...].astype(F32).reshape(far, 2 * rows, d), axis=0)
    owned = owned.astype(BF16).astype(F32)
    slot_out, slot_in_grad = owned[:rows], owned[rows:]
    col = jnp.sum(slot_in_grad * wide_ref[...], axis=1, keepdims=True)
    top, total = scalars_ref[:, 0:1], scalars_ref[:, 1:2]
    stats = lanes_of([top, total, col], rows)
    for at, value in ((0, slot_out), (d, slot_in_grad), (2 * d, stats)):
        copies = jnp.concatenate([value] * peers, axis=0).astype(BF16)
        back_ref[:, at : at + value.shape[1]] = copies


def finish(
    imgs, own_slots, back_ref, logits_ref, combine_ref, params_ref, both_ref,
    token_grad_ref, share_ref,
):
    tokens, cotangent = both_ref[0], both_ref[1]
    slots, d = params_ref.shape
    rows = logits_ref.shape[0]
    slot_out, slot_in_grad = back_ref[:, :d], back_ref[:, d : 2 * d]
    stats = back_ref[:, 2 * d :].astype(F32)
    top, total, col = [column_of(stats, at) for at in range(3)]
    combine = combine_ref[...]
    dispatch = jnp.exp(logits_ref[...] - top) / total
    combine_grad = dot(slot_out, cotangent, 1, 1)
    dispatch_grad = dot(slot_in_grad, tokens, 1, 1)
    row_sums = jnp.sum(combine * combine_grad, axis=0, keepdims=True)
    logit_grad = dispatch * (dispatch_grad - col) + combine * (combine_grad - row_sums)
    members = slot_rows(rows, slots, imgs, own_slots)
    by_slot = dot(members, logit_grad.astype(BF16), 0, 0).astype(BF16)
    share_ref[...] = dot(by_slot, tokens).astype(BF16)
    token_grad = dot(dispatch.astype(BF16), slot_in_grad, 0, 0)
    token_grad = token_grad + dot(by_slot, params_ref[...], 0, 0)
    token_grad_ref[...] = token_grad.astype(BF16)


def call(kernel, out_shape, flops, *operands, **options):
    shapes = [jax.ShapeDtypeStruct(shape, dtype) for shape, dtype in out_shape]
    size = sum(value.size * value.dtype.itemsize for value in list(operands) + shapes)
    return pl.pallas_call(
        kernel,
        out_shape=shapes,
        compiler_params=pltpu.CompilerParams(vmem_limit_bytes=32 * 1024 * 1024),
        cost_estimate=pl.CostEstimate(flops=flops, bytes_accessed=size, transcendentals=16384),
        **options,
    )(*operands)


def hidden(all_in, all_out_grad, w_in, w_out, own_slots):
    shape = (all_in.shape[0], w_in.shape[0])
    row = lax.broadcasted_iota(jnp.int32, shape, 0)
    column = lax.broadcasted_iota(jnp.int32, shape, 1)
    mine = row % own_slots == column // (shape[1] // own_slots)
    activated, slope = gelu_and_slope(dot(all_in, w_in, 1, 1))
    preact_grad = dot(all_out_grad, w_out, 1, 1) * slope
    return (
        jnp.where(mine, activated, 0.0).astype(BF16),
        jnp.where(mine, preact_grad, 0.0).astype(BF16),
    )


def rows_of(gathered_ref, which):
    return jnp.concatenate([gathered_ref[q, which] for q in range(gathered_ref.shape[0])], axis=0)


def experts(
    own_slots, gathered_ref, w_in_ref, w_out_ref, partial_ref, activated_ref, preact_grad_ref
):
    w_in, w_out = w_in_ref[...], w_out_ref[...]
    activated, preact_grad = hidden(
        rows_of(gathered_ref, 0), rows_of(gathered_ref, 1), w_in, w_out, own_slots
    )
    activated_ref[...] = activated
    preact_grad_ref[...] = preact_grad
    slot_out = dot(activated, w_out).astype(BF16)
    slot_in_grad = dot(preact_grad, w_in).astype(BF16)
    size = partial_ref.shape[2]
    for q in range(partial_ref.shape[0]):
        partial_ref[q, 0] = slot_out[q * size : (q + 1) * size]
        partial_ref[q, 1] = slot_in_grad[q * size : (q + 1) * size]


def weight_grads(gathered_ref, activated_ref, preact_grad_ref, w_in_grad_ref, w_out_grad_ref):
    all_in, all_out_grad = rows_of(gathered_ref, 0), rows_of(gathered_ref, 1)
    w_in_grad_ref[...] = dot(preact_grad_ref[...], all_in, 0, 0).astype(BF16)
    w_out_grad_ref[...] = dot(activated_ref[...], all_out_grad, 0, 0).astype(BF16)


def add_square(rows, taken_ref, total_ref):
    total = taken_ref[0].astype(F32)
    for q in range(1, taken_ref.shape[0]):
        total += taken_ref[q].astype(F32)
    pieces = [
        total[which, at : at + rows] for at in range(0, total.shape[1], rows) for which in range(2)
    ]
    total_ref[...] = jnp.concatenate(pieces, axis=0).astype(BF16)


def on_device(tokens, cotangent, slot_params, w_in, w_out):
    imgs, share, d = tokens.shape
    peers = lax.axis_size("expert")
    own_slots = slot_params.shape[1]
    slots = peers * own_slots
    rows = own_slots * imgs

    params = everywhere(slot_params.T, "expert").reshape(slots, d)
    pairs = (peers * rows, imgs * share)
    wide = 2 * d + 128
    flat = (imgs * share, d)
    sent, logits, combine, both = call(
        functools.partial(route, imgs, own_slots),
        [((peers * rows, wide), BF16), (pairs, F32), (pairs, F32), ((2,) + flat, BF16)],
        100_000_000, params, tokens.reshape(flat), cotangent.reshape(flat),
        in_specs=[pl.BlockSpec(memory_space=space) for space in (pltpu.VMEM, pltpu.HBM, pltpu.HBM)],
        scratch_shapes=[pltpu.SemaphoreType.DMA((2,))],
    )
    taken = exchange(sent.reshape(peers, rows, wide), "expert")
    own, slot_in_wide, scalars = call(
        functools.partial(collect, peers),
        [((2 * rows, d), BF16), ((rows, d), F32), ((rows, 128), F32)],
        1_000_000, taken.reshape(peers * rows, wide),
    )

    gathered = gather_dp(own)
    flat_in, flat_out = jnp.swapaxes(w_in, 1, 2).reshape(-1, d), w_out.reshape(-1, d)
    units = (gathered.shape[0] * gathered.shape[2], flat_in.shape[0])
    partial, activated, preact_grad = call(
        functools.partial(experts, own_slots),
        [(gathered.shape, BF16), (units, BF16), (units, BF16)],
        1_000_000_000, gathered, flat_in, flat_out,
    )
    w_in_grad, w_out_grad = call(
        weight_grads, [(flat_in.shape, BF16)] * 2, 600_000_000, gathered, activated, preact_grad
    )
    w_in_grad = jnp.swapaxes(w_in_grad.reshape(own_slots, -1, d), 1, 2)
    w_out_grad = w_out_grad.reshape(w_out.shape)
    terms = reduce_dp(partial, rows)
    (back,) = call(
        functools.partial(deliver, terms.shape[0], peers), [((peers * rows, wide), BF16)],
        1_000_000, terms.reshape(-1, d), slot_in_wide, scalars,
    )
    back = exchange(back.reshape(peers, rows, wide), "expert")

    token_grad, share_grad = call(
        functools.partial(finish, imgs, own_slots),
        [(both.shape[1:], BF16), ((slots, d), BF16)],
        100_000_000, back.reshape(peers * rows, wide), logits, combine, params, both,
    )
    token_grad = token_grad.reshape(tokens.shape)

    share_grad = jnp.broadcast_to(share_grad.reshape(1, peers, own_slots, d), (2, peers, own_slots, d))
    share_grad = exchange(
        share_grad.reshape(2 * peers, own_slots, d), ("dp", "expert"), plane_groups()
    )
    share_grad = jnp.sum(share_grad.astype(F32), axis=0).astype(BF16)
    share_grad = everywhere(share_grad, "dp", dp_groups(1, 2))
    share_grad = jnp.sum(share_grad.astype(F32), axis=0)
    slot_grad = share_grad.T
    return (token_grad, slot_grad, w_in_grad, w_out_grad)


def solution(mesh):
    placed = (
        P("dp", "expert", None),
        P("dp", "expert", None),
        P(None, "expert"),
        P("expert", None, "dp"),
        P("expert", "dp", None),
    )
    return jax.shard_map(
        on_device,
        mesh=mesh,
        in_specs=placed,
        out_specs=(
            P("dp", "expert", None),
            P(None, "expert"),
            P("expert", None, "dp"),
            P("expert", "dp", None),
        ),
        check_vma=False,
    )
```

```python
import functools

import jax
import jax.numpy as jnp
import numpy as np
from jax import lax
from jax.experimental import pallas as pl
from jax.experimental.pallas import tpu as pltpu
from jax.sharding import PartitionSpec as P

F32 = jnp.float32
BF16 = jnp.bfloat16


def gelu_and_slope(value):
    below = 0.5 * (1.0 + lax.erf(value * 0.5**0.5))
    density = jnp.exp(-0.5 * value * value) * (1.0 / (2.0 * np.pi) ** 0.5)
    return value * below, below + value * density


def groups_of(axis, sizes, inner):
    shape = [lax.axis_size(axis) // sizes[0] // sizes[1], sizes[0], sizes[1]]
    ids = np.arange(lax.axis_size(axis)).reshape(shape)
    outer = [part for part in range(3) if part not in inner]
    width = int(np.prod([shape[part] for part in inner]))
    return ids.transpose(outer + list(inner)).reshape(-1, width).tolist()


def exchange(value, axis, groups=None):
    return lax.all_to_all(
        value, axis, split_axis=0, concat_axis=0, axis_index_groups=groups, tiled=True
    )


def everywhere(value, axis, groups=None):
    peers = lax.axis_size(axis) if groups is None else len(groups[0])
    return exchange(jnp.broadcast_to(value[None], (peers,) + value.shape), axis, groups)


def dp_groups(*inner):
    return groups_of("dp", (lax.axis_size("dp") // 4, 2), inner)


def expert_groups(*inner):
    return groups_of("expert", (2, 2), inner)


def plane_groups():
    peers, depth = lax.axis_size("expert"), lax.axis_size("dp") // 2
    ids = np.arange(2 * depth * peers).reshape(2, depth, peers)
    return ids.transpose(1, 0, 2).reshape(depth, 2 * peers).tolist()


def gather_dp(own):
    rows, d = own.shape[0] // 2, own.shape[1]
    far = everywhere(own, "dp", dp_groups(1)).reshape(-1, 2, rows, d)
    far = jnp.transpose(far, (1, 0, 2, 3)).reshape(2, -1, d)
    return everywhere(far, "dp", dp_groups(0, 2))


def reduce_dp(partial, rows):
    d = partial.shape[-1]
    taken = exchange(partial, "dp", dp_groups(0, 2))
    (total,) = call(
        functools.partial(add_square, rows), [((2 * partial.shape[2], d), BF16)], 2_000_000, taken
    )
    return exchange(total.reshape(-1, 2 * rows, d), "dp", dp_groups(1))


def dot(left, right, left_dim=1, right_dim=0):
    return lax.dot_general(
        left, right, (((left_dim,), (right_dim,)), ((), ())), preferred_element_type=F32
    )


def own_image(rows, columns, imgs, own_slots, share):
    row = lax.broadcasted_iota(jnp.int32, (rows, columns), 0)
    column = lax.broadcasted_iota(jnp.int32, (rows, columns), 1)
    return (row // own_slots) % imgs == column // share


def slot_rows(rows, slots, imgs, own_slots, core_first=False):
    row = lax.broadcasted_iota(jnp.int32, (rows, slots), 0)
    column = lax.broadcasted_iota(jnp.int32, (rows, slots), 1)
    expert = row // (imgs * own_slots)
    if core_first:
        half = slots // own_slots // 2
        expert = (expert % half) * 2 + expert // half
    slot = expert * own_slots + row % own_slots
    return jnp.where(slot == column, 1.0, 0.0).astype(BF16)


def lanes_of(columns, rows):
    lane = lax.broadcasted_iota(jnp.int32, (rows, 128), 1)
    block = jnp.zeros((rows, 128), F32)
    at = 0
    for value in columns:
        high = value.astype(BF16).astype(F32)
        middle = (value - high).astype(BF16).astype(F32)
        for term in (high, middle, value - high - middle):
            block = jnp.where(lane == at, term, block)
            at += 1
    return block


def column_of(block, at):
    lane = lax.broadcasted_iota(jnp.int32, block.shape, 1)
    inside = (lane >= 3 * at) & (lane < 3 * at + 3)
    return jnp.sum(jnp.where(inside, block, 0.0), axis=1, keepdims=True)


def route(imgs, own_slots, params_ref, both_ref, sent_ref, logits_ref, combine_ref):
    tokens, cotangent = both_ref[0], both_ref[1]
    slots, d = params_ref.shape
    rows, columns = logits_ref.shape
    spread = dot(slot_rows(rows, slots, imgs, own_slots), params_ref[...]).astype(BF16)
    logits = dot(spread, tokens, 1, 1)
    mine = own_image(rows, columns, imgs, own_slots, columns // imgs)
    logits = jnp.where(mine, logits, jnp.finfo(F32).min)
    logits_ref[...] = logits
    raised = jnp.exp(logits - jnp.max(logits, axis=0, keepdims=True))
    combine = raised / jnp.sum(raised, axis=0, keepdims=True)
    combine_ref[...] = combine
    peak = jnp.max(logits, axis=1, keepdims=True)
    weight = jnp.exp(logits - peak)
    mass = jnp.sum(weight, axis=1, keepdims=True)
    sent_ref[:, :d] = dot(weight.astype(BF16), tokens).astype(BF16)
    sent_ref[:, d : d + 128] = lanes_of([peak, mass], rows).astype(BF16)
    sent_ref[:, d + 128 :] = dot(combine.astype(BF16), cotangent).astype(BF16)


def collect(peers, taken_ref, own_ref, wide_ref, scalars_ref):
    rows, d = wide_ref.shape
    stats = taken_ref[:, d : d + 128].astype(F32)
    peaks = column_of(stats, 0).reshape(peers, rows, 1)
    masses = column_of(stats, 1).reshape(peers, rows, 1)
    top = jnp.max(peaks, axis=0)
    scale = jnp.exp(peaks - top[None])
    total = jnp.sum(masses * scale, axis=0)
    part_in = taken_ref[:, :d].astype(F32).reshape(peers, rows, d)
    slot_in = jnp.sum(part_in * scale, axis=0) / total
    slot_out_grad = jnp.sum(taken_ref[:, d + 128 :].astype(F32).reshape(peers, rows, d), axis=0)
    own_ref[...] = jnp.concatenate([slot_in, slot_out_grad], axis=0).astype(BF16)
    wide_ref[...] = slot_in
    lane = lax.broadcasted_iota(jnp.int32, scalars_ref.shape, 1)
    scalars_ref[...] = jnp.where(lane == 0, top, total)


def deliver(far, peers, taken_ref, wide_ref, scalars_ref, back_ref):
    rows, d = wide_ref.shape
    owned = jnp.sum(taken_ref[...].astype(F32).reshape(far, 2 * rows, d), axis=0)
    owned = owned.astype(BF16).astype(F32)
    slot_out, slot_in_grad = owned[:rows], owned[rows:]
    col = jnp.sum(slot_in_grad * wide_ref[...], axis=1, keepdims=True)
    top, total = scalars_ref[:, 0:1], scalars_ref[:, 1:2]
    stats = lanes_of([top, total, col], rows)
    for at, value in ((0, slot_out), (d, slot_in_grad), (2 * d, stats)):
        copies = jnp.concatenate([value] * peers, axis=0).astype(BF16)
        back_ref[:, at : at + value.shape[1]] = copies


def finish(
    imgs, own_slots, back_ref, logits_ref, combine_ref, params_ref, both_ref,
    token_grad_ref, share_ref,
):
    tokens, cotangent = both_ref[0], both_ref[1]
    slots, d = params_ref.shape
    rows = logits_ref.shape[0]
    block = imgs * own_slots
    order = [at for core in range(2) for at in range(core * block, rows, 2 * block)]
    logits = jnp.concatenate([logits_ref[at : at + block] for at in order], axis=0)
    combine = jnp.concatenate([combine_ref[at : at + block] for at in order], axis=0)
    slot_out, slot_in_grad = back_ref[:, :d], back_ref[:, d : 2 * d]
    stats = back_ref[:, 2 * d :].astype(F32)
    top, total, col = [column_of(stats, at) for at in range(3)]
    dispatch = jnp.exp(logits - top) / total
    combine_grad = dot(slot_out, cotangent, 1, 1)
    dispatch_grad = dot(slot_in_grad, tokens, 1, 1)
    row_sums = jnp.sum(combine * combine_grad, axis=0, keepdims=True)
    logit_grad = dispatch * (dispatch_grad - col) + combine * (combine_grad - row_sums)
    members = slot_rows(rows, slots, imgs, own_slots, True)
    by_slot = dot(members, logit_grad.astype(BF16), 0, 0).astype(BF16)
    share_ref[...] = dot(by_slot, tokens).astype(BF16)
    token_grad = dot(dispatch.astype(BF16), slot_in_grad, 0, 0)
    token_grad = token_grad + dot(by_slot, params_ref[...], 0, 0)
    token_grad_ref[...] = token_grad.astype(BF16)


def call(kernel, out_shape, flops, *operands):
    shapes = [jax.ShapeDtypeStruct(shape, dtype) for shape, dtype in out_shape]
    size = sum(value.size * value.dtype.itemsize for value in list(operands) + shapes)
    return pl.pallas_call(
        kernel,
        out_shape=shapes,
        compiler_params=pltpu.CompilerParams(vmem_limit_bytes=32 * 1024 * 1024),
        cost_estimate=pl.CostEstimate(flops=flops, bytes_accessed=size, transcendentals=16384),
    )(*operands)


def hidden(all_in, all_out_grad, w_in, w_out, own_slots):
    shape = (all_in.shape[0], w_in.shape[0])
    row = lax.broadcasted_iota(jnp.int32, shape, 0)
    column = lax.broadcasted_iota(jnp.int32, shape, 1)
    mine = row % own_slots == column // (shape[1] // own_slots)
    activated, slope = gelu_and_slope(dot(all_in, w_in, 1, 1))
    preact_grad = dot(all_out_grad, w_out, 1, 1) * slope
    return (
        jnp.where(mine, activated, 0.0).astype(BF16),
        jnp.where(mine, preact_grad, 0.0).astype(BF16),
    )


def rows_of(gathered_ref, which):
    return jnp.concatenate([gathered_ref[q, which] for q in range(gathered_ref.shape[0])], axis=0)


def experts(
    own_slots, gathered_ref, w_in_ref, w_out_ref, partial_ref, activated_ref, preact_grad_ref
):
    w_in, w_out = w_in_ref[...], w_out_ref[...]
    activated, preact_grad = hidden(
        rows_of(gathered_ref, 0), rows_of(gathered_ref, 1), w_in, w_out, own_slots
    )
    activated_ref[...] = activated
    preact_grad_ref[...] = preact_grad
    slot_out = dot(activated, w_out).astype(BF16)
    slot_in_grad = dot(preact_grad, w_in).astype(BF16)
    size = partial_ref.shape[2]
    for q in range(partial_ref.shape[0]):
        partial_ref[q, 0] = slot_out[q * size : (q + 1) * size]
        partial_ref[q, 1] = slot_in_grad[q * size : (q + 1) * size]


def weight_grads(gathered_ref, activated_ref, preact_grad_ref, w_in_grad_ref, w_out_grad_ref):
    all_in, all_out_grad = rows_of(gathered_ref, 0), rows_of(gathered_ref, 1)
    w_in_grad_ref[...] = dot(preact_grad_ref[...], all_in, 0, 0).astype(BF16)
    w_out_grad_ref[...] = dot(activated_ref[...], all_out_grad, 0, 0).astype(BF16)


def add_square(rows, taken_ref, total_ref):
    total = taken_ref[0].astype(F32)
    for q in range(1, taken_ref.shape[0]):
        total += taken_ref[q].astype(F32)
    pieces = [
        total[which, at : at + rows] for at in range(0, total.shape[1], rows) for which in range(2)
    ]
    total_ref[...] = jnp.concatenate(pieces, axis=0).astype(BF16)


def on_device(tokens, cotangent, slot_params, w_in, w_out):
    imgs, share, d = tokens.shape
    peers = lax.axis_size("expert")
    own_slots = slot_params.shape[1]
    slots = peers * own_slots
    rows = own_slots * imgs

    params = everywhere(slot_params.T, "expert").reshape(slots, d)
    pairs = (peers * rows, imgs * share)
    wide = 2 * d + 128
    flat = (imgs * share, d)
    params, tokens, cotangent = lax.optimization_barrier((params, tokens, cotangent))
    both = jnp.stack([tokens.reshape(flat), cotangent.reshape(flat)])
    sent, logits, combine = call(
        functools.partial(route, imgs, own_slots),
        [((peers * rows, wide), BF16), (pairs, F32), (pairs, F32)],
        100_000_000, params, both,
    )
    taken = exchange(sent.reshape(peers, rows, wide), "expert")
    own, slot_in_wide, scalars = call(
        functools.partial(collect, peers),
        [((2 * rows, d), BF16), ((rows, d), F32), ((rows, 128), F32)],
        1_000_000, taken.reshape(peers * rows, wide),
    )

    gathered = gather_dp(own)
    flat_in, flat_out = jnp.swapaxes(w_in, 1, 2).reshape(-1, d), w_out.reshape(-1, d)
    units = (gathered.shape[0] * gathered.shape[2], flat_in.shape[0])
    partial, activated, preact_grad = call(
        functools.partial(experts, own_slots),
        [(gathered.shape, BF16), (units, BF16), (units, BF16)],
        1_000_000_000, gathered, flat_in, flat_out,
    )
    w_in_grad, w_out_grad = call(
        weight_grads, [(flat_in.shape, BF16)] * 2, 600_000_000, gathered, activated, preact_grad
    )
    w_in_grad = jnp.swapaxes(w_in_grad.reshape(own_slots, -1, d), 1, 2)
    w_out_grad = w_out_grad.reshape(w_out.shape)
    terms = reduce_dp(partial, rows)
    (back,) = call(
        functools.partial(deliver, terms.shape[0], peers // 2), [((peers // 2 * rows, wide), BF16)],
        1_000_000, terms.reshape(-1, d), slot_in_wide, scalars,
    )
    back = exchange(back.reshape(peers // 2, rows, wide), "expert", expert_groups(0, 1))
    back = everywhere(back.reshape(-1, wide), "expert", expert_groups(2))

    token_grad, share_grad = call(
        functools.partial(finish, imgs, own_slots),
        [(flat, BF16), ((slots, d), BF16)],
        100_000_000, back.reshape(peers * rows, wide), logits, combine, params, both,
    )
    token_grad = token_grad.reshape(tokens.shape)

    share_grad = jnp.broadcast_to(share_grad.reshape(1, peers, own_slots, d), (2, peers, own_slots, d))
    share_grad = exchange(
        share_grad.reshape(2 * peers, own_slots, d), ("dp", "expert"), plane_groups()
    )
    share_grad = jnp.sum(share_grad.astype(F32), axis=0).astype(BF16)
    share_grad = everywhere(share_grad, "dp", dp_groups(1, 2))
    share_grad = jnp.sum(share_grad.astype(F32), axis=0)
    slot_grad = share_grad.T
    return (token_grad, slot_grad, w_in_grad, w_out_grad)


def solution(mesh):
    placed = (
        P("dp", "expert", None),
        P("dp", "expert", None),
        P(None, "expert"),
        P("expert", None, "dp"),
        P("expert", "dp", None),
    )
    return jax.shard_map(
        on_device,
        mesh=mesh,
        in_specs=placed,
        out_specs=(
            P("dp", "expert", None),
            P(None, "expert"),
            P("expert", None, "dp"),
            P("expert", "dp", None),
        ),
        check_vma=False,
    )
```

```python
import functools

import jax
import jax.numpy as jnp
import numpy as np
from jax import lax
from jax.experimental import pallas as pl
from jax.experimental.pallas import tpu as pltpu
from jax.sharding import PartitionSpec as P

F32 = jnp.float32
BF16 = jnp.bfloat16


def gelu_and_slope(value):
    below = 0.5 * (1.0 + lax.erf(value * 0.5**0.5))
    density = jnp.exp(-0.5 * value * value) * (1.0 / (2.0 * np.pi) ** 0.5)
    return value * below, below + value * density


def groups_of(axis, sizes, inner):
    shape = [lax.axis_size(axis) // sizes[0] // sizes[1], sizes[0], sizes[1]]
    ids = np.arange(lax.axis_size(axis)).reshape(shape)
    outer = [part for part in range(3) if part not in inner]
    width = int(np.prod([shape[part] for part in inner]))
    return ids.transpose(outer + list(inner)).reshape(-1, width).tolist()


def exchange(value, axis, groups=None):
    return lax.all_to_all(
        value, axis, split_axis=0, concat_axis=0, axis_index_groups=groups, tiled=True
    )


def everywhere(value, axis, groups=None):
    peers = lax.axis_size(axis) if groups is None else len(groups[0])
    return exchange(jnp.broadcast_to(value[None], (peers,) + value.shape), axis, groups)


def dp_groups(*inner):
    return groups_of("dp", (lax.axis_size("dp") // 4, 2), inner)


def far_groups():
    depth = lax.axis_size("dp") // 2
    late = [int(pair >= depth // 4) for pair in range(depth // 2)]
    return [
        [y * depth + 2 * pair + (late[pair] ^ which) for pair in range(depth // 2)]
        for y in range(2)
        for which in range(2)
    ]


def expert_groups(*inner):
    return groups_of("expert", (2, 2), inner)


def plane_groups():
    peers, depth = lax.axis_size("expert"), lax.axis_size("dp") // 2
    ids = np.arange(2 * depth * peers).reshape(2, depth, peers)
    return ids.transpose(1, 0, 2).reshape(depth, 2 * peers).tolist()


def gather_dp(own):
    rows, d = own.shape[0] // 2, own.shape[1]
    far = everywhere(own, "dp", far_groups()).reshape(-1, 2, rows, d)
    far = jnp.transpose(far, (1, 0, 2, 3)).reshape(2, -1, d)
    return everywhere(far, "dp", dp_groups(0, 2))


def reduce_dp(partial, rows):
    d = partial.shape[-1]
    taken = exchange(partial, "dp", dp_groups(0, 2))
    (total,) = call(
        functools.partial(add_square, rows), [((2 * partial.shape[2], d), BF16)], 2_000_000, taken
    )
    return exchange(total.reshape(-1, 2 * rows, d), "dp", far_groups())


def dot(left, right, left_dim=1, right_dim=0):
    return lax.dot_general(
        left, right, (((left_dim,), (right_dim,)), ((), ())), preferred_element_type=F32
    )


def own_image(rows, columns, imgs, own_slots, share):
    row = lax.broadcasted_iota(jnp.int32, (rows, columns), 0)
    column = lax.broadcasted_iota(jnp.int32, (rows, columns), 1)
    return (row // own_slots) % imgs == column // share


def slot_rows(rows, slots, imgs, own_slots, core_first=False):
    row = lax.broadcasted_iota(jnp.int32, (rows, slots), 0)
    column = lax.broadcasted_iota(jnp.int32, (rows, slots), 1)
    expert = row // (imgs * own_slots)
    if core_first:
        half = slots // own_slots // 2
        expert = (expert % half) * 2 + expert // half
    slot = expert * own_slots + row % own_slots
    return jnp.where(slot == column, 1.0, 0.0).astype(BF16)


def lanes_of(columns, rows):
    lane = lax.broadcasted_iota(jnp.int32, (rows, 128), 1)
    block = jnp.zeros((rows, 128), F32)
    at = 0
    for value in columns:
        high = value.astype(BF16).astype(F32)
        middle = (value - high).astype(BF16).astype(F32)
        for term in (high, middle, value - high - middle):
            block = jnp.where(lane == at, term, block)
            at += 1
    return block


def column_of(block, at):
    lane = lax.broadcasted_iota(jnp.int32, block.shape, 1)
    inside = (lane >= 3 * at) & (lane < 3 * at + 3)
    return jnp.sum(jnp.where(inside, block, 0.0), axis=1, keepdims=True)


def route(imgs, own_slots, params_ref, both_ref, sent_ref, logits_ref, combine_ref):
    tokens, cotangent = both_ref[0], both_ref[1]
    slots, d = params_ref.shape
    rows, columns = logits_ref.shape
    spread = dot(slot_rows(rows, slots, imgs, own_slots), params_ref[...]).astype(BF16)
    logits = dot(spread, tokens, 1, 1)
    mine = own_image(rows, columns, imgs, own_slots, columns // imgs)
    logits = jnp.where(mine, logits, jnp.finfo(F32).min)
    logits_ref[...] = logits
    raised = jnp.exp(logits - jnp.max(logits, axis=0, keepdims=True))
    combine = raised / jnp.sum(raised, axis=0, keepdims=True)
    combine_ref[...] = combine
    peak = jnp.max(logits, axis=1, keepdims=True)
    weight = jnp.exp(logits - peak)
    mass = jnp.sum(weight, axis=1, keepdims=True)
    sent_ref[:, :d] = dot(weight.astype(BF16), tokens).astype(BF16)
    sent_ref[:, d : d + 128] = lanes_of([peak, mass], rows).astype(BF16)
    sent_ref[:, d + 128 :] = dot(combine.astype(BF16), cotangent).astype(BF16)


def collect(peers, taken_ref, own_ref, wide_ref, scalars_ref):
    rows, d = wide_ref.shape
    stats = taken_ref[:, d : d + 128].astype(F32)
    peaks = column_of(stats, 0).reshape(peers, rows, 1)
    masses = column_of(stats, 1).reshape(peers, rows, 1)
    top = jnp.max(peaks, axis=0)
    scale = jnp.exp(peaks - top[None])
    total = jnp.sum(masses * scale, axis=0)
    part_in = taken_ref[:, :d].astype(F32).reshape(peers, rows, d)
    slot_in = jnp.sum(part_in * scale, axis=0) / total
    slot_out_grad = jnp.sum(taken_ref[:, d + 128 :].astype(F32).reshape(peers, rows, d), axis=0)
    own_ref[...] = jnp.concatenate([slot_in, slot_out_grad], axis=0).astype(BF16)
    wide_ref[...] = slot_in
    lane = lax.broadcasted_iota(jnp.int32, scalars_ref.shape, 1)
    scalars_ref[...] = jnp.where(lane == 0, top, total)


def deliver(far, peers, taken_ref, wide_ref, scalars_ref, back_ref):
    rows, d = wide_ref.shape
    owned = jnp.sum(taken_ref[...].astype(F32).reshape(far, 2 * rows, d), axis=0)
    owned = owned.astype(BF16).astype(F32)
    slot_out, slot_in_grad = owned[:rows], owned[rows:]
    col = jnp.sum(slot_in_grad * wide_ref[...], axis=1, keepdims=True)
    top, total = scalars_ref[:, 0:1], scalars_ref[:, 1:2]
    stats = lanes_of([top, total, col], rows)
    for at, value in ((0, slot_out), (d, slot_in_grad), (2 * d, stats)):
        copies = jnp.concatenate([value] * peers, axis=0).astype(BF16)
        back_ref[:, at : at + value.shape[1]] = copies


def finish(
    imgs, own_slots, back_ref, logits_ref, combine_ref, params_ref, both_ref,
    token_grad_ref, share_ref,
):
    tokens, cotangent = both_ref[0], both_ref[1]
    slots, d = params_ref.shape
    rows = logits_ref.shape[0]
    block = imgs * own_slots
    order = [at for core in range(2) for at in range(core * block, rows, 2 * block)]
    logits = jnp.concatenate([logits_ref[at : at + block] for at in order], axis=0)
    combine = jnp.concatenate([combine_ref[at : at + block] for at in order], axis=0)
    slot_out, slot_in_grad = back_ref[:, :d], back_ref[:, d : 2 * d]
    stats = back_ref[:, 2 * d :].astype(F32)
    top, total, col = [column_of(stats, at) for at in range(3)]
    dispatch = jnp.exp(logits - top) / total
    combine_grad = dot(slot_out, cotangent, 1, 1)
    dispatch_grad = dot(slot_in_grad, tokens, 1, 1)
    row_sums = jnp.sum(combine * combine_grad, axis=0, keepdims=True)
    logit_grad = dispatch * (dispatch_grad - col) + combine * (combine_grad - row_sums)
    members = slot_rows(rows, slots, imgs, own_slots, True)
    by_slot = dot(members, logit_grad.astype(BF16), 0, 0).astype(BF16)
    share_ref[...] = dot(by_slot, tokens).astype(BF16)
    token_grad = dot(dispatch.astype(BF16), slot_in_grad, 0, 0)
    token_grad = token_grad + dot(by_slot, params_ref[...], 0, 0)
    token_grad_ref[...] = token_grad.astype(BF16)


def call(kernel, out_shape, flops, *operands):
    shapes = [jax.ShapeDtypeStruct(shape, dtype) for shape, dtype in out_shape]
    size = sum(value.size * value.dtype.itemsize for value in list(operands) + shapes)
    return pl.pallas_call(
        kernel,
        out_shape=shapes,
        compiler_params=pltpu.CompilerParams(vmem_limit_bytes=32 * 1024 * 1024),
        cost_estimate=pl.CostEstimate(flops=flops, bytes_accessed=size, transcendentals=16384),
    )(*operands)


def hidden(all_in, all_out_grad, w_in, w_out, own_slots):
    shape = (all_in.shape[0], w_in.shape[0])
    row = lax.broadcasted_iota(jnp.int32, shape, 0)
    column = lax.broadcasted_iota(jnp.int32, shape, 1)
    mine = row % own_slots == column // (shape[1] // own_slots)
    activated, slope = gelu_and_slope(dot(all_in, w_in, 1, 1))
    preact_grad = dot(all_out_grad, w_out, 1, 1) * slope
    return (
        jnp.where(mine, activated, 0.0).astype(BF16),
        jnp.where(mine, preact_grad, 0.0).astype(BF16),
    )


def rows_of(gathered_ref, which):
    return jnp.concatenate([gathered_ref[q, which] for q in range(gathered_ref.shape[0])], axis=0)


def experts(
    own_slots, gathered_ref, w_in_ref, w_out_ref, partial_ref, activated_ref, preact_grad_ref
):
    w_in, w_out = w_in_ref[...], w_out_ref[...]
    activated, preact_grad = hidden(
        rows_of(gathered_ref, 0), rows_of(gathered_ref, 1), w_in, w_out, own_slots
    )
    activated_ref[...] = activated
    preact_grad_ref[...] = preact_grad
    slot_out = dot(activated, w_out).astype(BF16)
    slot_in_grad = dot(preact_grad, w_in).astype(BF16)
    size = partial_ref.shape[2]
    for q in range(partial_ref.shape[0]):
        partial_ref[q, 0] = slot_out[q * size : (q + 1) * size]
        partial_ref[q, 1] = slot_in_grad[q * size : (q + 1) * size]


def weight_grads(gathered_ref, activated_ref, preact_grad_ref, w_in_grad_ref, w_out_grad_ref):
    all_in, all_out_grad = rows_of(gathered_ref, 0), rows_of(gathered_ref, 1)
    w_in_grad_ref[...] = dot(preact_grad_ref[...], all_in, 0, 0).astype(BF16)
    w_out_grad_ref[...] = dot(activated_ref[...], all_out_grad, 0, 0).astype(BF16)


def add_square(rows, taken_ref, total_ref):
    total = taken_ref[0].astype(F32)
    for q in range(1, taken_ref.shape[0]):
        total += taken_ref[q].astype(F32)
    pieces = [
        total[which, at : at + rows] for at in range(0, total.shape[1], rows) for which in range(2)
    ]
    total_ref[...] = jnp.concatenate(pieces, axis=0).astype(BF16)


def on_device(tokens, cotangent, slot_params, w_in, w_out):
    imgs, share, d = tokens.shape
    peers = lax.axis_size("expert")
    own_slots = slot_params.shape[1]
    slots = peers * own_slots
    rows = own_slots * imgs

    params = everywhere(slot_params.T, "expert").reshape(slots, d)
    pairs = (peers * rows, imgs * share)
    wide = 2 * d + 128
    flat = (imgs * share, d)
    params, tokens, cotangent = lax.optimization_barrier((params, tokens, cotangent))
    both = jnp.stack([tokens.reshape(flat), cotangent.reshape(flat)])
    sent, logits, combine = call(
        functools.partial(route, imgs, own_slots),
        [((peers * rows, wide), BF16), (pairs, F32), (pairs, F32)],
        100_000_000, params, both,
    )
    taken = exchange(sent.reshape(peers, rows, wide), "expert")
    own, slot_in_wide, scalars = call(
        functools.partial(collect, peers),
        [((2 * rows, d), BF16), ((rows, d), F32), ((rows, 128), F32)],
        1_000_000, taken.reshape(peers * rows, wide),
    )

    gathered = gather_dp(own)
    flat_in, flat_out = jnp.swapaxes(w_in, 1, 2).reshape(-1, d), w_out.reshape(-1, d)
    units = (gathered.shape[0] * gathered.shape[2], flat_in.shape[0])
    partial, activated, preact_grad = call(
        functools.partial(experts, own_slots),
        [(gathered.shape, BF16), (units, BF16), (units, BF16)],
        1_000_000_000, gathered, flat_in, flat_out,
    )
    w_in_grad, w_out_grad = call(
        weight_grads, [(flat_in.shape, BF16)] * 2, 600_000_000, gathered, activated, preact_grad
    )
    w_in_grad = jnp.swapaxes(w_in_grad.reshape(own_slots, -1, d), 1, 2)
    w_out_grad = w_out_grad.reshape(w_out.shape)
    terms = reduce_dp(partial, rows)
    (back,) = call(
        functools.partial(deliver, terms.shape[0], peers // 2), [((peers // 2 * rows, wide), BF16)],
        1_000_000, terms.reshape(-1, d), slot_in_wide, scalars,
    )
    back = exchange(back.reshape(peers // 2, rows, wide), "expert", expert_groups(0, 1))
    back = everywhere(back.reshape(-1, wide), "expert", expert_groups(2))

    token_grad, share_grad = call(
        functools.partial(finish, imgs, own_slots),
        [(flat, BF16), ((slots, d), BF16)],
        100_000_000, back.reshape(peers * rows, wide), logits, combine, params, both,
    )
    token_grad = token_grad.reshape(tokens.shape)

    share_grad = jnp.broadcast_to(share_grad.reshape(1, peers, own_slots, d), (2, peers, own_slots, d))
    share_grad = exchange(
        share_grad.reshape(2 * peers, own_slots, d), ("dp", "expert"), plane_groups()
    )
    share_grad = jnp.sum(share_grad.astype(F32), axis=0).astype(BF16)
    share_grad = everywhere(share_grad, "dp", dp_groups(1, 2))
    share_grad = jnp.sum(share_grad.astype(F32), axis=0)
    slot_grad = share_grad.T
    return (token_grad, slot_grad, w_in_grad, w_out_grad)


def solution(mesh):
    placed = (
        P("dp", "expert", None),
        P("dp", "expert", None),
        P(None, "expert"),
        P("expert", None, "dp"),
        P("expert", "dp", None),
    )
    return jax.shard_map(
        on_device,
        mesh=mesh,
        in_specs=placed,
        out_specs=(
            P("dp", "expert", None),
            P(None, "expert"),
            P("expert", None, "dp"),
            P("expert", "dp", None),
        ),
        check_vma=False,
    )
```

```python
import functools

import jax
import jax.numpy as jnp
import numpy as np
from jax import lax
from jax.experimental import pallas as pl
from jax.experimental.pallas import tpu as pltpu
from jax.sharding import PartitionSpec as P

F32 = jnp.float32
BF16 = jnp.bfloat16


def gelu_and_slope(value):
    below = 0.5 * (1.0 + lax.erf(value * 0.5**0.5))
    density = jnp.exp(-0.5 * value * value) * (1.0 / (2.0 * np.pi) ** 0.5)
    return value * below, below + value * density


def groups_of(axis, sizes, inner):
    shape = [lax.axis_size(axis) // sizes[0] // sizes[1], sizes[0], sizes[1]]
    ids = np.arange(lax.axis_size(axis)).reshape(shape)
    outer = [part for part in range(3) if part not in inner]
    width = int(np.prod([shape[part] for part in inner]))
    return ids.transpose(outer + list(inner)).reshape(-1, width).tolist()


def exchange(value, axis, groups=None):
    return lax.all_to_all(
        value, axis, split_axis=0, concat_axis=0, axis_index_groups=groups, tiled=True
    )


def everywhere(value, axis, groups=None):
    peers = lax.axis_size(axis) if groups is None else len(groups[0])
    return exchange(jnp.broadcast_to(value[None], (peers,) + value.shape), axis, groups)


def dp_groups(*inner):
    return groups_of("dp", (lax.axis_size("dp") // 4, 2), inner)


def z_groups(of_core):
    peers, depth = lax.axis_size("expert"), lax.axis_size("dp") // 2
    return [
        [(y * depth + z % depth) * peers + expert for y, z in group]
        for expert in range(peers)
        for group in of_core(expert % 2, depth)
    ]


def far_of_core(core, depth):
    late = [int(pair >= depth // 4) for pair in range(depth // 2)]
    return [
        [(y, 2 * pair + (late[pair] ^ which) + core) for pair in range(depth // 2)]
        for y in range(2)
        for which in range(2)
    ]


def square_of_core(core, depth):
    return [
        [(y, 2 * pair + near + core) for y in range(2) for near in range(2)]
        for pair in range(depth // 2)
    ]


def expert_groups(*inner):
    return groups_of("expert", (2, 2), inner)


def plane_groups():
    peers, depth = lax.axis_size("expert"), lax.axis_size("dp") // 2
    ids = np.arange(2 * depth * peers).reshape(2, depth, peers)
    return ids.transpose(1, 0, 2).reshape(depth, 2 * peers).tolist()


def gather_dp(own):
    rows, d = own.shape[0] // 2, own.shape[1]
    far = everywhere(own, ("dp", "expert"), z_groups(far_of_core)).reshape(-1, 2, rows, d)
    far = jnp.transpose(far, (1, 0, 2, 3)).reshape(2, -1, d)
    return everywhere(far, ("dp", "expert"), z_groups(square_of_core))


def reduce_dp(partial, rows):
    d = partial.shape[-1]
    taken = exchange(partial, ("dp", "expert"), z_groups(square_of_core))
    (total,) = call(
        functools.partial(add_square, rows), [((2 * partial.shape[2], d), BF16)], 2_000_000, taken
    )
    return exchange(total.reshape(-1, 2 * rows, d), ("dp", "expert"), z_groups(far_of_core))


def dot(left, right, left_dim=1, right_dim=0):
    return lax.dot_general(
        left, right, (((left_dim,), (right_dim,)), ((), ())), preferred_element_type=F32
    )


def own_image(rows, columns, imgs, own_slots, share):
    row = lax.broadcasted_iota(jnp.int32, (rows, columns), 0)
    column = lax.broadcasted_iota(jnp.int32, (rows, columns), 1)
    return (row // own_slots) % imgs == column // share


def slot_rows(rows, slots, imgs, own_slots, core_first=False):
    row = lax.broadcasted_iota(jnp.int32, (rows, slots), 0)
    column = lax.broadcasted_iota(jnp.int32, (rows, slots), 1)
    expert = row // (imgs * own_slots)
    if core_first:
        half = slots // own_slots // 2
        expert = (expert % half) * 2 + expert // half
    slot = expert * own_slots + row % own_slots
    return jnp.where(slot == column, 1.0, 0.0).astype(BF16)


def lanes_of(columns, rows):
    lane = lax.broadcasted_iota(jnp.int32, (rows, 128), 1)
    block = jnp.zeros((rows, 128), F32)
    at = 0
    for value in columns:
        high = value.astype(BF16).astype(F32)
        middle = (value - high).astype(BF16).astype(F32)
        for term in (high, middle, value - high - middle):
            block = jnp.where(lane == at, term, block)
            at += 1
    return block


def column_of(block, at):
    lane = lax.broadcasted_iota(jnp.int32, block.shape, 1)
    inside = (lane >= 3 * at) & (lane < 3 * at + 3)
    return jnp.sum(jnp.where(inside, block, 0.0), axis=1, keepdims=True)


def route(imgs, own_slots, params_ref, both_ref, sent_ref, logits_ref, combine_ref):
    tokens, cotangent = both_ref[0], both_ref[1]
    slots, d = params_ref.shape
    rows, columns = logits_ref.shape
    spread = dot(slot_rows(rows, slots, imgs, own_slots), params_ref[...]).astype(BF16)
    logits = dot(spread, tokens, 1, 1)
    mine = own_image(rows, columns, imgs, own_slots, columns // imgs)
    logits = jnp.where(mine, logits, jnp.finfo(F32).min)
    logits_ref[...] = logits
    raised = jnp.exp(logits - jnp.max(logits, axis=0, keepdims=True))
    combine = raised / jnp.sum(raised, axis=0, keepdims=True)
    combine_ref[...] = combine
    peak = jnp.max(logits, axis=1, keepdims=True)
    weight = jnp.exp(logits - peak)
    mass = jnp.sum(weight, axis=1, keepdims=True)
    sent_ref[:, :d] = dot(weight.astype(BF16), tokens).astype(BF16)
    sent_ref[:, d : d + 128] = lanes_of([peak, mass], rows).astype(BF16)
    sent_ref[:, d + 128 :] = dot(combine.astype(BF16), cotangent).astype(BF16)


def collect(peers, taken_ref, own_ref, wide_ref, scalars_ref):
    rows, d = wide_ref.shape
    stats = taken_ref[:, d : d + 128].astype(F32)
    peaks = column_of(stats, 0).reshape(peers, rows, 1)
    masses = column_of(stats, 1).reshape(peers, rows, 1)
    top = jnp.max(peaks, axis=0)
    scale = jnp.exp(peaks - top[None])
    total = jnp.sum(masses * scale, axis=0)
    part_in = taken_ref[:, :d].astype(F32).reshape(peers, rows, d)
    slot_in = jnp.sum(part_in * scale, axis=0) / total
    slot_out_grad = jnp.sum(taken_ref[:, d + 128 :].astype(F32).reshape(peers, rows, d), axis=0)
    own_ref[...] = jnp.concatenate([slot_in, slot_out_grad], axis=0).astype(BF16)
    wide_ref[...] = slot_in
    lane = lax.broadcasted_iota(jnp.int32, scalars_ref.shape, 1)
    scalars_ref[...] = jnp.where(lane == 0, top, total)


def deliver(far, peers, taken_ref, wide_ref, scalars_ref, back_ref):
    rows, d = wide_ref.shape
    owned = jnp.sum(taken_ref[...].astype(F32).reshape(far, 2 * rows, d), axis=0)
    owned = owned.astype(BF16).astype(F32)
    slot_out, slot_in_grad = owned[:rows], owned[rows:]
    col = jnp.sum(slot_in_grad * wide_ref[...], axis=1, keepdims=True)
    top, total = scalars_ref[:, 0:1], scalars_ref[:, 1:2]
    stats = lanes_of([top, total, col], rows)
    for at, value in ((0, slot_out), (d, slot_in_grad), (2 * d, stats)):
        copies = jnp.concatenate([value] * peers, axis=0).astype(BF16)
        back_ref[:, at : at + value.shape[1]] = copies


def finish(
    imgs, own_slots, back_ref, logits_ref, combine_ref, params_ref, both_ref,
    token_grad_ref, share_ref,
):
    tokens, cotangent = both_ref[0], both_ref[1]
    slots, d = params_ref.shape
    rows = logits_ref.shape[0]
    block = imgs * own_slots
    order = [at for core in range(2) for at in range(core * block, rows, 2 * block)]
    logits = jnp.concatenate([logits_ref[at : at + block] for at in order], axis=0)
    combine = jnp.concatenate([combine_ref[at : at + block] for at in order], axis=0)
    slot_out, slot_in_grad = back_ref[:, :d], back_ref[:, d : 2 * d]
    stats = back_ref[:, 2 * d :].astype(F32)
    top, total, col = [column_of(stats, at) for at in range(3)]
    dispatch = jnp.exp(logits - top) / total
    combine_grad = dot(slot_out, cotangent, 1, 1)
    dispatch_grad = dot(slot_in_grad, tokens, 1, 1)
    row_sums = jnp.sum(combine * combine_grad, axis=0, keepdims=True)
    logit_grad = dispatch * (dispatch_grad - col) + combine * (combine_grad - row_sums)
    members = slot_rows(rows, slots, imgs, own_slots, True)
    by_slot = dot(members, logit_grad.astype(BF16), 0, 0).astype(BF16)
    share_ref[...] = dot(by_slot, tokens).astype(BF16)
    token_grad = dot(dispatch.astype(BF16), slot_in_grad, 0, 0)
    token_grad = token_grad + dot(by_slot, params_ref[...], 0, 0)
    token_grad_ref[...] = token_grad.astype(BF16)


def call(kernel, out_shape, flops, *operands):
    shapes = [jax.ShapeDtypeStruct(shape, dtype) for shape, dtype in out_shape]
    size = sum(value.size * value.dtype.itemsize for value in list(operands) + shapes)
    return pl.pallas_call(
        kernel,
        out_shape=shapes,
        compiler_params=pltpu.CompilerParams(vmem_limit_bytes=32 * 1024 * 1024),
        cost_estimate=pl.CostEstimate(flops=flops, bytes_accessed=size, transcendentals=16384),
    )(*operands)


def hidden(all_in, all_out_grad, w_in, w_out, own_slots):
    shape = (all_in.shape[0], w_in.shape[0])
    row = lax.broadcasted_iota(jnp.int32, shape, 0)
    column = lax.broadcasted_iota(jnp.int32, shape, 1)
    mine = row % own_slots == column // (shape[1] // own_slots)
    activated, slope = gelu_and_slope(dot(all_in, w_in, 1, 1))
    preact_grad = dot(all_out_grad, w_out, 1, 1) * slope
    return (
        jnp.where(mine, activated, 0.0).astype(BF16),
        jnp.where(mine, preact_grad, 0.0).astype(BF16),
    )


def rows_of(gathered_ref, which):
    return jnp.concatenate([gathered_ref[q, which] for q in range(gathered_ref.shape[0])], axis=0)


def experts(
    own_slots, gathered_ref, w_in_ref, w_out_ref, partial_ref, activated_ref, preact_grad_ref
):
    w_in, w_out = w_in_ref[...], w_out_ref[...]
    activated, preact_grad = hidden(
        rows_of(gathered_ref, 0), rows_of(gathered_ref, 1), w_in, w_out, own_slots
    )
    activated_ref[...] = activated
    preact_grad_ref[...] = preact_grad
    slot_out = dot(activated, w_out).astype(BF16)
    slot_in_grad = dot(preact_grad, w_in).astype(BF16)
    size = partial_ref.shape[2]
    for q in range(partial_ref.shape[0]):
        partial_ref[q, 0] = slot_out[q * size : (q + 1) * size]
        partial_ref[q, 1] = slot_in_grad[q * size : (q + 1) * size]


def weight_grads(gathered_ref, activated_ref, preact_grad_ref, w_in_grad_ref, w_out_grad_ref):
    all_in, all_out_grad = rows_of(gathered_ref, 0), rows_of(gathered_ref, 1)
    w_in_grad_ref[...] = dot(preact_grad_ref[...], all_in, 0, 0).astype(BF16)
    w_out_grad_ref[...] = dot(activated_ref[...], all_out_grad, 0, 0).astype(BF16)


def add_square(rows, taken_ref, total_ref):
    total = taken_ref[0].astype(F32)
    for q in range(1, taken_ref.shape[0]):
        total += taken_ref[q].astype(F32)
    pieces = [
        total[which, at : at + rows] for at in range(0, total.shape[1], rows) for which in range(2)
    ]
    total_ref[...] = jnp.concatenate(pieces, axis=0).astype(BF16)


def on_device(tokens, cotangent, slot_params, w_in, w_out):
    imgs, share, d = tokens.shape
    peers = lax.axis_size("expert")
    own_slots = slot_params.shape[1]
    slots = peers * own_slots
    rows = own_slots * imgs

    params = everywhere(slot_params.T, "expert").reshape(slots, d)
    pairs = (peers * rows, imgs * share)
    wide = 2 * d + 128
    flat = (imgs * share, d)
    params, tokens, cotangent = lax.optimization_barrier((params, tokens, cotangent))
    both = jnp.stack([tokens.reshape(flat), cotangent.reshape(flat)])
    sent, logits, combine = call(
        functools.partial(route, imgs, own_slots),
        [((peers * rows, wide), BF16), (pairs, F32), (pairs, F32)],
        100_000_000, params, both,
    )
    taken = exchange(sent.reshape(peers, rows, wide), "expert")
    own, slot_in_wide, scalars = call(
        functools.partial(collect, peers),
        [((2 * rows, d), BF16), ((rows, d), F32), ((rows, 128), F32)],
        1_000_000, taken.reshape(peers * rows, wide),
    )

    gathered = gather_dp(own)
    flat_in, flat_out = jnp.swapaxes(w_in, 1, 2).reshape(-1, d), w_out.reshape(-1, d)
    units = (gathered.shape[0] * gathered.shape[2], flat_in.shape[0])
    partial, activated, preact_grad = call(
        functools.partial(experts, own_slots),
        [(gathered.shape, BF16), (units, BF16), (units, BF16)],
        1_000_000_000, gathered, flat_in, flat_out,
    )
    w_in_grad, w_out_grad = call(
        weight_grads, [(flat_in.shape, BF16)] * 2, 600_000_000, gathered, activated, preact_grad
    )
    w_in_grad = jnp.swapaxes(w_in_grad.reshape(own_slots, -1, d), 1, 2)
    w_out_grad = w_out_grad.reshape(w_out.shape)
    terms = reduce_dp(partial, rows)
    (back,) = call(
        functools.partial(deliver, terms.shape[0], peers // 2), [((peers // 2 * rows, wide), BF16)],
        1_000_000, terms.reshape(-1, d), slot_in_wide, scalars,
    )
    back = exchange(back.reshape(peers // 2, rows, wide), "expert", expert_groups(0, 1))
    back = everywhere(back.reshape(-1, wide), "expert", expert_groups(2))

    token_grad, share_grad = call(
        functools.partial(finish, imgs, own_slots),
        [(flat, BF16), ((slots, d), BF16)],
        100_000_000, back.reshape(peers * rows, wide), logits, combine, params, both,
    )
    token_grad = token_grad.reshape(tokens.shape)

    share_grad = jnp.broadcast_to(share_grad.reshape(1, peers, own_slots, d), (2, peers, own_slots, d))
    share_grad = exchange(
        share_grad.reshape(2 * peers, own_slots, d), ("dp", "expert"), plane_groups()
    )
    share_grad = jnp.sum(share_grad.astype(F32), axis=0).astype(BF16)
    share_grad = everywhere(share_grad, "dp", dp_groups(1, 2))
    share_grad = jnp.sum(share_grad.astype(F32), axis=0)
    slot_grad = share_grad.T
    return (token_grad, slot_grad, w_in_grad, w_out_grad)


def solution(mesh):
    placed = (
        P("dp", "expert", None),
        P("dp", "expert", None),
        P(None, "expert"),
        P("expert", None, "dp"),
        P("expert", "dp", None),
    )
    return jax.shard_map(
        on_device,
        mesh=mesh,
        in_specs=placed,
        out_specs=(
            P("dp", "expert", None),
            P(None, "expert"),
            P("expert", None, "dp"),
            P("expert", "dp", None),
        ),
        check_vma=False,
    )
```

```python
import functools

import jax
import jax.numpy as jnp
import numpy as np
from jax import lax
from jax.experimental import pallas as pl
from jax.experimental.pallas import tpu as pltpu
from jax.sharding import PartitionSpec as P

F32 = jnp.float32
BF16 = jnp.bfloat16


def gelu_and_slope(value):
    below = 0.5 * (1.0 + lax.erf(value * 0.5**0.5))
    density = jnp.exp(-0.5 * value * value) * (1.0 / (2.0 * np.pi) ** 0.5)
    return value * below, below + value * density


def groups_of(axis, sizes, inner):
    shape = [lax.axis_size(axis) // sizes[0] // sizes[1], sizes[0], sizes[1]]
    ids = np.arange(lax.axis_size(axis)).reshape(shape)
    outer = [part for part in range(3) if part not in inner]
    width = int(np.prod([shape[part] for part in inner]))
    return ids.transpose(outer + list(inner)).reshape(-1, width).tolist()


def exchange(value, axis, groups=None):
    return lax.all_to_all(
        value, axis, split_axis=0, concat_axis=0, axis_index_groups=groups, tiled=True
    )


def everywhere(value, axis, groups=None):
    peers = lax.axis_size(axis) if groups is None else len(groups[0])
    return exchange(jnp.broadcast_to(value[None], (peers,) + value.shape), axis, groups)


def dp_groups(*inner):
    return groups_of("dp", (lax.axis_size("dp") // 4, 2), inner)


def far_groups():
    depth = lax.axis_size("dp") // 2
    late = [int(pair >= depth // 4) for pair in range(depth // 2)]
    return [
        [y * depth + 2 * pair + (late[pair] ^ which) for pair in range(depth // 2)]
        for y in range(2)
        for which in range(2)
    ]


def expert_groups(*inner):
    return groups_of("expert", (2, 2), inner)


def plane_groups():
    peers, depth = lax.axis_size("expert"), lax.axis_size("dp") // 2
    ids = np.arange(2 * depth * peers).reshape(2, depth, peers)
    return ids.transpose(1, 0, 2).reshape(depth, 2 * peers).tolist()


def gather_dp(own):
    rows, d = own.shape[0] // 2, own.shape[1]
    far = everywhere(own, "dp", far_groups()).reshape(-1, 2, rows, d)
    far = jnp.transpose(far, (1, 0, 2, 3)).reshape(2, -1, d)
    return everywhere(far, "dp", dp_groups(0, 2))


def reduce_dp(partial, rows):
    d = partial.shape[-1]
    taken = exchange(partial, "dp", dp_groups(0, 2))
    (total,) = call(
        functools.partial(add_square, rows), [((2 * partial.shape[2], d), BF16)], 2_000_000, taken
    )
    return exchange(total.reshape(-1, 2 * rows, d), "dp", far_groups())


def dot(left, right, left_dim=1, right_dim=0):
    return lax.dot_general(
        left, right, (((left_dim,), (right_dim,)), ((), ())), preferred_element_type=F32
    )


def own_image(rows, columns, imgs, own_slots, share):
    row = lax.broadcasted_iota(jnp.int32, (rows, columns), 0)
    column = lax.broadcasted_iota(jnp.int32, (rows, columns), 1)
    return (row // own_slots) % imgs == column // share


def slot_rows(rows, slots, imgs, own_slots, core_first=False):
    row = lax.broadcasted_iota(jnp.int32, (rows, slots), 0)
    column = lax.broadcasted_iota(jnp.int32, (rows, slots), 1)
    expert = row // (imgs * own_slots)
    if core_first:
        half = slots // own_slots // 2
        expert = (expert % half) * 2 + expert // half
    slot = expert * own_slots + row % own_slots
    return jnp.where(slot == column, 1.0, 0.0).astype(BF16)


def lanes_of(columns, rows):
    lane = lax.broadcasted_iota(jnp.int32, (rows, 128), 1)
    block = jnp.zeros((rows, 128), F32)
    at = 0
    for value in columns:
        high = value.astype(BF16).astype(F32)
        middle = (value - high).astype(BF16).astype(F32)
        for term in (high, middle, value - high - middle):
            block = jnp.where(lane == at, term, block)
            at += 1
    return block


def column_of(block, at):
    lane = lax.broadcasted_iota(jnp.int32, block.shape, 1)
    inside = (lane >= 3 * at) & (lane < 3 * at + 3)
    return jnp.sum(jnp.where(inside, block, 0.0), axis=1, keepdims=True)


def route(imgs, own_slots, params_ref, both_ref, sent_ref, logits_ref, combine_ref):
    tokens, cotangent = both_ref[0], both_ref[1]
    slots, d = params_ref.shape
    rows, columns = logits_ref.shape
    spread = dot(slot_rows(rows, slots, imgs, own_slots), params_ref[...]).astype(BF16)
    logits = dot(spread, tokens, 1, 1)
    mine = own_image(rows, columns, imgs, own_slots, columns // imgs)
    logits = jnp.where(mine, logits, jnp.finfo(F32).min)
    logits_ref[...] = logits
    raised = jnp.exp(logits - jnp.max(logits, axis=0, keepdims=True))
    combine = raised / jnp.sum(raised, axis=0, keepdims=True)
    combine_ref[...] = combine
    peak = jnp.max(logits, axis=1, keepdims=True)
    weight = jnp.exp(logits - peak)
    mass = jnp.sum(weight, axis=1, keepdims=True)
    sent_ref[:, :d] = dot(weight.astype(BF16), tokens).astype(BF16)
    sent_ref[:, d : d + 128] = lanes_of([peak, mass], rows).astype(BF16)
    sent_ref[:, d + 128 :] = dot(combine.astype(BF16), cotangent).astype(BF16)


def collect(peers, taken_ref, own_ref, wide_ref, scalars_ref):
    rows, d = wide_ref.shape
    stats = taken_ref[:, d : d + 128].astype(F32)
    peaks = column_of(stats, 0).reshape(peers, rows, 1)
    masses = column_of(stats, 1).reshape(peers, rows, 1)
    top = jnp.max(peaks, axis=0)
    scale = jnp.exp(peaks - top[None])
    total = jnp.sum(masses * scale, axis=0)
    part_in = taken_ref[:, :d].astype(F32).reshape(peers, rows, d)
    slot_in = jnp.sum(part_in * scale, axis=0) / total
    slot_out_grad = jnp.sum(taken_ref[:, d + 128 :].astype(F32).reshape(peers, rows, d), axis=0)
    own_ref[...] = jnp.concatenate([slot_in, slot_out_grad], axis=0).astype(BF16)
    wide_ref[...] = slot_in
    lane = lax.broadcasted_iota(jnp.int32, scalars_ref.shape, 1)
    scalars_ref[...] = jnp.where(lane == 0, top, total)


def deliver(far, peers, taken_ref, wide_ref, scalars_ref, back_ref):
    rows, d = wide_ref.shape
    owned = jnp.sum(taken_ref[...].astype(F32).reshape(far, 2 * rows, d), axis=0)
    owned = owned.astype(BF16).astype(F32)
    slot_out, slot_in_grad = owned[:rows], owned[rows:]
    col = jnp.sum(slot_in_grad * wide_ref[...], axis=1, keepdims=True)
    top, total = scalars_ref[:, 0:1], scalars_ref[:, 1:2]
    stats = lanes_of([top, total, col], rows)
    for at, value in ((0, slot_out), (d, slot_in_grad), (2 * d, stats)):
        copies = jnp.concatenate([value] * peers, axis=0).astype(BF16)
        back_ref[:, at : at + value.shape[1]] = copies


def finish(
    imgs, own_slots, back_ref, logits_ref, combine_ref, both_ref, share_ref, dispatch_ref, grad_ref
):
    tokens, cotangent = both_ref[0], both_ref[1]
    slots, d = share_ref.shape
    rows = logits_ref.shape[0]
    block = imgs * own_slots
    order = [at for core in range(2) for at in range(core * block, rows, 2 * block)]
    logits = jnp.concatenate([logits_ref[at : at + block] for at in order], axis=0)
    combine = jnp.concatenate([combine_ref[at : at + block] for at in order], axis=0)
    slot_out, slot_in_grad = back_ref[:, :d], back_ref[:, d : 2 * d]
    stats = back_ref[:, 2 * d :].astype(F32)
    top, total, col = [column_of(stats, at) for at in range(3)]
    dispatch = jnp.exp(logits - top) / total
    combine_grad = dot(slot_out, cotangent, 1, 1)
    dispatch_grad = dot(slot_in_grad, tokens, 1, 1)
    row_sums = jnp.sum(combine * combine_grad, axis=0, keepdims=True)
    logit_grad = dispatch * (dispatch_grad - col) + combine * (combine_grad - row_sums)
    members = slot_rows(rows, slots, imgs, own_slots, True)
    by_slot = dot(members, logit_grad.astype(BF16), 0, 0).astype(BF16)
    share_ref[...] = dot(by_slot, tokens).astype(BF16)
    dispatch_ref[...] = dispatch.astype(BF16)
    grad_ref[...] = by_slot


def token_grads(back_ref, dispatch_ref, grad_ref, params_ref, token_grad_ref):
    d = params_ref.shape[1]
    token_grad = dot(dispatch_ref[...], back_ref[:, d : 2 * d], 0, 0)
    token_grad = token_grad + dot(grad_ref[...], params_ref[...], 0, 0)
    token_grad_ref[...] = token_grad.astype(BF16)


def call(kernel, out_shape, flops, *operands):
    shapes = [jax.ShapeDtypeStruct(shape, dtype) for shape, dtype in out_shape]
    size = sum(value.size * value.dtype.itemsize for value in list(operands) + shapes)
    return pl.pallas_call(
        kernel,
        out_shape=shapes,
        compiler_params=pltpu.CompilerParams(vmem_limit_bytes=32 * 1024 * 1024),
        cost_estimate=pl.CostEstimate(flops=flops, bytes_accessed=size, transcendentals=16384),
    )(*operands)


def hidden(all_in, all_out_grad, w_in, w_out, own_slots):
    shape = (all_in.shape[0], w_in.shape[0])
    row = lax.broadcasted_iota(jnp.int32, shape, 0)
    column = lax.broadcasted_iota(jnp.int32, shape, 1)
    mine = row % own_slots == column // (shape[1] // own_slots)
    activated, slope = gelu_and_slope(dot(all_in, w_in, 1, 1))
    preact_grad = dot(all_out_grad, w_out, 1, 1) * slope
    return (
        jnp.where(mine, activated, 0.0).astype(BF16),
        jnp.where(mine, preact_grad, 0.0).astype(BF16),
    )


def rows_of(gathered_ref, which):
    return jnp.concatenate([gathered_ref[q, which] for q in range(gathered_ref.shape[0])], axis=0)


def experts(
    own_slots, gathered_ref, w_in_ref, w_out_ref, partial_ref, activated_ref, preact_grad_ref
):
    w_in, w_out = w_in_ref[...], w_out_ref[...]
    activated, preact_grad = hidden(
        rows_of(gathered_ref, 0), rows_of(gathered_ref, 1), w_in, w_out, own_slots
    )
    activated_ref[...] = activated
    preact_grad_ref[...] = preact_grad
    slot_out = dot(activated, w_out).astype(BF16)
    slot_in_grad = dot(preact_grad, w_in).astype(BF16)
    size = partial_ref.shape[2]
    for q in range(partial_ref.shape[0]):
        partial_ref[q, 0] = slot_out[q * size : (q + 1) * size]
        partial_ref[q, 1] = slot_in_grad[q * size : (q + 1) * size]


def weight_grads(gathered_ref, activated_ref, preact_grad_ref, w_in_grad_ref, w_out_grad_ref):
    all_in, all_out_grad = rows_of(gathered_ref, 0), rows_of(gathered_ref, 1)
    w_in_grad_ref[...] = dot(preact_grad_ref[...], all_in, 0, 0).astype(BF16)
    w_out_grad_ref[...] = dot(activated_ref[...], all_out_grad, 0, 0).astype(BF16)


def add_square(rows, taken_ref, total_ref):
    total = taken_ref[0].astype(F32)
    for q in range(1, taken_ref.shape[0]):
        total += taken_ref[q].astype(F32)
    pieces = [
        total[which, at : at + rows] for at in range(0, total.shape[1], rows) for which in range(2)
    ]
    total_ref[...] = jnp.concatenate(pieces, axis=0).astype(BF16)


def on_device(tokens, cotangent, slot_params, w_in, w_out):
    imgs, share, d = tokens.shape
    peers = lax.axis_size("expert")
    own_slots = slot_params.shape[1]
    slots = peers * own_slots
    rows = own_slots * imgs

    params = everywhere(slot_params.T, "expert").reshape(slots, d)
    pairs = (peers * rows, imgs * share)
    wide = 2 * d + 128
    flat = (imgs * share, d)
    params, tokens, cotangent = lax.optimization_barrier((params, tokens, cotangent))
    both = jnp.stack([tokens.reshape(flat), cotangent.reshape(flat)])
    sent, logits, combine = call(
        functools.partial(route, imgs, own_slots),
        [((peers * rows, wide), BF16), (pairs, F32), (pairs, F32)],
        100_000_000, params, both,
    )
    taken = exchange(sent.reshape(peers, rows, wide), "expert")
    own, slot_in_wide, scalars = call(
        functools.partial(collect, peers),
        [((2 * rows, d), BF16), ((rows, d), F32), ((rows, 128), F32)],
        1_000_000, taken.reshape(peers * rows, wide),
    )

    gathered = gather_dp(own)
    flat_in, flat_out = jnp.swapaxes(w_in, 1, 2).reshape(-1, d), w_out.reshape(-1, d)
    units = (gathered.shape[0] * gathered.shape[2], flat_in.shape[0])
    partial, activated, preact_grad = call(
        functools.partial(experts, own_slots),
        [(gathered.shape, BF16), (units, BF16), (units, BF16)],
        1_000_000_000, gathered, flat_in, flat_out,
    )
    w_in_grad, w_out_grad = call(
        weight_grads, [(flat_in.shape, BF16)] * 2, 600_000_000, gathered, activated, preact_grad
    )
    w_in_grad = jnp.swapaxes(w_in_grad.reshape(own_slots, -1, d), 1, 2)
    w_out_grad = w_out_grad.reshape(w_out.shape)
    terms = reduce_dp(partial, rows)
    (back,) = call(
        functools.partial(deliver, terms.shape[0], peers // 2), [((peers // 2 * rows, wide), BF16)],
        1_000_000, terms.reshape(-1, d), slot_in_wide, scalars,
    )
    back = exchange(back.reshape(peers // 2, rows, wide), "expert", expert_groups(0, 1))
    back = everywhere(back.reshape(-1, wide), "expert", expert_groups(2))

    back = back.reshape(peers * rows, wide)
    share_grad, dispatch, by_slot = call(
        functools.partial(finish, imgs, own_slots),
        [((slots, d), BF16), (pairs, BF16), ((slots, imgs * share), BF16)],
        70_000_000, back, logits, combine, both,
    )
    (token_grad,) = call(
        token_grads, [(flat, BF16)], 30_000_000, back, dispatch, by_slot, params
    )
    token_grad = token_grad.reshape(tokens.shape)

    share_grad = jnp.broadcast_to(share_grad.reshape(1, peers, own_slots, d), (2, peers, own_slots, d))
    share_grad = exchange(
        share_grad.reshape(2 * peers, own_slots, d), ("dp", "expert"), plane_groups()
    )
    share_grad = jnp.sum(share_grad.astype(F32), axis=0).astype(BF16)
    share_grad = everywhere(share_grad, "dp", dp_groups(1, 2))
    share_grad = jnp.sum(share_grad.astype(F32), axis=0)
    slot_grad = share_grad.T
    return (token_grad, slot_grad, w_in_grad, w_out_grad)


def solution(mesh):
    placed = (
        P("dp", "expert", None),
        P("dp", "expert", None),
        P(None, "expert"),
        P("expert", None, "dp"),
        P("expert", "dp", None),
    )
    return jax.shard_map(
        on_device,
        mesh=mesh,
        in_specs=placed,
        out_specs=(
            P("dp", "expert", None),
            P(None, "expert"),
            P("expert", None, "dp"),
            P("expert", "dp", None),
        ),
        check_vma=False,
    )
```

```python
import functools

import jax
import jax.numpy as jnp
import numpy as np
from jax import lax
from jax.experimental import pallas as pl
from jax.experimental.pallas import tpu as pltpu
from jax.sharding import PartitionSpec as P

F32 = jnp.float32
BF16 = jnp.bfloat16


def gelu_and_slope(value):
    below = 0.5 * (1.0 + lax.erf(value * 0.5**0.5))
    density = jnp.exp(-0.5 * value * value) * (1.0 / (2.0 * np.pi) ** 0.5)
    return value * below, below + value * density


def groups_of(axis, sizes, inner):
    shape = [lax.axis_size(axis) // sizes[0] // sizes[1], sizes[0], sizes[1]]
    ids = np.arange(lax.axis_size(axis)).reshape(shape)
    outer = [part for part in range(3) if part not in inner]
    width = int(np.prod([shape[part] for part in inner]))
    return ids.transpose(outer + list(inner)).reshape(-1, width).tolist()


def exchange(value, axis, groups=None):
    return lax.all_to_all(
        value, axis, split_axis=0, concat_axis=0, axis_index_groups=groups, tiled=True
    )


def everywhere(value, axis, groups=None):
    peers = lax.axis_size(axis) if groups is None else len(groups[0])
    return exchange(jnp.broadcast_to(value[None], (peers,) + value.shape), axis, groups)


def dp_groups(*inner):
    return groups_of("dp", (lax.axis_size("dp") // 4, 2), inner)


def far_groups():
    depth = lax.axis_size("dp") // 2
    late = [int(pair >= depth // 4) for pair in range(depth // 2)]
    return [
        [y * depth + 2 * pair + (late[pair] ^ which) for pair in range(depth // 2)]
        for y in range(2)
        for which in range(2)
    ]


def square_groups():
    return [[at[0], at[1], at[3], at[2]] for at in dp_groups(0, 2)]


def expert_groups(*inner):
    return groups_of("expert", (2, 2), inner)


def plane_groups():
    peers, depth = lax.axis_size("expert"), lax.axis_size("dp") // 2
    ids = np.arange(2 * depth * peers).reshape(2, depth, peers)
    return ids.transpose(1, 0, 2).reshape(depth, 2 * peers).tolist()


def gather_dp(own):
    rows, d = own.shape[0] // 2, own.shape[1]
    far = everywhere(own, "dp", far_groups()).reshape(-1, 2, rows, d)
    far = jnp.transpose(far, (1, 0, 2, 3)).reshape(2, -1, d)
    return everywhere(far, "dp", square_groups())


def reduce_dp(partial, rows):
    d = partial.shape[-1]
    taken = exchange(partial, "dp", square_groups())
    (total,) = call(
        functools.partial(add_square, rows), [((2 * partial.shape[2], d), BF16)], 2_000_000, taken
    )
    return exchange(total.reshape(-1, 2 * rows, d), "dp", far_groups())


def dot(left, right, left_dim=1, right_dim=0):
    return lax.dot_general(
        left, right, (((left_dim,), (right_dim,)), ((), ())), preferred_element_type=F32
    )


def own_image(rows, columns, imgs, own_slots, share):
    row = lax.broadcasted_iota(jnp.int32, (rows, columns), 0)
    column = lax.broadcasted_iota(jnp.int32, (rows, columns), 1)
    return (row // own_slots) % imgs == column // share


def slot_rows(rows, slots, imgs, own_slots, core_first=False):
    row = lax.broadcasted_iota(jnp.int32, (rows, slots), 0)
    column = lax.broadcasted_iota(jnp.int32, (rows, slots), 1)
    expert = row // (imgs * own_slots)
    if core_first:
        half = slots // own_slots // 2
        expert = (expert % half) * 2 + expert // half
    slot = expert * own_slots + row % own_slots
    return jnp.where(slot == column, 1.0, 0.0).astype(BF16)


def lanes_of(columns, rows):
    lane = lax.broadcasted_iota(jnp.int32, (rows, 128), 1)
    block = jnp.zeros((rows, 128), F32)
    at = 0
    for value in columns:
        high = value.astype(BF16).astype(F32)
        middle = (value - high).astype(BF16).astype(F32)
        for term in (high, middle, value - high - middle):
            block = jnp.where(lane == at, term, block)
            at += 1
    return block


def column_of(block, at):
    lane = lax.broadcasted_iota(jnp.int32, block.shape, 1)
    inside = (lane >= 3 * at) & (lane < 3 * at + 3)
    return jnp.sum(jnp.where(inside, block, 0.0), axis=1, keepdims=True)


def route(imgs, own_slots, params_ref, both_ref, sent_ref, logits_ref, combine_ref):
    tokens, cotangent = both_ref[0], both_ref[1]
    slots, d = params_ref.shape
    rows, columns = logits_ref.shape
    spread = dot(slot_rows(rows, slots, imgs, own_slots), params_ref[...]).astype(BF16)
    logits = dot(spread, tokens, 1, 1)
    mine = own_image(rows, columns, imgs, own_slots, columns // imgs)
    logits = jnp.where(mine, logits, jnp.finfo(F32).min)
    logits_ref[...] = logits
    raised = jnp.exp(logits - jnp.max(logits, axis=0, keepdims=True))
    combine = raised / jnp.sum(raised, axis=0, keepdims=True)
    combine_ref[...] = combine
    peak = jnp.max(logits, axis=1, keepdims=True)
    weight = jnp.exp(logits - peak)
    mass = jnp.sum(weight, axis=1, keepdims=True)
    sent_ref[:, :d] = dot(weight.astype(BF16), tokens).astype(BF16)
    sent_ref[:, d : d + 128] = lanes_of([peak, mass], rows).astype(BF16)
    sent_ref[:, d + 128 :] = dot(combine.astype(BF16), cotangent).astype(BF16)


def collect(peers, taken_ref, own_ref, wide_ref, scalars_ref):
    rows, d = wide_ref.shape
    stats = taken_ref[:, d : d + 128].astype(F32)
    peaks = column_of(stats, 0).reshape(peers, rows, 1)
    masses = column_of(stats, 1).reshape(peers, rows, 1)
    top = jnp.max(peaks, axis=0)
    scale = jnp.exp(peaks - top[None])
    total = jnp.sum(masses * scale, axis=0)
    part_in = taken_ref[:, :d].astype(F32).reshape(peers, rows, d)
    slot_in = jnp.sum(part_in * scale, axis=0) / total
    slot_out_grad = jnp.sum(taken_ref[:, d + 128 :].astype(F32).reshape(peers, rows, d), axis=0)
    own_ref[...] = jnp.concatenate([slot_in, slot_out_grad], axis=0).astype(BF16)
    wide_ref[...] = slot_in
    lane = lax.broadcasted_iota(jnp.int32, scalars_ref.shape, 1)
    scalars_ref[...] = jnp.where(lane == 0, top, total)


def deliver(far, peers, taken_ref, wide_ref, scalars_ref, back_ref):
    rows, d = wide_ref.shape
    owned = jnp.sum(taken_ref[...].astype(F32).reshape(far, 2 * rows, d), axis=0)
    owned = owned.astype(BF16).astype(F32)
    slot_out, slot_in_grad = owned[:rows], owned[rows:]
    col = jnp.sum(slot_in_grad * wide_ref[...], axis=1, keepdims=True)
    top, total = scalars_ref[:, 0:1], scalars_ref[:, 1:2]
    stats = lanes_of([top, total, col], rows)
    for at, value in ((0, slot_out), (d, slot_in_grad), (2 * d, stats)):
        copies = jnp.concatenate([value] * peers, axis=0).astype(BF16)
        back_ref[:, at : at + value.shape[1]] = copies


def finish(
    imgs, own_slots, back_ref, logits_ref, combine_ref, both_ref, share_ref, dispatch_ref, grad_ref
):
    tokens, cotangent = both_ref[0], both_ref[1]
    slots, d = share_ref.shape
    rows = logits_ref.shape[0]
    block = imgs * own_slots
    order = [at for core in range(2) for at in range(core * block, rows, 2 * block)]
    logits = jnp.concatenate([logits_ref[at : at + block] for at in order], axis=0)
    combine = jnp.concatenate([combine_ref[at : at + block] for at in order], axis=0)
    slot_out, slot_in_grad = back_ref[:, :d], back_ref[:, d : 2 * d]
    stats = back_ref[:, 2 * d :].astype(F32)
    top, total, col = [column_of(stats, at) for at in range(3)]
    dispatch = jnp.exp(logits - top) / total
    combine_grad = dot(slot_out, cotangent, 1, 1)
    dispatch_grad = dot(slot_in_grad, tokens, 1, 1)
    row_sums = jnp.sum(combine * combine_grad, axis=0, keepdims=True)
    logit_grad = dispatch * (dispatch_grad - col) + combine * (combine_grad - row_sums)
    members = slot_rows(rows, slots, imgs, own_slots, True)
    by_slot = dot(members, logit_grad.astype(BF16), 0, 0).astype(BF16)
    share_ref[...] = dot(by_slot, tokens).astype(BF16)
    dispatch_ref[...] = dispatch.astype(BF16)
    grad_ref[...] = by_slot


def token_grads(back_ref, dispatch_ref, grad_ref, params_ref, token_grad_ref):
    d = params_ref.shape[1]
    token_grad = dot(dispatch_ref[...], back_ref[:, d : 2 * d], 0, 0)
    token_grad = token_grad + dot(grad_ref[...], params_ref[...], 0, 0)
    token_grad_ref[...] = token_grad.astype(BF16)


def call(kernel, out_shape, flops, *operands):
    shapes = [jax.ShapeDtypeStruct(shape, dtype) for shape, dtype in out_shape]
    size = sum(value.size * value.dtype.itemsize for value in list(operands) + shapes)
    return pl.pallas_call(
        kernel,
        out_shape=shapes,
        compiler_params=pltpu.CompilerParams(vmem_limit_bytes=32 * 1024 * 1024),
        cost_estimate=pl.CostEstimate(flops=flops, bytes_accessed=size, transcendentals=16384),
    )(*operands)


def hidden(all_in, all_out_grad, w_in, w_out, own_slots):
    shape = (all_in.shape[0], w_in.shape[0])
    row = lax.broadcasted_iota(jnp.int32, shape, 0)
    column = lax.broadcasted_iota(jnp.int32, shape, 1)
    mine = row % own_slots == column // (shape[1] // own_slots)
    activated, slope = gelu_and_slope(dot(all_in, w_in, 1, 1))
    preact_grad = dot(all_out_grad, w_out, 1, 1) * slope
    return (
        jnp.where(mine, activated, 0.0).astype(BF16),
        jnp.where(mine, preact_grad, 0.0).astype(BF16),
    )


def rows_of(gathered_ref, which):
    return jnp.concatenate([gathered_ref[q, which] for q in range(gathered_ref.shape[0])], axis=0)


def experts(
    own_slots, gathered_ref, w_in_ref, w_out_ref, partial_ref, activated_ref, preact_grad_ref
):
    w_in, w_out = w_in_ref[...], w_out_ref[...]
    activated, preact_grad = hidden(
        rows_of(gathered_ref, 0), rows_of(gathered_ref, 1), w_in, w_out, own_slots
    )
    activated_ref[...] = activated
    preact_grad_ref[...] = preact_grad
    slot_out = dot(activated, w_out).astype(BF16)
    slot_in_grad = dot(preact_grad, w_in).astype(BF16)
    size = partial_ref.shape[2]
    for q in range(partial_ref.shape[0]):
        partial_ref[q, 0] = slot_out[q * size : (q + 1) * size]
        partial_ref[q, 1] = slot_in_grad[q * size : (q + 1) * size]


def weight_grads(gathered_ref, activated_ref, preact_grad_ref, w_in_grad_ref, w_out_grad_ref):
    all_in, all_out_grad = rows_of(gathered_ref, 0), rows_of(gathered_ref, 1)
    w_in_grad_ref[...] = dot(preact_grad_ref[...], all_in, 0, 0).astype(BF16)
    w_out_grad_ref[...] = dot(activated_ref[...], all_out_grad, 0, 0).astype(BF16)


def add_square(rows, taken_ref, total_ref):
    total = taken_ref[0].astype(F32)
    for q in range(1, taken_ref.shape[0]):
        total += taken_ref[q].astype(F32)
    pieces = [
        total[which, at : at + rows] for at in range(0, total.shape[1], rows) for which in range(2)
    ]
    total_ref[...] = jnp.concatenate(pieces, axis=0).astype(BF16)


def on_device(tokens, cotangent, slot_params, w_in, w_out):
    imgs, share, d = tokens.shape
    peers = lax.axis_size("expert")
    own_slots = slot_params.shape[1]
    slots = peers * own_slots
    rows = own_slots * imgs

    params = everywhere(slot_params.T, "expert").reshape(slots, d)
    pairs = (peers * rows, imgs * share)
    wide = 2 * d + 128
    flat = (imgs * share, d)
    params, tokens, cotangent = lax.optimization_barrier((params, tokens, cotangent))
    both = jnp.stack([tokens.reshape(flat), cotangent.reshape(flat)])
    sent, logits, combine = call(
        functools.partial(route, imgs, own_slots),
        [((peers * rows, wide), BF16), (pairs, F32), (pairs, F32)],
        100_000_000, params, both,
    )
    taken = exchange(sent.reshape(peers, rows, wide), "expert")
    own, slot_in_wide, scalars = call(
        functools.partial(collect, peers),
        [((2 * rows, d), BF16), ((rows, d), F32), ((rows, 128), F32)],
        1_000_000, taken.reshape(peers * rows, wide),
    )

    gathered = gather_dp(own)
    flat_in, flat_out = jnp.swapaxes(w_in, 1, 2).reshape(-1, d), w_out.reshape(-1, d)
    units = (gathered.shape[0] * gathered.shape[2], flat_in.shape[0])
    partial, activated, preact_grad = call(
        functools.partial(experts, own_slots),
        [(gathered.shape, BF16), (units, BF16), (units, BF16)],
        1_000_000_000, gathered, flat_in, flat_out,
    )
    w_in_grad, w_out_grad = call(
        weight_grads, [(flat_in.shape, BF16)] * 2, 600_000_000, gathered, activated, preact_grad
    )
    w_in_grad = jnp.swapaxes(w_in_grad.reshape(own_slots, -1, d), 1, 2)
    w_out_grad = w_out_grad.reshape(w_out.shape)
    terms = reduce_dp(partial, rows)
    (back,) = call(
        functools.partial(deliver, terms.shape[0], peers // 2), [((peers // 2 * rows, wide), BF16)],
        1_000_000, terms.reshape(-1, d), slot_in_wide, scalars,
    )
    back = exchange(back.reshape(peers // 2, rows, wide), "expert", expert_groups(0, 1))
    back = everywhere(back.reshape(-1, wide), "expert", expert_groups(2))

    back = back.reshape(peers * rows, wide)
    share_grad, dispatch, by_slot = call(
        functools.partial(finish, imgs, own_slots),
        [((slots, d), BF16), (pairs, BF16), ((slots, imgs * share), BF16)],
        70_000_000, back, logits, combine, both,
    )
    (token_grad,) = call(
        token_grads, [(flat, BF16)], 30_000_000, back, dispatch, by_slot, params
    )
    token_grad = token_grad.reshape(tokens.shape)

    share_grad = jnp.broadcast_to(share_grad.reshape(1, peers, own_slots, d), (2, peers, own_slots, d))
    share_grad = exchange(
        share_grad.reshape(2 * peers, own_slots, d), ("dp", "expert"), plane_groups()
    )
    share_grad = jnp.sum(share_grad.astype(F32), axis=0).astype(BF16)
    share_grad = everywhere(share_grad, "dp", dp_groups(1, 2))
    share_grad = jnp.sum(share_grad.astype(F32), axis=0)
    slot_grad = share_grad.T
    return (token_grad, slot_grad, w_in_grad, w_out_grad)


def solution(mesh):
    placed = (
        P("dp", "expert", None),
        P("dp", "expert", None),
        P(None, "expert"),
        P("expert", None, "dp"),
        P("expert", "dp", None),
    )
    return jax.shard_map(
        on_device,
        mesh=mesh,
        in_specs=placed,
        out_specs=(
            P("dp", "expert", None),
            P(None, "expert"),
            P("expert", None, "dp"),
            P("expert", "dp", None),
        ),
        check_vma=False,
    )
```
